256 devices in a mesh: cp: 128 (over y, x, z), hd: 2 (over core).
Axes of the slice: x: 4, y: 4, z: 8, core: 2. Of those that a mesh axis runs over, the one named last changes fastest.
Arguments:
- queries: bfloat16 [32768, 1024], P('cp', 'hd'), may hold values from -32 to 32
- keys: bfloat16 [32768, 256], P('cp', 'hd'), may hold values from -13 to 13
- values: bfloat16 [32768, 256], P('cp', 'hd'), may hold values from -6 to 6
- out_weight: bfloat16 [4096, 1024], P(None, 'hd'), may hold values from -0.1875 to 0.1875
- doc_lengths: int32 [64], replicated, may hold values from 1 to 1024, 32768 in all
- doc_full: int32 [64], replicated, may hold values 0 or 1
- out_grad: bfloat16 [32768, 4096], P('cp', 'hd'), may hold values from -6 to 6
Outputs:
- layer_out: bfloat16 [32768, 4096], P('cp', 'hd')
- query_grad: bfloat16 [32768, 1024], P('cp', 'hd')
- key_grad: bfloat16 [32768, 256], P('cp', 'hd')
- value_grad: bfloat16 [32768, 256], P('cp', 'hd')
The draws below stay inside these ranges and needn't reach their ends.
Inputs may be any that keep to these rules, and one draw needn't show every extreme that they name: `doc_lengths`: the lengths add up to 32768; the longest document has exactly 1024 tokens.
All inputs are finite; a program needn't handle non-finite values.
Results may differ from the reference program's by a relative error of at most 0.035.
Values may be sent and summed in bfloat16 or wider, within the bound.
No kernel may reach another device: no remote copies, remote signals or barrier semaphores. Data moves between devices by JAX's collectives and lax.ppermute only.
A program may use at most 128 MiB of HBM per device.

```python
import math
import jax
import jax.numpy as jnp
import numpy as np
from jax import lax

HQ = 8
HK = 2
DH = 128
D_MODEL = 4096
TOK_DEV = 256
SPAN = 4
SEQ = 32768
DOC_MOST = 1024
NDOC = 64
N_CP = 128


def shared_keys(key):
    return jnp.clip(jax.random.normal(key, (SEQ, HK * DH), jnp.float32), -4.0, 4.0)


def draw_keys(key, part):
    base = shared_keys(key)
    return base.astype(jnp.bfloat16)


def draw_queries(key, part):
    key = jax.random.fold_in(key, 12)
    return jnp.clip(jax.random.normal(key, (SEQ, HQ * DH), jnp.float32), -4.0, 4.0).astype(jnp.bfloat16)


def with_ends(values, rng, low, high):
    longest = values.shape.index(max(values.shape))
    spots = []
    for shift in (0, 1):
        where = [jax.random.randint(jax.random.fold_in(rng, axis), (), 0, length) for axis, length in enumerate(values.shape)]
        where[longest] = (where[longest] + shift) % values.shape[longest]
        spots.append(tuple(where))
    return values.at[spots[0]].set(low).at[spots[1]].set(high)


def shard_levels(own_key, shape, split, least, largest):
    level, own = 1.0, jax.random.fold_in(own_key, 6)
    for axis_at, parts in split:
        draws = jnp.exp(jax.random.uniform(jax.random.fold_in(own, axis_at), (parts,), jnp.float32, least / len(split), largest / len(split)))
        level = level * jnp.repeat(draws, shape[axis_at] // parts).reshape([-1 if axis == axis_at else 1 for axis in range(len(shape))])
    return level


def split_up(number_of, total, most, slope):
    loads = [(1 << 20) // math.isqrt(rank ** slope) + 1 for rank in range(2, number_of + 1)]
    rest, given = total - most - (number_of - 1), [1] * (number_of - 1)
    while rest > 0:
        candidates = [i for i in range(number_of - 1) if given[i] < most]
        whole, budget = sum([loads[i] for i in candidates]), rest
        for i in candidates:
            extra = min(most - given[i], max(1, budget * loads[i] // whole), rest)
            given[i] = given[i] + extra
            rest = rest - extra
    return np.array([most] + given)


def ragged(own_key, number_of, total, most, slope):
    if number_of == 2:
        one = jax.random.randint(own_key, (), max(1, total - most), min(most, total - 1) + 1)
        return jnp.stack([one, total - one])
    sizes = jnp.asarray(split_up(number_of, total, most, slope), jnp.int32)
    pairs = (number_of - 1) // 2
    donor, taker = sizes[1:1 + 2 * pairs:2], sizes[2:2 + 2 * pairs:2]
    room = jnp.minimum(donor - 1, most - taker)
    moved = jax.random.randint(jax.random.fold_in(own_key, 1), (pairs,), 0, 1 << 20) % (room + 1)
    sizes = sizes.at[1:1 + 2 * pairs:2].set(donor - moved).at[2:2 + 2 * pairs:2].set(taker + moved)
    return sizes[jax.random.permutation(jax.random.fold_in(own_key, 2), number_of)]


def bell_draw(key, dims, deviation, bound, cuts=(), kind=jnp.bfloat16):
    factor_of = shard_levels(key, dims, cuts, -0.22, 0.18) if cuts else 1.0
    values = jax.random.normal(key, dims, jnp.float32) * deviation * factor_of
    return jnp.minimum(jnp.maximum(values, -bound), bound).astype(kind)


def setup_inputs(seed: int = 0) -> dict:
    streams_of = jax.random.split(jax.random.key(seed), 8)
    return {
        "queries": draw_queries(jax.random.fold_in(streams_of[7], 71), 0),
        "keys": draw_keys(jax.random.fold_in(streams_of[7], 71), 0),
        "values": bell_draw(streams_of[2], (SEQ, HK * DH), 1.0, 6.0, ((0, 128), (1, 2))),
        "out_weight": bell_draw(streams_of[3], (D_MODEL, HQ * DH), (HQ * DH) ** -0.5, 0.1875, ((1, 2),)),
        "doc_lengths": ragged(streams_of[4], NDOC, SEQ, DOC_MOST, 0).astype(jnp.int32),
        "doc_full": with_ends((jax.random.randint(streams_of[5], (NDOC,), 0, 2) < 1).astype(jnp.int32), jax.random.fold_in(streams_of[5], 1), 0, 1),
        "out_grad": bell_draw(streams_of[6], (SEQ, D_MODEL), 1.0, 6.0, ((0, 128), (1, 2))),
    }


def doc_layout(doc_lengths, doc_full, positions, total):
    ends = jnp.cumsum(doc_lengths).astype(jnp.int32)
    doc_index = lax.optimization_barrier(jnp.sum((positions[:, None] >= ends[None, :]).astype(jnp.int32), axis=1))
    inside = (positions >= 0) & (positions < total)
    labels = jnp.arange(doc_lengths.shape[0], dtype=jnp.int32)
    full_flag = lax.optimization_barrier(jnp.sum(jnp.where(doc_index[:, None] == labels[None, :], doc_full[None, :], 0), axis=1))
    return (doc_index, full_flag, inside)

def allowed_mask(doc_lengths, doc_full, query_pos, key_pos, total):
    query_doc, query_full, _ = doc_layout(doc_lengths, doc_full, query_pos, total)
    key_doc, _, key_inside = doc_layout(doc_lengths, doc_full, key_pos, total)
    same = key_doc[None, :] == query_doc[:, None]
    order = (query_full[:, None] == 1) | (key_pos[None, :] <= query_pos[:, None])
    return key_inside[None, :] & same & order

def block_forward(q_block, key_win, val_win, mask):
    rows = q_block.shape[0]
    width_rows = key_win.shape[0]
    groups = HQ // HK
    scale = 1.0 / math.sqrt(DH)
    q_heads = q_block.astype(jnp.float32).reshape(rows, HK, groups, DH)
    k_heads = key_win.astype(jnp.float32).reshape(width_rows, HK, DH)
    v_heads = val_win.astype(jnp.float32).reshape(width_rows, HK, DH)
    scores = jnp.einsum('tkgd,skd->kgts', q_heads, k_heads) * scale
    masked = jnp.where(mask[None, None], scores, jnp.float32(-1e+30))
    top = lax.optimization_barrier(jnp.max(masked, axis=-1, keepdims=True))
    expo = jnp.where(mask[None, None], jnp.exp(masked - top), jnp.float32(0.0))
    probs = expo / lax.optimization_barrier(jnp.sum(expo, axis=-1, keepdims=True))
    weights = probs.astype(jnp.bfloat16)
    attn = jnp.einsum('kgts,skd->tkgd', weights.astype(jnp.float32), v_heads)
    return (attn.astype(jnp.bfloat16).reshape(rows, HQ * DH), probs, weights)

def reference(queries, keys, values, out_weight, doc_lengths, doc_full, out_grad):
    rows = TOK_DEV
    margin = SPAN * rows
    width_rows = (2 * SPAN + 1) * rows
    groups = HQ // HK
    scale = 1.0 / math.sqrt(DH)
    key_pad = jnp.pad(keys, ((margin, margin), (0, 0)))
    val_pad = jnp.pad(values, ((margin, margin), (0, 0)))

    def window(block):
        start = (block * rows).astype(jnp.int32)
        q_block = lax.dynamic_slice_in_dim(queries, start, rows, 0)
        key_win = lax.dynamic_slice_in_dim(key_pad, start, width_rows, 0)
        val_win = lax.dynamic_slice_in_dim(val_pad, start, width_rows, 0)
        query_pos = start + jnp.arange(rows, dtype=jnp.int32)
        key_pos = start - margin + jnp.arange(width_rows, dtype=jnp.int32)
        mask = allowed_mask(doc_lengths, doc_full, query_pos, key_pos, SEQ)
        return (start, q_block, key_win, val_win, mask)

    def forward_block(block):
        start, q_block, key_win, val_win, mask = window(block)
        attn_block, probs, weights = block_forward(q_block, key_win, val_win, mask)
        return attn_block
    blocks = jnp.arange(N_CP, dtype=jnp.int32)
    attn = lax.map(forward_block, blocks).reshape(SEQ, HQ * DH)
    layer_out = jnp.dot(attn, out_weight.T, preferred_element_type=jnp.float32).astype(jnp.bfloat16)
    attn_grad = jnp.dot(out_grad, out_weight, preferred_element_type=jnp.float32).astype(jnp.bfloat16)

    def backward_block(carry, block):
        key_acc, val_acc = carry
        start, q_block, key_win, val_win, mask = window(block)
        attn_block, probs, weights = block_forward(q_block, key_win, val_win, mask)
        grad_block = lax.dynamic_slice_in_dim(attn_grad, start, rows, 0)
        grad_heads = grad_block.astype(jnp.float32).reshape(rows, HK, groups, DH)
        attn_heads = attn_block.astype(jnp.float32).reshape(rows, HK, groups, DH)
        q_heads = q_block.astype(jnp.float32).reshape(rows, HK, groups, DH)
        k_heads = key_win.astype(jnp.float32).reshape(width_rows, HK, DH)
        v_heads = val_win.astype(jnp.float32).reshape(width_rows, HK, DH)
        delta = jnp.einsum('tkgd,tkgd->kgt', grad_heads, attn_heads)
        dprob = jnp.einsum('tkgd,skd->kgts', grad_heads, v_heads)
        dscore = (probs * (dprob - delta[..., None]) * scale).astype(jnp.bfloat16)
        dscore_f = dscore.astype(jnp.float32)
        dq = jnp.einsum('kgts,skd->tkgd', dscore_f, k_heads).astype(jnp.bfloat16).reshape(rows, HQ * DH)
        dk = jnp.einsum('kgts,tkgd->skd', dscore_f, q_heads).reshape(width_rows, HK * DH)
        dv = jnp.einsum('kgts,tkgd->skd', weights.astype(jnp.float32), grad_heads).reshape(width_rows, HK * DH)
        key_acc = lax.dynamic_update_slice_in_dim(key_acc, lax.dynamic_slice_in_dim(key_acc, start, width_rows, 0) + dk, start, 0)
        val_acc = lax.dynamic_update_slice_in_dim(val_acc, lax.dynamic_slice_in_dim(val_acc, start, width_rows, 0) + dv, start, 0)
        return ((key_acc, val_acc), dq)
    empty = jnp.zeros((SEQ + 2 * margin, HK * DH), jnp.float32)
    (key_acc, val_acc), dq_blocks = lax.scan(backward_block, (empty, empty), blocks)
    query_grad = dq_blocks.reshape(SEQ, HQ * DH)
    key_grad = key_acc[margin:margin + SEQ].astype(jnp.bfloat16)
    value_grad = val_acc[margin:margin + SEQ].astype(jnp.bfloat16)
    return (layer_out, query_grad, key_grad, value_grad)
```

```python
import math

import jax
import jax.numpy as jnp
from jax import lax
from jax.experimental import pallas as pl
from jax.experimental.pallas import tpu as pltpu
from jax.sharding import PartitionSpec as P

HQ = 8
HK = 2
DH = 128
SPAN = 4
ROWS = 256
GROUPS = HQ // HK
WIDE = 2 * SPAN + 1
NEG = -1e30
SCALE = 1.0 / math.sqrt(DH)
SCALE2 = SCALE / math.log(2.0)
VMEM = pl.BlockSpec(memory_space=pltpu.VMEM)
HBM = pl.BlockSpec(memory_space=pltpu.HBM)
SMALL = pltpu.CompilerParams(vmem_limit_bytes=4 * 1024 * 1024)
SMEM = pl.BlockSpec(memory_space=pltpu.SMEM)


def dot_nn(a, b):
    return lax.dot_general(a, b, (((1,), (0,)), ((), ())), preferred_element_type=jnp.float32)


def dot_nt(a, b):
    return lax.dot_general(a, b, (((1,), (1,)), ((), ())), preferred_element_type=jnp.float32)


def limits(index, lengths_row, full_row):
    n = lengths_row.shape[1]
    row = lax.broadcasted_iota(jnp.int32, (n, n), 0)
    col = lax.broadcasted_iota(jnp.int32, (n, n), 1)
    ends = jnp.sum(jnp.where(col <= row, lengths_row, 0), axis=1, keepdims=True)
    starts = jnp.sum(jnp.where(col < row, lengths_row, 0), axis=1, keepdims=True)
    full = jnp.sum(jnp.where(col == row, full_row, 0), axis=1, keepdims=True)
    pos = index * ROWS + lax.broadcasted_iota(jnp.int32, (n, ROWS), 1)
    inside = (pos >= starts) & (pos < ends)
    low = jnp.sum(jnp.where(inside, starts, 0), axis=0, keepdims=True)
    high = jnp.sum(jnp.where(inside, jnp.where(full == 1, ends, pos + 1), 0), axis=0, keepdims=True)
    return low, high


def attention_kernel(
    place_ref, len_ref, full_ref, q_ref, own_ref, *refs,
):
    ring_refs = refs[0:SPAN]
    twin_refs = refs[SPAN : 2 * SPAN]
    do_ref, attn_ref, dq_ref, mid_ref, ahead_ref, across_ref = refs[2 * SPAN : 2 * SPAN + 6]
    win, s_scr, p_scr, q_st, do_st, qs_st, dos_st, acc, dq_acc = refs[2 * SPAN + 6 :]
    index = place_ref[0]
    way = 1 - 2 * place_ref[1]
    low, high = limits(index, len_ref[...], full_ref[...])
    first = jnp.min(low)
    last = jnp.max(high)
    base = index - SPAN
    r_low = jnp.maximum(first // ROWS - base, 0)
    r_high = jnp.minimum((last + ROWS - 1) // ROWS - base, WIDE)

    def rows_of(r):
        return pl.ds(pl.multiple_of(r * ROWS, ROWS), ROWS)

    def keys_of(r):
        return pl.ds(pl.multiple_of(r * 2 * ROWS, ROWS), ROWS)

    def vals_of(r):
        return pl.ds(pl.multiple_of(r * 2 * ROWS + ROWS, ROWS), ROWS)

    def pair_of(r):
        return pl.ds(pl.multiple_of(r * 2 * ROWS, ROWS), 2 * ROWS)

    for h in range(GROUPS):
        cols = slice(h * DH, (h + 1) * DH)
        rows = slice(h * ROWS, (h + 1) * ROWS)
        q_st[rows, :] = q_ref[:, cols]
        do_st[rows, :] = do_ref[:, cols]

    win[pair_of(SPAN), :] = own_ref[...]
    for k in range(1, SPAN + 1):
        win[pair_of(SPAN - k * way), :] = ring_refs[k - 1][0 : 2 * ROWS, :]
        win[pair_of(SPAN + k * way), :] = twin_refs[k - 1][...]

    def scores(r, top):
        keys = win[keys_of(r), :]
        key_pos = (base + r) * ROWS + lax.broadcasted_iota(jnp.int32, (ROWS, ROWS), 0)
        valid = (key_pos >= low) & (key_pos < high)
        out = []
        for h in range(GROUPS):
            rows = slice(h * ROWS, (h + 1) * ROWS)
            s = dot_nt(keys, q_st[rows, :]) * SCALE2
            s = jnp.where(valid, s, NEG)
            s_scr[rows_of(r), rows] = s
            out.append(jnp.maximum(top[h], jnp.max(s, axis=0, keepdims=True)))
        return tuple(out)

    none = jnp.full((1, ROWS), NEG, jnp.float32)
    top = lax.fori_loop(r_low, r_high, scores, (none,) * GROUPS)

    acc[...] = jnp.zeros_like(acc)

    def weigh(r, total):
        vals_t = win[vals_of(r), :].T
        out = []
        for h in range(GROUPS):
            rows = slice(h * ROWS, (h + 1) * ROWS)
            p = jnp.exp2(s_scr[rows_of(r), rows] - top[h])
            out.append(total[h] + jnp.sum(p, axis=0, keepdims=True))
            p = p.astype(jnp.bfloat16)
            p_scr[rows_of(r), rows] = p
            acc[:, rows] += dot_nn(vals_t, p)
        return tuple(out)

    zero = jnp.zeros((1, ROWS), jnp.float32)
    total = lax.fori_loop(r_low, r_high, weigh, (zero,) * GROUPS)

    deltas = []
    invs = []
    for h in range(GROUPS):
        cols = slice(h * DH, (h + 1) * DH)
        rows = slice(h * ROWS, (h + 1) * ROWS)
        inv = 1.0 / total[h]
        attn = (acc[:, rows] * inv).T.astype(jnp.bfloat16)
        attn_ref[:, cols] = attn
        grad = do_st[rows, :].astype(jnp.float32)
        prod = jnp.sum(attn.astype(jnp.float32) * grad, axis=1, keepdims=True)
        deltas.append(jnp.broadcast_to(prod, (ROWS, DH)).T[0:1, :])
        inv_col = jnp.broadcast_to(inv, (DH, ROWS)).T
        dos_st[rows, :] = (grad * inv_col).astype(jnp.bfloat16)
        qs_st[rows, :] = (q_st[rows, :].astype(jnp.float32) * (inv_col * SCALE)).astype(jnp.bfloat16)
        invs.append(inv)

    dq_acc[...] = jnp.zeros_like(dq_acc)
    ahead_ref[...] = jnp.zeros_like(ahead_ref)
    across_ref[...] = jnp.zeros_like(across_ref)

    def backward(r, carry):
        keys_t = win[keys_of(r), :].T
        vals = win[vals_of(r), :]
        dk = jnp.zeros((ROWS, DH), jnp.float32)
        dv = jnp.zeros((ROWS, DH), jnp.float32)
        for h in range(GROUPS):
            rows = slice(h * ROWS, (h + 1) * ROWS)
            p = p_scr[rows_of(r), rows]
            dp = dot_nt(vals, do_st[rows, :])
            ds = (p.astype(jnp.float32) * (dp - deltas[h])).astype(jnp.bfloat16)
            dq_acc[:, rows] += dot_nn(keys_t, ds)
            dk += dot_nn(ds, qs_st[rows, :])
            dv += dot_nn(p, dos_st[rows, :])
        off = (r - SPAN) * way
        at = jnp.abs(off) - 1
        dk = dk.astype(jnp.bfloat16)
        dv = dv.astype(jnp.bfloat16)

        @pl.when(off > 0)
        def _():
            ahead_ref[keys_of(at), :] = dk
            ahead_ref[vals_of(at), :] = dv

        @pl.when(off < 0)
        def _():
            across_ref[keys_of(at), :] = dk
            across_ref[vals_of(at), :] = dv

        @pl.when(off == 0)
        def _():
            mid_ref[0:ROWS, :] = dk
            mid_ref[ROWS : 2 * ROWS, :] = dv

        return carry

    lax.fori_loop(r_low, r_high, backward, 0)
    for h in range(GROUPS):
        cols = slice(h * DH, (h + 1) * DH)
        rows = slice(h * ROWS, (h + 1) * ROWS)
        dq_ref[:, cols] = (dq_acc[:, rows] * (invs[h] * SCALE)).T.astype(jnp.bfloat16)


def attention(place, lengths, full, q, own, ring, twins, do):
    wide = GROUPS * ROWS
    return pl.pallas_call(
        attention_kernel,
        out_shape=(
            jax.ShapeDtypeStruct(q.shape, jnp.bfloat16),
            jax.ShapeDtypeStruct(q.shape, jnp.bfloat16),
            jax.ShapeDtypeStruct((2 * ROWS, DH), jnp.bfloat16),
            jax.ShapeDtypeStruct((SPAN * 2 * ROWS, DH), jnp.bfloat16),
            jax.ShapeDtypeStruct((SPAN * 2 * ROWS, DH), jnp.bfloat16),
        ),
        in_specs=[SMEM] + [VMEM] * (5 + 2 * SPAN),
        out_specs=(VMEM,) * 5,
        scratch_shapes=[
            pltpu.VMEM((WIDE * 2 * ROWS, DH), jnp.bfloat16),
            pltpu.VMEM((WIDE * ROWS, wide), jnp.float32),
            pltpu.VMEM((WIDE * ROWS, wide), jnp.bfloat16),
            pltpu.VMEM((wide, DH), jnp.bfloat16),
            pltpu.VMEM((wide, DH), jnp.bfloat16),
            pltpu.VMEM((wide, DH), jnp.bfloat16),
            pltpu.VMEM((wide, DH), jnp.bfloat16),
            pltpu.VMEM((DH, wide), jnp.float32),
            pltpu.VMEM((DH, wide), jnp.float32),
        ],
        compiler_params=pltpu.CompilerParams(vmem_limit_bytes=28 * 1024 * 1024),
        cost_estimate=pl.CostEstimate(flops=3 * 10**9, bytes_accessed=6 * 10**6, transcendentals=10**6),
    )(place, lengths, full, q, own, *ring, *twins, do)


def small_call(body, out_rows, *args):
    shapes = [jax.ShapeDtypeStruct((rows, DH), jnp.bfloat16) for rows in out_rows]
    return pl.pallas_call(
        body,
        out_shape=shapes,
        in_specs=[VMEM] * len(args),
        out_specs=[VMEM] * len(shapes),
        compiler_params=SMALL,
        cost_estimate=pl.CostEstimate(flops=10**5, bytes_accessed=10**5, transcendentals=0),
    )(*args)


def stack_body(*refs):
    at = 0
    for ref in refs[:-1]:
        refs[-1][at : at + ref.shape[0], :] = ref[...]
        at += ref.shape[0]


def part_of(k):
    return slice((k - 1) * 2 * ROWS, k * 2 * ROWS)


def both_heads(ahead, across, which):
    n = 2 * ROWS

    def body(ahead_ref, across_ref, *out_refs):
        for k, out_ref in zip(which, out_refs):
            out_ref[0:n, :] = ahead_ref[part_of(k), :]
            out_ref[n : 2 * n, :] = across_ref[part_of(k), :]

    return small_call(body, [2 * n] * len(which), ahead, across)


def summed(ahead, across, k, *others):
    n = 2 * ROWS

    def body(ahead_ref, across_ref, *refs):
        for at, ref in ((0, ahead_ref), (n, across_ref)):
            total = ref[part_of(k), :].astype(jnp.float32)
            for other in refs[:-1]:
                total += other[at : at + n, :].astype(jnp.float32)
            refs[-1][at : at + n, :] = total.astype(jnp.bfloat16)

    return small_call(body, [2 * n], ahead, across, *others)[0]


def last_sum(mid, near, far, near_twin, far_twin):
    n = 2 * ROWS

    def body(*refs):
        for out_ref, rows in ((refs[-2], slice(0, ROWS)), (refs[-1], slice(ROWS, n))):
            total = refs[0][rows, :].astype(jnp.float32)
            for ref in refs[1:-2]:
                total += ref[rows, :].astype(jnp.float32)
            out_ref[...] = total.astype(jnp.bfloat16)

    return small_call(body, [ROWS, ROWS], mid, near, far, near_twin, far_twin)


def project_back(core, own, other, w):
    rows, depth = own.shape
    cols = w.shape[1]

    def body(core_ref, own_ref, other_ref, w_ref, out_ref, w_buf, sems):
        core = core_ref[0]
        copies = []
        for n, half in enumerate((core, 1 - core)):
            where = pl.ds(pl.multiple_of(half * depth, depth), depth)
            copies.append(pltpu.make_async_copy(w_ref.at[where, :], w_buf.at[n], sems.at[n]))
            copies[n].start()
        copies[0].wait()
        part = dot_nn(own_ref[...], w_buf[0])
        copies[1].wait()
        out_ref[...] = (part + dot_nn(other_ref[...], w_buf[1])).astype(jnp.bfloat16)

    return pl.pallas_call(
        body,
        out_shape=jax.ShapeDtypeStruct((rows, cols), jnp.bfloat16),
        in_specs=[SMEM, VMEM, VMEM, HBM],
        out_specs=VMEM,
        scratch_shapes=[pltpu.VMEM((2, depth, cols), jnp.bfloat16), pltpu.SemaphoreType.DMA((2,))],
        compiler_params=pltpu.CompilerParams(vmem_limit_bytes=12 * 1024 * 1024),
        cost_estimate=pl.CostEstimate(flops=4 * rows * depth * cols, bytes_accessed=6 * 10**6, transcendentals=0),
    )(core, own, other, w)


def project(half, attn, w, other=None):
    rows, depth = attn.shape
    cols = w.shape[0] // 2
    parts = 2
    wide = cols // parts
    more = () if other is None else (other,)

    def body(half_ref, a_ref, w_ref, *refs):
        out_ref, w_buf, sems = refs[-3:]
        copies = []
        for n in range(parts):
            where = pl.ds(pl.multiple_of(half_ref[0] * cols + n * wide, wide), wide)
            copies.append(pltpu.make_async_copy(w_ref.at[where, :], w_buf.at[n], sems.at[n]))
            copies[n].start()
        for n in range(parts):
            copies[n].wait()
            at = slice(n * wide, (n + 1) * wide)
            out = dot_nt(a_ref[...], w_buf[n])
            if more:
                out += refs[0][:, at].astype(jnp.float32)
            out_ref[:, at] = out.astype(jnp.bfloat16)

    return pl.pallas_call(
        body,
        out_shape=jax.ShapeDtypeStruct((rows, cols), jnp.bfloat16),
        in_specs=[SMEM, VMEM, HBM] + [VMEM] * len(more),
        out_specs=VMEM,
        scratch_shapes=[pltpu.VMEM((parts, wide, depth), jnp.bfloat16), pltpu.SemaphoreType.DMA((parts,))],
        compiler_params=pltpu.CompilerParams(vmem_limit_bytes=12 * 1024 * 1024),
        cost_estimate=pl.CostEstimate(flops=2 * rows * depth * cols, bytes_accessed=4 * 10**6, transcendentals=0),
    )(half, attn, w, *more)


def on_device(queries, keys, values, out_weight, doc_lengths, doc_full, out_grad):
    devices = lax.axis_size("cp")
    index = lax.axis_index("cp").astype(jnp.int32)
    core = lax.axis_index("hd").astype(jnp.int32)
    place = jnp.stack([index, core])
    core = core.reshape(1)
    half = 2 * ROWS

    def step(block, far):
        ways = [(2 * i, 2 * (i + far)) for i in range(devices - far)]
        ways += [(2 * (i + far) + 1, 2 * i + 1) for i in range(devices - far)]
        return lax.ppermute(block, ("cp", "hd"), ways)

    def twin(block):
        return lax.ppermute(block, "hd", [(0, 1), (1, 0)])

    block = small_call(stack_body, [2 * half], keys, values, twin(keys), twin(values))[0]
    other_grad = twin(out_grad)
    at2 = step(block, 2)
    at1 = step(block, 1)
    attn_grad = project_back(core, out_grad, other_grad, out_weight)
    at2, attn_grad = lax.optimization_barrier((at2, attn_grad))
    at4 = step(at2, 2)
    at3 = step(at2, 1)
    ring = (at1, at2, at3, at4)
    twins = [twin(got[half:]) for got in ring]

    attn, query_grad, mid, ahead, across = attention(
        place, doc_lengths.reshape(1, -1), doc_full.reshape(1, -1), queries, block[:half], ring, twins, attn_grad
    )
    across = twin(across)
    out4, out3, out1 = both_heads(ahead, across, (4, 3, 1))
    in4 = step(out4, 2)
    in3 = step(out3, 1)
    away = project(1 - core, attn, out_weight)
    near = step(out1, 1)
    far = step(summed(ahead, across, 2, in4, in3), 2)
    layer_out = project(core, attn, out_weight, twin(away))
    far, layer_out = lax.optimization_barrier((far, layer_out))
    key_grad, value_grad = last_sum(mid, near[:half], far[:half], twin(near[half:]), twin(far[half:]))
    return (layer_out, query_grad, key_grad, value_grad)


def solution(mesh):
    placed = (P("cp", "hd"), P("cp", "hd"), P("cp", "hd"), P(None, "hd"), P(), P(), P("cp", "hd"))
    return jax.shard_map(
        on_device,
        mesh=mesh,
        in_specs=placed,
        out_specs=(P("cp", "hd"), P("cp", "hd"), P("cp", "hd"), P("cp", "hd")),
        check_vma=False,
    )
```

```python
import math

import jax
import jax.numpy as jnp
from jax import lax
from jax.experimental import pallas as pl
from jax.experimental.pallas import tpu as pltpu
from jax.sharding import PartitionSpec as P

HQ = 8
HK = 2
DH = 128
SPAN = 4
ROWS = 256
GROUPS = HQ // HK
WIDE = 2 * SPAN + 1
REACH = 2
NEAR = 2 * REACH + 1
FAR = WIDE - NEAR
SUB = 128
SUBS = ROWS // SUB
TILE = GROUPS * SUB
STACK = SUBS * TILE
CHUNK = 256
CHUNKS = TILE // CHUNK
NEG = -1e30
MASKED = -2e30
BIG = 60 * 1024 * 1024
SCALE = 1.0 / math.sqrt(DH)
SCALE2 = SCALE / math.log(2.0)
VMEM = pl.BlockSpec(memory_space=pltpu.VMEM)
ANY = pl.BlockSpec(memory_space=pl.ANY)
SMALL = pltpu.CompilerParams(vmem_limit_bytes=4 * 1024 * 1024)
SMEM = pl.BlockSpec(memory_space=pltpu.SMEM)


def dot_nn(a, b):
    return lax.dot_general(a, b, (((1,), (0,)), ((), ())), preferred_element_type=jnp.float32)


def dot_nt(a, b):
    return lax.dot_general(a, b, (((1,), (1,)), ((), ())), preferred_element_type=jnp.float32)


def limits(index, lengths_row, full_row):
    n = lengths_row.shape[1]
    row = lax.broadcasted_iota(jnp.int32, (n, n), 0)
    col = lax.broadcasted_iota(jnp.int32, (n, n), 1)
    ends = jnp.sum(jnp.where(col <= row, lengths_row, 0), axis=1, keepdims=True)
    starts = jnp.sum(jnp.where(col < row, lengths_row, 0), axis=1, keepdims=True)
    full = jnp.sum(jnp.where(col == row, full_row, 0), axis=1, keepdims=True)
    pos = index * ROWS + lax.broadcasted_iota(jnp.int32, (n, ROWS), 1)
    inside = (pos >= starts) & (pos < ends)
    low = jnp.sum(jnp.where(inside, starts, 0), axis=0, keepdims=True)
    high = jnp.sum(jnp.where(inside, jnp.where(full == 1, ends, pos + 1), 0), axis=0, keepdims=True)
    return low, high


def rows_of(r):
    return pl.ds(pl.multiple_of(r * ROWS, ROWS), ROWS)


def keys_of(r):
    return pl.ds(pl.multiple_of(r * 2 * ROWS, ROWS), ROWS)


def vals_of(r):
    return pl.ds(pl.multiple_of(r * 2 * ROWS + ROWS, ROWS), ROWS)


def pair_of(r):
    return pl.ds(pl.multiple_of(r * 2 * ROWS, ROWS), 2 * ROWS)


def tile_cols(sub, c):
    return slice(sub * TILE + c * CHUNK, sub * TILE + (c + 1) * CHUNK)


def staged(sub, h):
    return slice(sub * TILE + h * SUB, sub * TILE + (h + 1) * SUB)


def sub_rows(sub):
    return slice(sub * SUB, (sub + 1) * SUB)


def head_cols(h):
    return slice(h * DH, (h + 1) * DH)


def fold_block(sub, at, key_pos, low, high, win, q_st, acc, p_ref, tops, state):
    keys = win[keys_of(at), :]
    vals_t = win[vals_of(at), :].T
    valid = (key_pos >= low) & (key_pos < high)
    out = []
    for c in range(CHUNKS):
        cols = tile_cols(sub, c)
        top, total = state[c]
        s = jnp.where(valid, dot_nt(keys, q_st[cols, :]) * SCALE2, MASKED)
        new = jnp.maximum(top, jnp.max(s, axis=0, keepdims=True))
        p = jnp.exp2(s - new)
        fix = jnp.exp2(top - new)
        out.append((new, total * fix + jnp.sum(p, axis=0, keepdims=True)))
        p = p.astype(jnp.bfloat16)
        p_ref[rows_of(at), cols] = p
        tops[pl.ds(at, 1), cols] = new
        acc[:, cols] = acc[:, cols] * fix + dot_nn(vals_t, p)
    return tuple(out)


def back_block(sub, at, win, q_st, do_st, p_ref, tops, top, inv, delta, dq_acc, dkv):
    keys_t = win[keys_of(at), :].T
    vals = win[vals_of(at), :]
    dk = jnp.zeros((ROWS, DH), jnp.float32)
    dv = jnp.zeros((ROWS, DH), jnp.float32)
    for c in range(CHUNKS):
        cols = tile_cols(sub, c)
        share = jnp.exp2(tops[pl.ds(at, 1), cols] - top[:, cols]) * inv[:, cols]
        w = p_ref[rows_of(at), cols].astype(jnp.float32) * share
        dp = dot_nt(vals, do_st[cols, :])
        ds = (w * (dp - delta[:, cols])).astype(jnp.bfloat16)
        dq_acc[:, cols] += dot_nn(keys_t, ds)
        dk += dot_nn(ds, q_st[cols, :])
        dv += dot_nn(w.astype(jnp.bfloat16), do_st[cols, :])
    dkv[keys_of(at), :] += dk * SCALE
    dkv[vals_of(at), :] += dv


def key_positions(first):
    return first + lax.broadcasted_iota(jnp.int32, (ROWS, CHUNK), 0)


def near_forward_kernel(
    place_ref, len_ref, full_ref, q_ref, own_ref, at1, at2, twin1, twin2,
    range_ref, limit_ref, q_st, win, acc, p_ref, tops, state_ref,
):
    index = place_ref[0]
    way = 1 - 2 * place_ref[1]
    base = index - SPAN
    low, high = limits(index, len_ref[...], full_ref[...])
    for sub in range(SUBS):
        for h in range(GROUPS):
            q_st[staged(sub, h), :] = q_ref[sub_rows(sub), head_cols(h)]
    win[pair_of(REACH), :] = own_ref[0 : 2 * ROWS, :]
    for k, (ring, twin) in enumerate(((at1, twin1), (at2, twin2))):
        win[pair_of(REACH - (k + 1) * way), :] = ring[0 : 2 * ROWS, :]
        win[pair_of(REACH + (k + 1) * way), :] = twin[...]
    acc[...] = jnp.zeros_like(acc)
    limit_ref[...] = jnp.zeros_like(limit_ref)
    for sub in range(SUBS):
        cut = slice(sub * SUB, (sub + 1) * SUB)
        low_row = jnp.concatenate([low[:, cut]] * (CHUNK // SUB), axis=1)
        high_row = jnp.concatenate([high[:, cut]] * (CHUNK // SUB), axis=1)
        limit_ref[2 * sub : 2 * sub + 1, :] = low_row
        limit_ref[2 * sub + 1 : 2 * sub + 2, :] = high_row
        r_low = jnp.maximum(jnp.min(low[:, cut]) // ROWS - base, 0)
        r_high = jnp.minimum((jnp.max(high[:, cut]) + ROWS - 1) // ROWS - base, WIDE)
        range_ref[2 * sub] = r_low
        range_ref[2 * sub + 1] = r_high

        def body(at, state):
            key_pos = key_positions((base + SPAN - REACH + at) * ROWS)
            return fold_block(sub, at, key_pos, low_row, high_row, win, q_st, acc, p_ref, tops, state)

        none = (jnp.full((1, CHUNK), NEG, jnp.float32), jnp.zeros((1, CHUNK), jnp.float32))
        skip = SPAN - REACH
        state = lax.fori_loop(
            jnp.maximum(r_low - skip, 0), jnp.minimum(r_high - skip, NEAR), body, (none,) * CHUNKS
        )
        for c in range(CHUNKS):
            state_ref[0:1, tile_cols(sub, c)] = state[c][0]
            state_ref[1:2, tile_cols(sub, c)] = state[c][1]


def far_kernel(
    place_ref, range_ref, limit_ref, q_st, acc1, state_ref, at3, at4, twin3, twin4, do_ref,
    attn_ref, do_st, stats_ref, dq_acc, ahead_ref, across_ref,
    win, acc, p_ref, tops, dkv,
):
    index = place_ref[0]
    core = place_ref[1]
    base = index - SPAN

    def slot(n):
        return n + core * (FAR - 1 - 2 * n)

    for n, part in enumerate((at4, at3, twin3, twin4)):
        win[pair_of(slot(n)), :] = part[0 : 2 * ROWS, :]
    acc[...] = acc1[...]
    tops[...] = jnp.zeros_like(tops)
    dkv[...] = jnp.zeros_like(dkv)
    dq_acc[...] = jnp.zeros_like(dq_acc)
    stats_ref[...] = jnp.zeros_like(stats_ref)
    side = FAR // 2
    gap = WIDE - FAR
    spans = []
    for sub in range(SUBS):
        r_low = range_ref[2 * sub]
        r_high = range_ref[2 * sub + 1]
        spans.append(((r_low, jnp.minimum(r_high, side)), (jnp.maximum(r_low - gap, side), r_high - gap)))
        low_row = limit_ref[2 * sub : 2 * sub + 1, :]
        high_row = limit_ref[2 * sub + 1 : 2 * sub + 2, :]

        def body(at, state):
            r = jnp.where(at < side, at, at + gap)
            key_pos = key_positions((base + r) * ROWS)
            return fold_block(sub, at, key_pos, low_row, high_row, win, q_st, acc, p_ref, tops, state)

        state = tuple(
            (state_ref[0:1, tile_cols(sub, c)], state_ref[1:2, tile_cols(sub, c)]) for c in range(CHUNKS)
        )
        for lower, upper in spans[sub]:
            state = lax.fori_loop(lower, upper, body, state)
        for c in range(CHUNKS):
            cols = tile_cols(sub, c)
            stats_ref[0:1, cols] = state[c][0]
            stats_ref[1:2, cols] = 1.0 / state[c][1]
        for h in range(GROUPS):
            cols = staged(sub, h)
            attn_t = (acc[:, cols] * stats_ref[1:2, cols]).astype(jnp.bfloat16).astype(jnp.float32)
            attn_ref[sub_rows(sub), head_cols(h)] = attn_t.T.astype(jnp.bfloat16)
            grad = do_ref[sub_rows(sub), head_cols(h)]
            do_st[cols, :] = grad
            stats_ref[2:3, cols] = jnp.sum(attn_t * grad.astype(jnp.float32).T, axis=0, keepdims=True)
    for sub in range(SUBS):
        def back(at, carry):
            back_block(
                sub, at, win, q_st, do_st, p_ref, tops,
                stats_ref[0:1, :], stats_ref[1:2, :], stats_ref[2:3, :], dq_acc, dkv,
            )
            return carry

        for lower, upper in spans[sub]:
            lax.fori_loop(lower, upper, back, 0)
    for n in range(side):
        ahead_ref[pair_of(n), :] = dkv[pair_of(slot(side + n)), :].astype(jnp.bfloat16)
        across_ref[pair_of(n), :] = dkv[pair_of(slot(side - 1 - n)), :].astype(jnp.bfloat16)


def near_backward_kernel(
    place_ref, range_ref, q_st, do_st, win, p_ref, tops, stats_ref, dq_far,
    dq_ref, ahead_ref, across_ref, mid_ref,
    dq_acc, dkv,
):
    way = 1 - 2 * place_ref[1]
    skip = SPAN - REACH
    dkv[...] = jnp.zeros_like(dkv)
    dq_acc[...] = dq_far[...]
    for sub in range(SUBS):
        def back(at, carry):
            back_block(
                sub, at, win, q_st, do_st, p_ref, tops,
                stats_ref[0:1, :], stats_ref[1:2, :], stats_ref[2:3, :], dq_acc, dkv,
            )
            return carry

        lax.fori_loop(
            jnp.maximum(range_ref[2 * sub] - skip, 0), jnp.minimum(range_ref[2 * sub + 1] - skip, NEAR), back, 0
        )
    for sub in range(SUBS):
        for h in range(GROUPS):
            dq_ref[sub_rows(sub), head_cols(h)] = (dq_acc[:, staged(sub, h)] * SCALE).T.astype(jnp.bfloat16)
    mid_ref[...] = dkv[pair_of(REACH), :].astype(jnp.bfloat16)
    for k in range(1, REACH + 1):
        ahead_ref[pair_of(k - 1), :] = dkv[pair_of(REACH + k * way), :].astype(jnp.bfloat16)
        across_ref[pair_of(k - 1), :] = dkv[pair_of(REACH - k * way), :].astype(jnp.bfloat16)


def bf16(*shape):
    return jax.ShapeDtypeStruct(shape, jnp.bfloat16)


def f32(*shape):
    return jax.ShapeDtypeStruct(shape, jnp.float32)


def i32(*shape):
    return jax.ShapeDtypeStruct(shape, jnp.int32)


def near_forward(place, lengths, full, q, own, at1, at2, twin1, twin2):
    return pl.pallas_call(
        near_forward_kernel,
        out_shape=(
            i32(2 * SUBS), i32(8, CHUNK), bf16(STACK, DH), bf16(NEAR * 2 * ROWS, DH),
            f32(DH, STACK), bf16(NEAR * ROWS, STACK), f32(8, STACK), f32(8, STACK),
        ),
        in_specs=[SMEM] + [VMEM] * 8,
        out_specs=(SMEM,) + (VMEM,) * 7,
        compiler_params=pltpu.CompilerParams(vmem_limit_bytes=16 * 1024 * 1024),
        cost_estimate=pl.CostEstimate(flops=10**9, bytes_accessed=6 * 10**6, transcendentals=10**6),
    )(place, lengths, full, q, own, at1, at2, twin1, twin2)


def far_part(place, ranges, limit, q_st, acc, state, at3, at4, twin3, twin4, do):
    return pl.pallas_call(
        far_kernel,
        out_shape=(
            bf16(ROWS, GROUPS * DH), bf16(STACK, DH), f32(8, STACK), f32(DH, STACK),
            bf16(FAR * ROWS, DH), bf16(FAR * ROWS, DH),
        ),
        in_specs=[SMEM, SMEM] + [VMEM] * 9,
        out_specs=(VMEM,) * 6,
        scratch_shapes=[
            pltpu.VMEM((FAR * 2 * ROWS, DH), jnp.bfloat16),
            pltpu.VMEM((DH, STACK), jnp.float32),
            pltpu.VMEM((FAR * ROWS, STACK), jnp.bfloat16),
            pltpu.VMEM((8, STACK), jnp.float32),
            pltpu.VMEM((FAR * 2 * ROWS, DH), jnp.float32),
        ],
        compiler_params=pltpu.CompilerParams(vmem_limit_bytes=16 * 1024 * 1024),
        cost_estimate=pl.CostEstimate(flops=5 * 10**8, bytes_accessed=4 * 10**6, transcendentals=10**6),
    )(place, ranges, limit, q_st, acc, state, at3, at4, twin3, twin4, do)


def near_backward(place, ranges, q_st, do_st, win, p, tops, stats, dq_far):
    return pl.pallas_call(
        near_backward_kernel,
        out_shape=(
            bf16(ROWS, GROUPS * DH), bf16(REACH * 2 * ROWS, DH), bf16(REACH * 2 * ROWS, DH), bf16(2 * ROWS, DH),
        ),
        in_specs=[SMEM, SMEM] + [VMEM] * 7,
        out_specs=(VMEM,) * 4,
        scratch_shapes=[
            pltpu.VMEM((DH, STACK), jnp.float32),
            pltpu.VMEM((NEAR * 2 * ROWS, DH), jnp.float32),
        ],
        compiler_params=pltpu.CompilerParams(vmem_limit_bytes=16 * 1024 * 1024),
        cost_estimate=pl.CostEstimate(flops=2 * 10**9, bytes_accessed=6 * 10**6, transcendentals=10**6),
    )(place, ranges, q_st, do_st, win, p, tops, stats, dq_far)


def small_call(body, out_rows, *args):
    shapes = [jax.ShapeDtypeStruct((rows, DH), jnp.bfloat16) for rows in out_rows]
    return pl.pallas_call(
        body,
        out_shape=shapes,
        in_specs=[VMEM] * len(args),
        out_specs=[VMEM] * len(shapes),
        compiler_params=SMALL,
        cost_estimate=pl.CostEstimate(flops=10**5, bytes_accessed=10**5, transcendentals=0),
    )(*args)


def stacked(*parts):
    n = len(parts)
    total = sum(part.shape[0] for part in parts)

    def body(*refs):
        sems = refs[n + 1]
        copies = []
        at = 0
        for k in range(n):
            rows = parts[k].shape[0]
            copies.append(pltpu.make_async_copy(refs[k], refs[n].at[at : at + rows, :], sems.at[k]))
            copies[k].start()
            at += rows
        for copy in copies:
            copy.wait()

    return pl.pallas_call(
        body,
        out_shape=bf16(total, DH),
        in_specs=[ANY] * n,
        out_specs=ANY,
        scratch_shapes=[pltpu.SemaphoreType.DMA((n,))],
        compiler_params=pltpu.CompilerParams(vmem_limit_bytes=BIG),
        cost_estimate=pl.CostEstimate(flops=0, bytes_accessed=10**6, transcendentals=0),
    )(*parts)


def both_heads(ahead, across, which):
    n = 2 * ROWS

    def body(ahead_ref, across_ref, *out_refs):
        for k, out_ref in zip(which, out_refs):
            out_ref[0:n, :] = ahead_ref[k * n : (k + 1) * n, :]
            out_ref[n : 2 * n, :] = across_ref[k * n : (k + 1) * n, :]

    return small_call(body, [2 * n] * len(which), ahead, across)


def summed(ahead, across, k, *others):
    n = 2 * ROWS

    def body(ahead_ref, across_ref, *refs):
        for at, ref in ((0, ahead_ref), (n, across_ref)):
            total = ref[k * n : (k + 1) * n, :].astype(jnp.float32)
            for other in refs[:-1]:
                total += other[at : at + n, :].astype(jnp.float32)
            refs[-1][at : at + n, :] = total.astype(jnp.bfloat16)

    return small_call(body, [2 * n], ahead, across, *others)[0]


def last_sum(mid, near, far, near_twin, far_twin):
    n = 2 * ROWS

    def body(*refs):
        for out_ref, rows in ((refs[-2], slice(0, ROWS)), (refs[-1], slice(ROWS, n))):
            total = refs[0][rows, :].astype(jnp.float32)
            for ref in refs[1:-2]:
                total += ref[rows, :].astype(jnp.float32)
            out_ref[...] = total.astype(jnp.bfloat16)

    return small_call(body, [ROWS, ROWS], mid, near, far, near_twin, far_twin)


def project_back(core, own, other, w):
    rows, depth = own.shape
    cols = w.shape[1]

    def body(core_ref, own_ref, other_ref, w_ref, out_ref, a_buf, w_buf, sems):
        core = core_ref[0]
        copies = []
        for n, (a_ref, half) in enumerate(((own_ref, core), (other_ref, 1 - core))):
            where = pl.ds(pl.multiple_of(half * depth, depth), depth)
            copies.append(pltpu.make_async_copy(a_ref, a_buf.at[n], sems.at[0, n]))
            copies.append(pltpu.make_async_copy(w_ref.at[where, :], w_buf.at[n], sems.at[1, n]))
        for copy in copies:
            copy.start()
        copies[0].wait()
        copies[1].wait()
        part = dot_nn(a_buf[0], w_buf[0])
        copies[2].wait()
        copies[3].wait()
        out_ref[...] = (part + dot_nn(a_buf[1], w_buf[1])).astype(jnp.bfloat16)

    return pl.pallas_call(
        body,
        out_shape=bf16(rows, cols),
        in_specs=[SMEM, ANY, ANY, ANY],
        out_specs=VMEM,
        scratch_shapes=[
            pltpu.VMEM((2, rows, depth), jnp.bfloat16),
            pltpu.VMEM((2, depth, cols), jnp.bfloat16),
            pltpu.SemaphoreType.DMA((2, 2)),
        ],
        compiler_params=pltpu.CompilerParams(vmem_limit_bytes=BIG),
        cost_estimate=pl.CostEstimate(flops=4 * rows * depth * cols, bytes_accessed=6 * 10**6, transcendentals=0),
    )(core, own, other, w)


def project(half, attn, w, other=None):
    rows, depth = attn.shape
    cols = w.shape[0] // 2
    parts = 4
    wide = cols // parts
    more = () if other is None else (other,)

    def body(half_ref, a_ref, w_ref, *refs):
        out_ref, w_buf, sems = refs[-3:]
        copies = []
        for n in range(parts):
            where = pl.ds(pl.multiple_of(half_ref[0] * cols + n * wide, wide), wide)
            copies.append(pltpu.make_async_copy(w_ref.at[where, :], w_buf.at[n], sems.at[n]))
            copies[n].start()
        for n in range(parts):
            copies[n].wait()
            at = slice(n * wide, (n + 1) * wide)
            out = dot_nt(a_ref[...], w_buf[n])
            if more:
                out += refs[0][:, at].astype(jnp.float32)
            out_ref[:, at] = out.astype(jnp.bfloat16)

    return pl.pallas_call(
        body,
        out_shape=bf16(rows, cols),
        in_specs=[SMEM, VMEM, ANY] + [VMEM] * len(more),
        out_specs=VMEM,
        scratch_shapes=[pltpu.VMEM((parts, wide, depth), jnp.bfloat16), pltpu.SemaphoreType.DMA((parts,))],
        compiler_params=pltpu.CompilerParams(vmem_limit_bytes=BIG),
        cost_estimate=pl.CostEstimate(flops=2 * rows * depth * cols, bytes_accessed=4 * 10**6, transcendentals=0),
    )(half, attn, w, *more)


def on_device(queries, keys, values, out_weight, doc_lengths, doc_full, out_grad):
    devices = lax.axis_size("cp")
    index = lax.axis_index("cp").astype(jnp.int32)
    core = lax.axis_index("hd").astype(jnp.int32)
    place = jnp.stack([index, core])
    core = core.reshape(1)
    half = 2 * ROWS

    def step(block, far):
        ways = [(2 * i, 2 * (i + far)) for i in range(devices - far)]
        ways += [(2 * (i + far) + 1, 2 * i + 1) for i in range(devices - far)]
        return lax.ppermute(block, ("cp", "hd"), ways)

    def twin(block):
        return lax.ppermute(block, "hd", [(0, 1), (1, 0)])

    other_keys, other_values, late_grad = lax.optimization_barrier((twin(keys), twin(values), out_grad))
    block = stacked(keys, values, other_keys, other_values)
    other_grad = twin(late_grad)
    at2 = step(block, 2)
    at1 = step(block, 1)
    attn_grad = project_back(core, out_grad, other_grad, out_weight)
    at2, attn_grad = lax.optimization_barrier((at2, attn_grad))
    at4 = step(at2, 2)
    at3 = step(at2, 1)
    twin1, twin2 = twin(at1[half:]), twin(at2[half:])
    ranges, limit, q_st, win, acc, p, tops, state = near_forward(
        place, doc_lengths.reshape(1, -1), doc_full.reshape(1, -1), queries, block, at1, at2, twin1, twin2
    )
    at3, at4, state = lax.optimization_barrier((at3, at4, state))
    twin3, twin4 = twin(at3[half:]), twin(at4[half:])
    attn, do_st, stats, dq_far, ahead, across = far_part(
        place, ranges, limit, q_st, acc, state, at3, at4, twin3, twin4, attn_grad
    )
    out3, out4 = both_heads(ahead, twin(across), (0, 1))
    in4 = step(out4, 2)
    in3 = step(out3, 1)
    query_grad, ahead, across, mid = near_backward(place, ranges, q_st, do_st, win, p, tops, stats, dq_far)
    attn, across = lax.optimization_barrier((attn, twin(across)))
    far = step(summed(ahead, across, 1, in4, in3), 2)
    near = step(both_heads(ahead, across, (0,))[0], 1)
    away = project(1 - core, attn, out_weight)
    layer_out = project(core, attn, out_weight, twin(away))
    far, near, layer_out = lax.optimization_barrier((far, near, layer_out))
    key_grad, value_grad = last_sum(mid, near, far, twin(near[half:]), twin(far[half:]))
    return (layer_out, query_grad, key_grad, value_grad)


def solution(mesh):
    placed = (P("cp", "hd"), P("cp", "hd"), P("cp", "hd"), P(None, "hd"), P(), P(), P("cp", "hd"))
    return jax.shard_map(
        on_device,
        mesh=mesh,
        in_specs=placed,
        out_specs=(P("cp", "hd"), P("cp", "hd"), P("cp", "hd"), P("cp", "hd")),
        check_vma=False,
    )
```

```python
import math

import jax
import jax.numpy as jnp
from jax import lax
from jax.experimental import pallas as pl
from jax.experimental.pallas import tpu as pltpu
from jax.sharding import PartitionSpec as P

HQ = 8
HK = 2
DH = 128
SPAN = 4
ROWS = 256
GROUPS = HQ // HK
WIDE = 2 * SPAN + 1
PAIR = 2 * ROWS
REACH = 2
NEAR = 2 * REACH + 1
FAR = WIDE - NEAR
SIDE = FAR // 2
SUB = 128
SUBS = ROWS // SUB
TILE = GROUPS * SUB
CHUNK = 256
CHUNKS = TILE // CHUNK
STACK = SUBS * TILE
NEG = -1e30
BIG = 60 * 1024 * 1024
SCALE = 1.0 / math.sqrt(DH)
SCALE2 = SCALE / math.log(2.0)
VMEM = pl.BlockSpec(memory_space=pltpu.VMEM)
ANY = pl.BlockSpec(memory_space=pl.ANY)
SMALL = pltpu.CompilerParams(vmem_limit_bytes=4 * 1024 * 1024)
SMEM = pl.BlockSpec(memory_space=pltpu.SMEM)


def dot_nn(a, b):
    return lax.dot_general(a, b, (((1,), (0,)), ((), ())), preferred_element_type=jnp.float32)


def dot_nt(a, b):
    return lax.dot_general(a, b, (((1,), (1,)), ((), ())), preferred_element_type=jnp.float32)


def limits(index, lengths_row, full_row):
    n = lengths_row.shape[1]
    row = lax.broadcasted_iota(jnp.int32, (n, n), 0)
    col = lax.broadcasted_iota(jnp.int32, (n, n), 1)
    ends = jnp.sum(jnp.where(col <= row, lengths_row, 0), axis=1, keepdims=True)
    starts = jnp.sum(jnp.where(col < row, lengths_row, 0), axis=1, keepdims=True)
    full = jnp.sum(jnp.where(col == row, full_row, 0), axis=1, keepdims=True)
    pos = index * ROWS + lax.broadcasted_iota(jnp.int32, (n, ROWS), 1)
    inside = (pos >= starts) & (pos < ends)
    low = jnp.sum(jnp.where(inside, starts, 0), axis=0, keepdims=True)
    high = jnp.sum(jnp.where(inside, jnp.where(full == 1, ends, pos + 1), 0), axis=0, keepdims=True)
    return low, high


def rows_of(r):
    return pl.ds(pl.multiple_of(r * ROWS, ROWS), ROWS)


def keys_of(r):
    return pl.ds(pl.multiple_of(r * 2 * ROWS, ROWS), ROWS)


def vals_of(r):
    return pl.ds(pl.multiple_of(r * 2 * ROWS + ROWS, ROWS), ROWS)


def pair_of(r):
    return pl.ds(pl.multiple_of(r * PAIR, ROWS), PAIR)


def staged(sub, h):
    return slice(sub * TILE + h * SUB, sub * TILE + (h + 1) * SUB)


def sub_rows(sub):
    return slice(sub * SUB, (sub + 1) * SUB)


def head_cols(h):
    return slice(h * DH, (h + 1) * DH)


def chunks_of(subs):
    return range(subs[0] * CHUNKS, (subs[-1] + 1) * CHUNKS)


def chunk_cols(c):
    return slice(c * CHUNK, (c + 1) * CHUNK)


def segments_of(range_ref):
    low0, high0, low1, high1 = [range_ref[n] for n in range(4)]
    return (
        ((0,), low0, jnp.minimum(low1, high0)),
        ((0, 1), low1, high0),
        ((1,), jnp.maximum(low1, high0), high1),
    )


def every_near(range_ref, make, state):
    skip = SPAN - REACH
    for subs, lower, upper in segments_of(range_ref):
        state = lax.fori_loop(jnp.maximum(lower - skip, 0), jnp.minimum(upper - skip, NEAR), make(subs), state)
    return state


def every_far(range_ref, make, state):
    end = SPAN + REACH + 1
    for subs, lower, upper in segments_of(range_ref):
        first = jnp.where(lower < SIDE, lower, jnp.maximum(lower, end) - NEAR)
        last = jnp.where(upper > end, upper - NEAR, jnp.minimum(upper, SIDE))
        state = lax.fori_loop(first, last, make(subs), state)
    return state


def score_block(subs, at, first_key, limit_ref, win, q_st, s_ref, top):
    keys = win[keys_of(at), :]
    key_pos = first_key + lax.broadcasted_iota(jnp.int32, (ROWS, CHUNK), 0)
    valid = {
        sub: (key_pos >= limit_ref[2 * sub : 2 * sub + 1, :]) & (key_pos < limit_ref[2 * sub + 1 : 2 * sub + 2, :])
        for sub in subs
    }
    out = list(top)
    for c in chunks_of(subs):
        s = dot_nt(keys, q_st[chunk_cols(c), :]) * SCALE2
        s = jnp.where(valid[c // CHUNKS], s, NEG)
        s_ref[rows_of(at), chunk_cols(c)] = s
        out[c] = jnp.maximum(top[c], jnp.max(s, axis=0, keepdims=True))
    return tuple(out)


def weigh_block(subs, at, win, s_ref, p_ref, acc, top, total):
    vals_t = win[vals_of(at), :].T
    out = list(total)
    for c in chunks_of(subs):
        cols = chunk_cols(c)
        p = jnp.exp2(s_ref[rows_of(at), cols] - top[c])
        out[c] = total[c] + jnp.sum(p, axis=0, keepdims=True)
        p = p.astype(jnp.bfloat16)
        p_ref[rows_of(at), cols] = p
        acc[:, cols] += dot_nn(vals_t, p)
    return tuple(out)


def back_block(subs, at, win, p_ref, do_st, qs_st, dos_st, stats_ref, ds_scr, dq_acc, out_win):
    keys_t = win[keys_of(at), :].T
    vals = win[vals_of(at), :]
    for c in chunks_of(subs):
        cols = chunk_cols(c)
        dp = dot_nt(vals, do_st[cols, :])
        ds = (p_ref[rows_of(at), cols].astype(jnp.float32) * (dp - stats_ref[1:2, cols])).astype(jnp.bfloat16)
        ds_scr[:, cols] = ds
        dq_acc[:, cols] += dot_nn(keys_t, ds)
    cols = slice(subs[0] * TILE, (subs[-1] + 1) * TILE)
    out_win[keys_of(at), :] = dot_nn(ds_scr[:, cols], qs_st[cols, :]).astype(jnp.bfloat16)
    out_win[vals_of(at), :] = dot_nn(p_ref[rows_of(at), cols], dos_st[cols, :]).astype(jnp.bfloat16)


def near_scores_kernel(
    place_ref, len_ref, full_ref, q_ref, own_ref, at1_ref, at2_ref, twin1_ref, twin2_ref,
    range_ref, limit_ref, q_st, win, s_ref, top_ref,
):
    way = 1 - 2 * place_ref[1]
    base = place_ref[0] - SPAN
    low, high = limits(place_ref[0], len_ref[...], full_ref[...])
    for sub in range(SUBS):
        cut = sub_rows(sub)
        limit_ref[2 * sub : 2 * sub + 1, :] = jnp.concatenate([low[:, cut]] * (CHUNK // SUB), axis=1)
        limit_ref[2 * sub + 1 : 2 * sub + 2, :] = jnp.concatenate([high[:, cut]] * (CHUNK // SUB), axis=1)
        range_ref[2 * sub] = jnp.maximum(jnp.min(low[:, cut]) // ROWS - base, 0)
        range_ref[2 * sub + 1] = jnp.minimum((jnp.max(high[:, cut]) + ROWS - 1) // ROWS - base, WIDE)
        for h in range(GROUPS):
            q_st[staged(sub, h), :] = q_ref[cut, head_cols(h)]
    win[pair_of(REACH), :] = own_ref[0:PAIR, :]
    for k, ring, twin in ((1, at1_ref, twin1_ref), (2, at2_ref, twin2_ref)):
        win[pair_of(REACH - k * way), :] = ring[0:PAIR, :]
        win[pair_of(REACH + k * way), :] = twin[...]

    def scores(subs):
        def body(at, top):
            first_key = (base + SPAN - REACH + at) * ROWS
            return score_block(subs, at, first_key, limit_ref, win, q_st, s_ref, top)

        return body

    none = jnp.full((1, CHUNK), NEG, jnp.float32)
    top = every_near(range_ref, scores, (none,) * (SUBS * CHUNKS))
    for c in range(SUBS * CHUNKS):
        top_ref[0:1, chunk_cols(c)] = top[c]


def middle_kernel(
    place_ref, range_ref, limit_ref, q_st, near_win, near_s, top_ref, at3_ref, at4_ref, twin3_ref, twin4_ref, do_ref,
    attn_ref, do_st, qs_st, dos_st, near_p, stats_ref, dq_acc, ahead_ref, across_ref,
    win, out_win, s_scr, p_scr, ds_scr, acc,
):
    core = place_ref[1]
    base = place_ref[0] - SPAN

    def slot(n):
        return n + core * (FAR - 1 - 2 * n)

    for n, ref in enumerate((at4_ref, at3_ref, twin3_ref, twin4_ref)):
        win[pair_of(slot(n)), :] = ref[0:PAIR, :]
    for sub in range(SUBS):
        for h in range(GROUPS):
            do_st[staged(sub, h), :] = do_ref[sub_rows(sub), head_cols(h)]

    def scores(subs):
        def body(at, top):
            first_key = (base + jnp.where(at < SIDE, at, at + NEAR)) * ROWS
            return score_block(subs, at, first_key, limit_ref, win, q_st, s_scr, top)

        return body

    top = tuple(top_ref[0:1, chunk_cols(c)] for c in range(SUBS * CHUNKS))
    top = every_far(range_ref, scores, top)
    acc[...] = jnp.zeros_like(acc)

    def weigh(subs):
        return lambda at, total: weigh_block(subs, at, near_win, near_s, near_p, acc, top, total)

    def weigh_far(subs):
        return lambda at, total: weigh_block(subs, at, win, s_scr, p_scr, acc, top, total)

    total = every_near(range_ref, weigh, (jnp.zeros((1, CHUNK), jnp.float32),) * (SUBS * CHUNKS))
    total = every_far(range_ref, weigh_far, total)
    for c in range(SUBS * CHUNKS):
        stats_ref[0:1, chunk_cols(c)] = 1.0 / total[c]
    for sub in range(SUBS):
        for h in range(GROUPS):
            cols = staged(sub, h)
            inv = stats_ref[0:1, cols]
            attn_t = (acc[:, cols] * inv).astype(jnp.bfloat16).astype(jnp.float32)
            attn_ref[sub_rows(sub), head_cols(h)] = attn_t.T.astype(jnp.bfloat16)
            grad = do_st[cols, :].astype(jnp.float32)
            stats_ref[1:2, cols] = jnp.sum(attn_t * grad.T, axis=0, keepdims=True)
            inv_col = jnp.broadcast_to(inv, (DH, SUB)).T
            dos_st[cols, :] = (grad * inv_col).astype(jnp.bfloat16)
            qs_st[cols, :] = (q_st[cols, :].astype(jnp.float32) * (inv_col * SCALE)).astype(jnp.bfloat16)
    dq_acc[...] = jnp.zeros_like(dq_acc)
    out_win[...] = jnp.zeros_like(out_win)

    def back(subs):
        def body(at, carry):
            back_block(subs, at, win, p_scr, do_st, qs_st, dos_st, stats_ref, ds_scr, dq_acc, out_win)
            return carry

        return body

    every_far(range_ref, back, 0)
    for n in range(SIDE):
        ahead_ref[n * PAIR : (n + 1) * PAIR, :] = out_win[pair_of(slot(FAR - 1 - n)), :]
        across_ref[n * PAIR : (n + 1) * PAIR, :] = out_win[pair_of(slot(n)), :]


def near_back_kernel(
    place_ref, range_ref, win, p_ref, do_st, qs_st, dos_st, stats_ref, dq_far,
    dq_ref, ahead_ref, across_ref, mid_ref,
    out_win, ds_scr, dq_acc,
):
    way = 1 - 2 * place_ref[1]
    dq_acc[...] = dq_far[...]
    out_win[...] = jnp.zeros_like(out_win)

    def back(subs):
        def body(at, carry):
            back_block(subs, at, win, p_ref, do_st, qs_st, dos_st, stats_ref, ds_scr, dq_acc, out_win)
            return carry

        return body

    every_near(range_ref, back, 0)
    mid_ref[...] = out_win[pair_of(REACH), :]
    for n in range(REACH):
        k = REACH - n
        ahead_ref[n * PAIR : (n + 1) * PAIR, :] = out_win[pair_of(REACH + k * way), :]
        across_ref[n * PAIR : (n + 1) * PAIR, :] = out_win[pair_of(REACH - k * way), :]
    for sub in range(SUBS):
        for h in range(GROUPS):
            cols = staged(sub, h)
            dq = dq_acc[:, cols] * (stats_ref[0:1, cols] * SCALE)
            dq_ref[sub_rows(sub), head_cols(h)] = dq.T.astype(jnp.bfloat16)


def bf16(*shape):
    return jax.ShapeDtypeStruct(shape, jnp.bfloat16)


def f32(*shape):
    return jax.ShapeDtypeStruct(shape, jnp.float32)


def i32(*shape):
    return jax.ShapeDtypeStruct(shape, jnp.int32)


def near_scores(*args):
    return pl.pallas_call(
        near_scores_kernel,
        out_shape=(
            i32(4), i32(8, CHUNK), bf16(STACK, DH), bf16(NEAR * PAIR, DH), f32(NEAR * ROWS, STACK), f32(8, STACK),
        ),
        in_specs=[SMEM] + [VMEM] * 8,
        out_specs=(SMEM,) + (VMEM,) * 5,
        compiler_params=pltpu.CompilerParams(vmem_limit_bytes=16 * 1024 * 1024),
        cost_estimate=pl.CostEstimate(flops=10**9, bytes_accessed=6 * 10**6, transcendentals=0),
    )(*args)


def middle(*args):
    return pl.pallas_call(
        middle_kernel,
        out_shape=(
            bf16(ROWS, GROUPS * DH), bf16(STACK, DH), bf16(STACK, DH), bf16(STACK, DH), bf16(NEAR * ROWS, STACK),
            f32(8, STACK), f32(DH, STACK), bf16(SIDE * PAIR, DH), bf16(SIDE * PAIR, DH),
        ),
        in_specs=[SMEM, SMEM] + [VMEM] * 10,
        out_specs=(VMEM,) * 9,
        scratch_shapes=[
            pltpu.VMEM((FAR * PAIR, DH), jnp.bfloat16),
            pltpu.VMEM((FAR * PAIR, DH), jnp.bfloat16),
            pltpu.VMEM((FAR * ROWS, STACK), jnp.float32),
            pltpu.VMEM((FAR * ROWS, STACK), jnp.bfloat16),
            pltpu.VMEM((ROWS, STACK), jnp.bfloat16),
            pltpu.VMEM((DH, STACK), jnp.float32),
        ],
        compiler_params=pltpu.CompilerParams(vmem_limit_bytes=26 * 1024 * 1024),
        cost_estimate=pl.CostEstimate(flops=10**9, bytes_accessed=6 * 10**6, transcendentals=10**6),
    )(*args)


def near_back(*args):
    return pl.pallas_call(
        near_back_kernel,
        out_shape=(bf16(ROWS, GROUPS * DH), bf16(REACH * PAIR, DH), bf16(REACH * PAIR, DH), bf16(PAIR, DH)),
        in_specs=[SMEM, SMEM] + [VMEM] * 7,
        out_specs=(VMEM,) * 4,
        scratch_shapes=[
            pltpu.VMEM((NEAR * PAIR, DH), jnp.bfloat16),
            pltpu.VMEM((ROWS, STACK), jnp.bfloat16),
            pltpu.VMEM((DH, STACK), jnp.float32),
        ],
        compiler_params=pltpu.CompilerParams(vmem_limit_bytes=16 * 1024 * 1024),
        cost_estimate=pl.CostEstimate(flops=2 * 10**10, bytes_accessed=3 * 10**7, transcendentals=0),
    )(*args)


def small_call(body, out_rows, *args):
    shapes = [jax.ShapeDtypeStruct((rows, DH), jnp.bfloat16) for rows in out_rows]
    return pl.pallas_call(
        body,
        out_shape=shapes,
        in_specs=[VMEM] * len(args),
        out_specs=[VMEM] * len(shapes),
        compiler_params=SMALL,
        cost_estimate=pl.CostEstimate(flops=10**5, bytes_accessed=10**5, transcendentals=0),
    )(*args)


def stacked(*parts):
    def body(*refs):
        at = 0
        for ref in refs[:-1]:
            refs[-1][at : at + ref.shape[0], :] = ref[...]
            at += ref.shape[0]

    return small_call(body, [sum(part.shape[0] for part in parts)], *parts)[0]


def far_and_near(ahead, across, came):
    def body(ahead_ref, across_ref, came_ref, far_ref, near_ref):
        for n, ref in enumerate((ahead_ref, across_ref)):
            at = slice(n * PAIR, (n + 1) * PAIR)
            far_ref[at, :] = (ref[0:PAIR, :].astype(jnp.float32) + came_ref[at, :].astype(jnp.float32)).astype(jnp.bfloat16)
            near_ref[at, :] = ref[PAIR : 2 * PAIR, :]

    return small_call(body, [2 * PAIR] * 2, ahead, across, came)


def packed(*parts):
    n = len(parts)
    rows = parts[0].shape[0]

    def body(*refs):
        copies = [
            pltpu.make_async_copy(refs[k], refs[n].at[k * rows : (k + 1) * rows, :], refs[n + 1].at[k]) for k in range(n)
        ]
        for copy in copies:
            copy.start()
        for copy in copies:
            copy.wait()

    return pl.pallas_call(
        body,
        out_shape=bf16(n * rows, DH),
        in_specs=[ANY] * n,
        out_specs=VMEM,
        scratch_shapes=[pltpu.SemaphoreType.DMA((n,))],
        compiler_params=pltpu.CompilerParams(vmem_limit_bytes=BIG),
        cost_estimate=pl.CostEstimate(flops=0, bytes_accessed=10**6, transcendentals=0),
    )(*parts)


def both_heads(ahead, across):
    def body(ahead_ref, across_ref, *out_refs):
        for n, out_ref in enumerate(out_refs):
            out_ref[0:PAIR, :] = ahead_ref[n * PAIR : (n + 1) * PAIR, :]
            out_ref[PAIR : 2 * PAIR, :] = across_ref[n * PAIR : (n + 1) * PAIR, :]

    return small_call(body, [2 * PAIR] * 2, ahead, across)


def summed(*parts):
    def body(*refs):
        total = refs[0][...].astype(jnp.float32)
        for ref in refs[1:-1]:
            total += ref[...].astype(jnp.float32)
        refs[-1][...] = total.astype(jnp.bfloat16)

    return small_call(body, [parts[0].shape[0]], *parts)[0]


def last_sum(*parts):
    def body(*refs):
        for at, out_ref in ((0, refs[-2]), (ROWS, refs[-1])):
            total = refs[0][at : at + ROWS, :].astype(jnp.float32)
            for ref in refs[1:-2]:
                total += ref[at : at + ROWS, :].astype(jnp.float32)
            out_ref[...] = total.astype(jnp.bfloat16)

    return small_call(body, [ROWS, ROWS], *parts)


def half_of(core, size):
    return pl.ds(pl.multiple_of(core * size, size), size)


def project_back(core, own, other, w):
    rows, depth = own.shape
    cols = w.shape[1]

    def body(core_ref, own_ref, other_ref, w_ref, out_ref):
        core = core_ref[0]
        part = dot_nn(own_ref[...], w_ref[half_of(core, depth), :])
        out_ref[...] = (part + dot_nn(other_ref[...], w_ref[half_of(1 - core, depth), :])).astype(jnp.bfloat16)

    return pl.pallas_call(
        body,
        out_shape=bf16(rows, cols),
        in_specs=[SMEM, VMEM, VMEM, VMEM],
        out_specs=VMEM,
        compiler_params=pltpu.CompilerParams(vmem_limit_bytes=12 * 1024 * 1024),
        cost_estimate=pl.CostEstimate(flops=4 * rows * depth * cols, bytes_accessed=6 * 10**6, transcendentals=0),
    )(core, own, other, w)


def project(half, attn, w, other=None):
    rows, depth = attn.shape
    cols = w.shape[0] // 2
    more = () if other is None else (other,)

    def body(half_ref, a_ref, w_ref, *refs):
        out = dot_nt(a_ref[...], w_ref[half_of(half_ref[0], cols), :])
        if more:
            out += refs[0][...].astype(jnp.float32)
        refs[-1][...] = out.astype(jnp.bfloat16)

    return pl.pallas_call(
        body,
        out_shape=bf16(rows, cols),
        in_specs=[SMEM, VMEM, VMEM] + [VMEM] * len(more),
        out_specs=VMEM,
        compiler_params=pltpu.CompilerParams(vmem_limit_bytes=12 * 1024 * 1024),
        cost_estimate=pl.CostEstimate(flops=2 * rows * depth * cols, bytes_accessed=4 * 10**6, transcendentals=0),
    )(half, attn, w, *more)


def on_device(queries, keys, values, out_weight, doc_lengths, doc_full, out_grad):
    devices = lax.axis_size("cp")
    index = lax.axis_index("cp").astype(jnp.int32)
    core = lax.axis_index("hd").astype(jnp.int32)
    place = jnp.stack([index, core])
    core = core.reshape(1)

    def step(block, far):
        ways = [(2 * i, 2 * (i + far)) for i in range(devices - far)]
        ways += [(2 * (i + far) + 1, 2 * i + 1) for i in range(devices - far)]
        return lax.ppermute(block, ("cp", "hd"), ways)

    def twin(block):
        return lax.ppermute(block, "hd", [(0, 1), (1, 0)])

    own = packed(keys, values)
    other_keys, other_values, late_grad, own = lax.optimization_barrier((twin(keys), twin(values), out_grad, own))
    block = stacked(own, other_keys, other_values)
    other_grad = twin(late_grad)
    at2 = step(block, 2)
    at1 = step(block, 1)
    attn_grad = project_back(core, out_grad, other_grad, out_weight)
    at2, attn_grad = lax.optimization_barrier((at2, attn_grad))
    at4 = step(at2, 2)
    at3 = step(at2, 1)
    ranges, limit, q_st, win, s, top = near_scores(
        place, doc_lengths.reshape(1, -1), doc_full.reshape(1, -1), queries,
        own, at1, at2, twin(at1[PAIR:]), twin(at2[PAIR:]),
    )
    at4, top = lax.optimization_barrier((at4, top))
    at3, twin4 = lax.optimization_barrier((at3, twin(at4[PAIR:])))
    attn, do_st, qs_st, dos_st, p, stats, dq_far, ahead, across = middle(
        place, ranges, limit, q_st, win, s, top, at3, at4, twin(at3[PAIR:]), twin4, attn_grad
    )
    away = project(1 - core, attn, out_weight)
    across, away = lax.optimization_barrier((twin(across), away))
    out4, out3 = both_heads(ahead, across)
    out4, out3, stats = lax.optimization_barrier((out4, out3, stats))
    in4 = step(out4, 2)
    in3 = step(out3, 1)
    query_grad, ahead, across, mid = near_back(place, ranges, win, p, do_st, qs_st, dos_st, stats, dq_far)
    came = summed(in4, in3)
    came, across = lax.optimization_barrier((came, twin(across)))
    far_out, near_out = far_and_near(ahead, across, came)
    far_out, away = lax.optimization_barrier((far_out, away))
    far = step(far_out, 2)
    near = step(near_out, 1)
    layer_out = project(core, attn, out_weight, twin(away))
    near, layer_out = lax.optimization_barrier((near, layer_out))
    far, near_twin = lax.optimization_barrier((far, twin(near[PAIR:])))
    key_grad, value_grad = last_sum(mid, near, far, near_twin, twin(far[PAIR:]))
    return (layer_out, query_grad, key_grad, value_grad)


def solution(mesh):
    placed = (P("cp", "hd"), P("cp", "hd"), P("cp", "hd"), P(None, "hd"), P(), P(), P("cp", "hd"))
    return jax.shard_map(
        on_device,
        mesh=mesh,
        in_specs=placed,
        out_specs=(P("cp", "hd"), P("cp", "hd"), P("cp", "hd"), P("cp", "hd")),
        check_vma=False,
    )
```

```python
import math

import jax
import jax.numpy as jnp
from jax import lax
from jax.experimental import pallas as pl
from jax.experimental.pallas import tpu as pltpu
from jax.sharding import PartitionSpec as P

HQ = 8
HK = 2
DH = 128
SPAN = 4
ROWS = 256
GROUPS = HQ // HK
WIDE = 2 * SPAN + 1
PAIR = 2 * ROWS
REACH = 2
NEAR = 2 * REACH + 1
FAR = WIDE - NEAR
SIDE = FAR // 2
SUB = 128
SUBS = ROWS // SUB
TILE = GROUPS * SUB
CHUNK = 256
CHUNKS = TILE // CHUNK
STACK = SUBS * TILE
NEG = -1e30
BIG = 60 * 1024 * 1024
SCALE = 1.0 / math.sqrt(DH)
SCALE2 = SCALE / math.log(2.0)
VMEM = pl.BlockSpec(memory_space=pltpu.VMEM)
ANY = pl.BlockSpec(memory_space=pl.ANY)
SMALL = pltpu.CompilerParams(vmem_limit_bytes=4 * 1024 * 1024)
SMEM = pl.BlockSpec(memory_space=pltpu.SMEM)


def dot_nn(a, b):
    return lax.dot_general(a, b, (((1,), (0,)), ((), ())), preferred_element_type=jnp.float32)


def dot_nt(a, b):
    return lax.dot_general(a, b, (((1,), (1,)), ((), ())), preferred_element_type=jnp.float32)


def limits(index, lengths_row, full_row):
    n = lengths_row.shape[1]
    row = lax.broadcasted_iota(jnp.int32, (n, n), 0)
    col = lax.broadcasted_iota(jnp.int32, (n, n), 1)
    ends = jnp.sum(jnp.where(col <= row, lengths_row, 0), axis=1, keepdims=True)
    starts = jnp.sum(jnp.where(col < row, lengths_row, 0), axis=1, keepdims=True)
    full = jnp.sum(jnp.where(col == row, full_row, 0), axis=1, keepdims=True)
    pos = index * ROWS + lax.broadcasted_iota(jnp.int32, (n, ROWS), 1)
    inside = (pos >= starts) & (pos < ends)
    low = jnp.sum(jnp.where(inside, starts, 0), axis=0, keepdims=True)
    high = jnp.sum(jnp.where(inside, jnp.where(full == 1, ends, pos + 1), 0), axis=0, keepdims=True)
    return low, high


def rows_of(r):
    return pl.ds(pl.multiple_of(r * ROWS, ROWS), ROWS)


def keys_of(r):
    return pl.ds(pl.multiple_of(r * 2 * ROWS, ROWS), ROWS)


def vals_of(r):
    return pl.ds(pl.multiple_of(r * 2 * ROWS + ROWS, ROWS), ROWS)


def pair_of(r):
    return pl.ds(pl.multiple_of(r * PAIR, ROWS), PAIR)


def staged(sub, h):
    return slice(sub * TILE + h * SUB, sub * TILE + (h + 1) * SUB)


def sub_rows(sub):
    return slice(sub * SUB, (sub + 1) * SUB)


def head_cols(h):
    return slice(h * DH, (h + 1) * DH)


def chunks_of(subs):
    return range(subs[0] * CHUNKS, (subs[-1] + 1) * CHUNKS)


def chunk_cols(c):
    return slice(c * CHUNK, (c + 1) * CHUNK)


def segments_of(range_ref):
    low0, high0, low1, high1 = [range_ref[n] for n in range(4)]
    return (
        ((0,), low0, jnp.minimum(low1, high0)),
        ((0, 1), low1, high0),
        ((1,), jnp.maximum(low1, high0), high1),
    )


def every_near(range_ref, make, state):
    skip = SPAN - REACH
    for subs, lower, upper in segments_of(range_ref):
        state = lax.fori_loop(jnp.maximum(lower - skip, 0), jnp.minimum(upper - skip, NEAR), make(subs), state)
    return state


def every_far(range_ref, make, state):
    end = SPAN + REACH + 1
    for subs, lower, upper in segments_of(range_ref):
        first = jnp.where(lower < SIDE, lower, jnp.maximum(lower, end) - NEAR)
        last = jnp.where(upper > end, upper - NEAR, jnp.minimum(upper, SIDE))
        state = lax.fori_loop(first, last, make(subs), state)
    return state


def score_block(subs, at, first_key, limit_ref, win, q_st, s_ref, top):
    keys = win[keys_of(at), :]
    key_pos = first_key + lax.broadcasted_iota(jnp.int32, (ROWS, CHUNK), 0)
    valid = {
        sub: (key_pos >= limit_ref[2 * sub : 2 * sub + 1, :]) & (key_pos < limit_ref[2 * sub + 1 : 2 * sub + 2, :])
        for sub in subs
    }
    out = list(top)
    for c in chunks_of(subs):
        s = dot_nt(keys, q_st[chunk_cols(c), :]) * SCALE2
        s = jnp.where(valid[c // CHUNKS], s, NEG)
        s_ref[rows_of(at), chunk_cols(c)] = s
        out[c] = jnp.maximum(top[c], jnp.max(s, axis=0, keepdims=True))
    return tuple(out)


def weigh_block(subs, at, win, s_ref, p_ref, acc, top, total):
    vals_t = win[vals_of(at), :].T
    out = list(total)
    for c in chunks_of(subs):
        cols = chunk_cols(c)
        p = jnp.exp2(s_ref[rows_of(at), cols] - top[c])
        out[c] = total[c] + jnp.sum(p, axis=0, keepdims=True)
        p = p.astype(jnp.bfloat16)
        p_ref[rows_of(at), cols] = p
        acc[:, cols] += dot_nn(vals_t, p)
    return tuple(out)


def back_block(subs, at, win, p_ref, do_st, qs_st, dos_st, stats_ref, ds_scr, dq_acc, out_win):
    keys_t = win[keys_of(at), :].T
    vals = win[vals_of(at), :]
    for c in chunks_of(subs):
        cols = chunk_cols(c)
        dp = dot_nt(vals, do_st[cols, :])
        ds = (p_ref[rows_of(at), cols].astype(jnp.float32) * (dp - stats_ref[1:2, cols])).astype(jnp.bfloat16)
        ds_scr[:, cols] = ds
        dq_acc[:, cols] += dot_nn(keys_t, ds)
    cols = slice(subs[0] * TILE, (subs[-1] + 1) * TILE)
    out_win[keys_of(at), :] = dot_nn(ds_scr[:, cols], qs_st[cols, :]).astype(jnp.bfloat16)
    out_win[vals_of(at), :] = dot_nn(p_ref[rows_of(at), cols], dos_st[cols, :]).astype(jnp.bfloat16)


def near_scores_kernel(
    place_ref, len_ref, full_ref, q_ref, own_ref, at1_ref, twin1_ref, at2_ref, other2_ref,
    range_ref, limit_ref, q_st, win, s_ref, top_ref,
):
    way = 1 - 2 * place_ref[1]
    base = place_ref[0] - SPAN
    low, high = limits(place_ref[0], len_ref[...], full_ref[...])
    for sub in range(SUBS):
        cut = sub_rows(sub)
        limit_ref[2 * sub : 2 * sub + 1, :] = jnp.concatenate([low[:, cut]] * (CHUNK // SUB), axis=1)
        limit_ref[2 * sub + 1 : 2 * sub + 2, :] = jnp.concatenate([high[:, cut]] * (CHUNK // SUB), axis=1)
        range_ref[2 * sub] = jnp.maximum(jnp.min(low[:, cut]) // ROWS - base, 0)
        range_ref[2 * sub + 1] = jnp.minimum((jnp.max(high[:, cut]) + ROWS - 1) // ROWS - base, WIDE)
        for h in range(GROUPS):
            q_st[staged(sub, h), :] = q_ref[cut, head_cols(h)]
    win[pair_of(REACH), :] = own_ref[0:PAIR, :]
    win[pair_of(REACH - way), :] = at1_ref[0:PAIR, :]
    win[pair_of(REACH + way), :] = twin1_ref[...]
    win[pair_of(REACH + 2 * way), :] = at2_ref[PAIR : 2 * PAIR, :]
    win[pair_of(REACH - 2 * way), :] = other2_ref[0:PAIR, :]

    def scores(subs):
        def body(at, top):
            first_key = (base + SPAN - REACH + at) * ROWS
            return score_block(subs, at, first_key, limit_ref, win, q_st, s_ref, top)

        return body

    none = jnp.full((1, CHUNK), NEG, jnp.float32)
    top = every_near(range_ref, scores, (none,) * (SUBS * CHUNKS))
    for c in range(SUBS * CHUNKS):
        top_ref[0:1, chunk_cols(c)] = top[c]


def middle_kernel(
    place_ref, range_ref, limit_ref, q_st, near_win, near_s, top_ref, at3_ref, at4_ref, twin3_ref, twin4_ref, do_ref,
    attn_ref, do_st, qs_st, dos_st, near_p, stats_ref, dq_acc, ahead_ref, across_ref,
    win, out_win, s_scr, p_scr, ds_scr, acc,
):
    core = place_ref[1]
    base = place_ref[0] - SPAN

    def slot(n):
        return n + core * (FAR - 1 - 2 * n)

    for n, part in enumerate((twin4_ref[...], at3_ref[0:PAIR, :], twin3_ref[...], at4_ref[PAIR : 2 * PAIR, :])):
        win[pair_of(slot(n)), :] = part
    for sub in range(SUBS):
        for h in range(GROUPS):
            do_st[staged(sub, h), :] = do_ref[sub_rows(sub), head_cols(h)]

    def scores(subs):
        def body(at, top):
            first_key = (base + jnp.where(at < SIDE, at, at + NEAR)) * ROWS
            return score_block(subs, at, first_key, limit_ref, win, q_st, s_scr, top)

        return body

    top = tuple(top_ref[0:1, chunk_cols(c)] for c in range(SUBS * CHUNKS))
    top = every_far(range_ref, scores, top)
    acc[...] = jnp.zeros_like(acc)

    def weigh(subs):
        return lambda at, total: weigh_block(subs, at, near_win, near_s, near_p, acc, top, total)

    def weigh_far(subs):
        return lambda at, total: weigh_block(subs, at, win, s_scr, p_scr, acc, top, total)

    total = every_near(range_ref, weigh, (jnp.zeros((1, CHUNK), jnp.float32),) * (SUBS * CHUNKS))
    total = every_far(range_ref, weigh_far, total)
    for c in range(SUBS * CHUNKS):
        stats_ref[0:1, chunk_cols(c)] = 1.0 / total[c]
    for sub in range(SUBS):
        for h in range(GROUPS):
            cols = staged(sub, h)
            inv = stats_ref[0:1, cols]
            attn_t = (acc[:, cols] * inv).astype(jnp.bfloat16).astype(jnp.float32)
            attn_ref[sub_rows(sub), head_cols(h)] = attn_t.T.astype(jnp.bfloat16)
            grad = do_st[cols, :].astype(jnp.float32)
            stats_ref[1:2, cols] = jnp.sum(attn_t * grad.T, axis=0, keepdims=True)
            inv_col = jnp.broadcast_to(inv, (DH, SUB)).T
            dos_st[cols, :] = (grad * inv_col).astype(jnp.bfloat16)
            qs_st[cols, :] = (q_st[cols, :].astype(jnp.float32) * (inv_col * SCALE)).astype(jnp.bfloat16)
    dq_acc[...] = jnp.zeros_like(dq_acc)
    out_win[...] = jnp.zeros_like(out_win)

    def back(subs):
        def body(at, carry):
            back_block(subs, at, win, p_scr, do_st, qs_st, dos_st, stats_ref, ds_scr, dq_acc, out_win)
            return carry

        return body

    every_far(range_ref, back, 0)
    for n in range(SIDE):
        ahead_ref[n * PAIR : (n + 1) * PAIR, :] = out_win[pair_of(slot(FAR - 1 - n)), :]
        across_ref[n * PAIR : (n + 1) * PAIR, :] = out_win[pair_of(slot(n)), :]


def near_back_kernel(
    place_ref, range_ref, win, p_ref, do_st, qs_st, dos_st, stats_ref, dq_far,
    dq_ref, ahead_ref, across_ref, mid_ref,
    out_win, ds_scr, dq_acc,
):
    way = 1 - 2 * place_ref[1]
    dq_acc[...] = dq_far[...]
    out_win[...] = jnp.zeros_like(out_win)

    def back(subs):
        def body(at, carry):
            back_block(subs, at, win, p_ref, do_st, qs_st, dos_st, stats_ref, ds_scr, dq_acc, out_win)
            return carry

        return body

    every_near(range_ref, back, 0)
    mid_ref[...] = out_win[pair_of(REACH), :]
    for n in range(REACH):
        k = REACH - n
        ahead_ref[n * PAIR : (n + 1) * PAIR, :] = out_win[pair_of(REACH + k * way), :]
        across_ref[n * PAIR : (n + 1) * PAIR, :] = out_win[pair_of(REACH - k * way), :]
    for sub in range(SUBS):
        for h in range(GROUPS):
            cols = staged(sub, h)
            dq = dq_acc[:, cols] * (stats_ref[0:1, cols] * SCALE)
            dq_ref[sub_rows(sub), head_cols(h)] = dq.T.astype(jnp.bfloat16)


def bf16(*shape):
    return jax.ShapeDtypeStruct(shape, jnp.bfloat16)


def f32(*shape):
    return jax.ShapeDtypeStruct(shape, jnp.float32)


def i32(*shape):
    return jax.ShapeDtypeStruct(shape, jnp.int32)


def near_scores(*args):
    return pl.pallas_call(
        near_scores_kernel,
        out_shape=(
            i32(4), i32(8, CHUNK), bf16(STACK, DH), bf16(NEAR * PAIR, DH), f32(NEAR * ROWS, STACK), f32(8, STACK),
        ),
        in_specs=[SMEM] + [VMEM] * 8,
        out_specs=(SMEM,) + (VMEM,) * 5,
        compiler_params=pltpu.CompilerParams(vmem_limit_bytes=16 * 1024 * 1024),
        cost_estimate=pl.CostEstimate(flops=10**9, bytes_accessed=6 * 10**6, transcendentals=0),
    )(*args)


def middle(*args):
    return pl.pallas_call(
        middle_kernel,
        out_shape=(
            bf16(ROWS, GROUPS * DH), bf16(STACK, DH), bf16(STACK, DH), bf16(STACK, DH), bf16(NEAR * ROWS, STACK),
            f32(8, STACK), f32(DH, STACK), bf16(SIDE * PAIR, DH), bf16(SIDE * PAIR, DH),
        ),
        in_specs=[SMEM, SMEM] + [VMEM] * 10,
        out_specs=(VMEM,) * 9,
        scratch_shapes=[
            pltpu.VMEM((FAR * PAIR, DH), jnp.bfloat16),
            pltpu.VMEM((FAR * PAIR, DH), jnp.bfloat16),
            pltpu.VMEM((FAR * ROWS, STACK), jnp.float32),
            pltpu.VMEM((FAR * ROWS, STACK), jnp.bfloat16),
            pltpu.VMEM((ROWS, STACK), jnp.bfloat16),
            pltpu.VMEM((DH, STACK), jnp.float32),
        ],
        compiler_params=pltpu.CompilerParams(vmem_limit_bytes=26 * 1024 * 1024),
        cost_estimate=pl.CostEstimate(flops=10**9, bytes_accessed=6 * 10**6, transcendentals=10**6),
    )(*args)


def near_back(*args):
    return pl.pallas_call(
        near_back_kernel,
        out_shape=(bf16(ROWS, GROUPS * DH), bf16(REACH * PAIR, DH), bf16(REACH * PAIR, DH), bf16(PAIR, DH)),
        in_specs=[SMEM, SMEM] + [VMEM] * 7,
        out_specs=(VMEM,) * 4,
        scratch_shapes=[
            pltpu.VMEM((NEAR * PAIR, DH), jnp.bfloat16),
            pltpu.VMEM((ROWS, STACK), jnp.bfloat16),
            pltpu.VMEM((DH, STACK), jnp.float32),
        ],
        compiler_params=pltpu.CompilerParams(vmem_limit_bytes=16 * 1024 * 1024),
        cost_estimate=pl.CostEstimate(flops=2 * 10**10, bytes_accessed=3 * 10**7, transcendentals=0),
    )(*args)


def small_call(body, out_rows, *args):
    shapes = [jax.ShapeDtypeStruct((rows, DH), jnp.bfloat16) for rows in out_rows]
    return pl.pallas_call(
        body,
        out_shape=shapes,
        in_specs=[VMEM] * len(args),
        out_specs=[VMEM] * len(shapes),
        compiler_params=SMALL,
        cost_estimate=pl.CostEstimate(flops=10**5, bytes_accessed=10**5, transcendentals=0),
    )(*args)


def stacked(*parts):
    def body(*refs):
        at = 0
        for ref in refs[:-1]:
            refs[-1][at : at + ref.shape[0], :] = ref[...]
            at += ref.shape[0]

    return small_call(body, [sum(part.shape[0] for part in parts)], *parts)[0]


def far_and_near(ahead, across, came):
    def body(ahead_ref, across_ref, came_ref, far_ref, near_ref):
        for n, ref in enumerate((ahead_ref, across_ref)):
            at = slice(n * PAIR, (n + 1) * PAIR)
            far_ref[at, :] = (ref[0:PAIR, :].astype(jnp.float32) + came_ref[at, :].astype(jnp.float32)).astype(jnp.bfloat16)
            near_ref[at, :] = ref[PAIR : 2 * PAIR, :]

    return small_call(body, [2 * PAIR] * 2, ahead, across, came)


def packed(*parts):
    n = len(parts)
    rows = parts[0].shape[0]

    def body(*refs):
        copies = [
            pltpu.make_async_copy(refs[k], refs[n].at[k * rows : (k + 1) * rows, :], refs[n + 1].at[k]) for k in range(n)
        ]
        for copy in copies:
            copy.start()
        for copy in copies:
            copy.wait()

    return pl.pallas_call(
        body,
        out_shape=bf16(n * rows, DH),
        in_specs=[ANY] * n,
        out_specs=VMEM,
        scratch_shapes=[pltpu.SemaphoreType.DMA((n,))],
        compiler_params=pltpu.CompilerParams(vmem_limit_bytes=BIG),
        cost_estimate=pl.CostEstimate(flops=0, bytes_accessed=10**6, transcendentals=0),
    )(*parts)


def both_heads(ahead, across):
    def body(ahead_ref, across_ref, *out_refs):
        for n, out_ref in enumerate(out_refs):
            out_ref[0:PAIR, :] = ahead_ref[n * PAIR : (n + 1) * PAIR, :]
            out_ref[PAIR : 2 * PAIR, :] = across_ref[n * PAIR : (n + 1) * PAIR, :]

    return small_call(body, [2 * PAIR] * 2, ahead, across)


def summed(*parts):
    def body(*refs):
        total = refs[0][...].astype(jnp.float32)
        for ref in refs[1:-1]:
            total += ref[...].astype(jnp.float32)
        refs[-1][...] = total.astype(jnp.bfloat16)

    return small_call(body, [parts[0].shape[0]], *parts)[0]


def last_sum(mid, near, far, near_twin, far_twin):
    def body(mid_ref, near_ref, far_ref, near_twin_ref, far_twin_ref, key_ref, val_ref):
        for at, out_ref in ((0, key_ref), (ROWS, val_ref)):
            rows = slice(at, at + ROWS)
            total = mid_ref[rows, :].astype(jnp.float32) + near_ref[rows, :].astype(jnp.float32)
            total += far_ref[PAIR + at : PAIR + at + ROWS, :].astype(jnp.float32)
            total += near_twin_ref[rows, :].astype(jnp.float32) + far_twin_ref[rows, :].astype(jnp.float32)
            out_ref[...] = total.astype(jnp.bfloat16)

    return small_call(body, [ROWS, ROWS], mid, near, far, near_twin, far_twin)


def half_of(core, size):
    return pl.ds(pl.multiple_of(core * size, size), size)


def project_back(core, own, other, w):
    rows, depth = own.shape
    cols = w.shape[1]

    def body(core_ref, own_ref, other_ref, w_ref, out_ref):
        core = core_ref[0]
        part = dot_nn(own_ref[...], w_ref[half_of(core, depth), :])
        out_ref[...] = (part + dot_nn(other_ref[...], w_ref[half_of(1 - core, depth), :])).astype(jnp.bfloat16)

    return pl.pallas_call(
        body,
        out_shape=bf16(rows, cols),
        in_specs=[SMEM, VMEM, VMEM, VMEM],
        out_specs=VMEM,
        compiler_params=pltpu.CompilerParams(vmem_limit_bytes=12 * 1024 * 1024),
        cost_estimate=pl.CostEstimate(flops=4 * rows * depth * cols, bytes_accessed=6 * 10**6, transcendentals=0),
    )(core, own, other, w)


def project(half, attn, w, other=None):
    rows, depth = attn.shape
    cols = w.shape[0] // 2
    more = () if other is None else (other,)

    def body(half_ref, a_ref, w_ref, *refs):
        out = dot_nt(a_ref[...], w_ref[half_of(half_ref[0], cols), :])
        if more:
            out += refs[0][...].astype(jnp.float32)
        refs[-1][...] = out.astype(jnp.bfloat16)

    return pl.pallas_call(
        body,
        out_shape=bf16(rows, cols),
        in_specs=[SMEM, VMEM, VMEM] + [VMEM] * len(more),
        out_specs=VMEM,
        compiler_params=pltpu.CompilerParams(vmem_limit_bytes=12 * 1024 * 1024),
        cost_estimate=pl.CostEstimate(flops=2 * rows * depth * cols, bytes_accessed=4 * 10**6, transcendentals=0),
    )(half, attn, w, *more)


def on_device(queries, keys, values, out_weight, doc_lengths, doc_full, out_grad):
    devices = lax.axis_size("cp")
    index = lax.axis_index("cp").astype(jnp.int32)
    core = lax.axis_index("hd").astype(jnp.int32)
    place = jnp.stack([index, core])
    core = core.reshape(1)

    def onward(block):
        ways = [(2 * i, 2 * (i + 1) if i + 1 < devices else 2 * i + 1) for i in range(devices)]
        ways += [(2 * i + 1, 2 * (i - 1) + 1 if i >= 1 else 2 * i) for i in range(devices)]
        return lax.ppermute(block, ("cp", "hd"), ways)

    def traded(block):
        pairs = [(2 * i, 2 * (i + 2) + 1) for i in range(devices - 2)]
        pairs += [(1, 3), (2 * devices - 4, 2 * devices - 2)]
        return lax.ppermute(block, ("cp", "hd"), pairs + [(b, a) for a, b in pairs])

    def twin(block):
        return lax.ppermute(block, "hd", [(0, 1), (1, 0)])

    own = packed(keys, values)
    other_keys, other_values, late_grad, own = lax.optimization_barrier((twin(keys), twin(values), out_grad, own))
    block = stacked(own, other_keys, other_values)
    other_grad = twin(late_grad)
    at2 = traded(block)
    at1 = onward(block)
    attn_grad = project_back(core, out_grad, other_grad, out_weight)
    at2, attn_grad = lax.optimization_barrier((at2, attn_grad))
    other2 = twin(at2)
    at4 = traded(other2)
    at3 = onward(other2)
    ranges, limit, q_st, win, s, top = near_scores(
        place, doc_lengths.reshape(1, -1), doc_full.reshape(1, -1), queries,
        own, at1, twin(at1[PAIR:]), at2, other2,
    )
    at4, top = lax.optimization_barrier((at4, top))
    at3, twin4 = lax.optimization_barrier((at3, twin(at4[:PAIR])))
    attn, do_st, qs_st, dos_st, p, stats, dq_far, ahead, across = middle(
        place, ranges, limit, q_st, win, s, top, at3, at4, twin(at3[PAIR:]), twin4, attn_grad
    )
    away = project(1 - core, attn, out_weight)
    across, away = lax.optimization_barrier((twin(across), away))
    out4, out3 = both_heads(ahead, across)
    out4, out3, stats = lax.optimization_barrier((out4, out3, stats))
    in4 = traded(out4)
    in3 = onward(out3)
    query_grad, ahead, across, mid = near_back(place, ranges, win, p, do_st, qs_st, dos_st, stats, dq_far)
    came = summed(in3, twin(in4))
    came, across = lax.optimization_barrier((came, twin(across)))
    far_out, near_out = far_and_near(ahead, across, came)
    far_out, away = lax.optimization_barrier((far_out, away))
    far = traded(far_out)
    near = onward(near_out)
    layer_out = project(core, attn, out_weight, twin(away))
    near, layer_out = lax.optimization_barrier((near, layer_out))
    far, near_twin = lax.optimization_barrier((far, twin(near[PAIR:])))
    key_grad, value_grad = last_sum(mid, near, far, near_twin, twin(far[:PAIR]))
    return (layer_out, query_grad, key_grad, value_grad)


def solution(mesh):
    placed = (P("cp", "hd"), P("cp", "hd"), P("cp", "hd"), P(None, "hd"), P(), P(), P("cp", "hd"))
    return jax.shard_map(
        on_device,
        mesh=mesh,
        in_specs=placed,
        out_specs=(P("cp", "hd"), P("cp", "hd"), P("cp", "hd"), P("cp", "hd")),
        check_vma=False,
    )
```

```python
import math

import jax
import jax.numpy as jnp
from jax import lax
from jax.experimental import pallas as pl
from jax.experimental.pallas import tpu as pltpu
from jax.sharding import PartitionSpec as P

HQ = 8
HK = 2
DH = 128
SPAN = 4
ROWS = 256
GROUPS = HQ // HK
WIDE = 2 * SPAN + 1
PAIR = 2 * ROWS
REACH = 2
NEAR = 2 * REACH + 1
FAR = WIDE - NEAR
SIDE = FAR // 2
SUB = 128
SUBS = ROWS // SUB
TILE = GROUPS * SUB
CHUNK = 256
CHUNKS = TILE // CHUNK
STACK = SUBS * TILE
NEG = -1e30
BIG = 60 * 1024 * 1024
SCALE = 1.0 / math.sqrt(DH)
SCALE2 = SCALE / math.log(2.0)
VMEM = pl.BlockSpec(memory_space=pltpu.VMEM)
ANY = pl.BlockSpec(memory_space=pl.ANY)
SMALL = pltpu.CompilerParams(vmem_limit_bytes=4 * 1024 * 1024)
SMEM = pl.BlockSpec(memory_space=pltpu.SMEM)


def dot_nn(a, b):
    return lax.dot_general(a, b, (((1,), (0,)), ((), ())), preferred_element_type=jnp.float32)


def dot_nt(a, b):
    return lax.dot_general(a, b, (((1,), (1,)), ((), ())), preferred_element_type=jnp.float32)


def limits(index, lengths_row, full_row):
    n = lengths_row.shape[1]
    row = lax.broadcasted_iota(jnp.int32, (n, n), 0)
    col = lax.broadcasted_iota(jnp.int32, (n, n), 1)
    ends = jnp.sum(jnp.where(col <= row, lengths_row, 0), axis=1, keepdims=True)
    starts = jnp.sum(jnp.where(col < row, lengths_row, 0), axis=1, keepdims=True)
    full = jnp.sum(jnp.where(col == row, full_row, 0), axis=1, keepdims=True)
    pos = index * ROWS + lax.broadcasted_iota(jnp.int32, (n, ROWS), 1)
    inside = (pos >= starts) & (pos < ends)
    low = jnp.sum(jnp.where(inside, starts, 0), axis=0, keepdims=True)
    high = jnp.sum(jnp.where(inside, jnp.where(full == 1, ends, pos + 1), 0), axis=0, keepdims=True)
    return low, high


def rows_of(r):
    return pl.ds(pl.multiple_of(r * ROWS, ROWS), ROWS)


def keys_of(r):
    return pl.ds(pl.multiple_of(r * 2 * ROWS, ROWS), ROWS)


def vals_of(r):
    return pl.ds(pl.multiple_of(r * 2 * ROWS + ROWS, ROWS), ROWS)


def pair_of(r):
    return pl.ds(pl.multiple_of(r * PAIR, ROWS), PAIR)


def staged(sub, h):
    return slice(sub * TILE + h * SUB, sub * TILE + (h + 1) * SUB)


def sub_rows(sub):
    return slice(sub * SUB, (sub + 1) * SUB)


def head_cols(h):
    return slice(h * DH, (h + 1) * DH)


def chunks_of(subs):
    return range(subs[0] * CHUNKS, (subs[-1] + 1) * CHUNKS)


def chunk_cols(c):
    return slice(c * CHUNK, (c + 1) * CHUNK)


def segments_of(range_ref):
    low0, high0, low1, high1 = [range_ref[n] for n in range(4)]
    return (
        ((0,), low0, jnp.minimum(low1, high0)),
        ((0, 1), low1, high0),
        ((1,), jnp.maximum(low1, high0), high1),
    )


def every_near(range_ref, make, state):
    skip = SPAN - REACH
    for subs, lower, upper in segments_of(range_ref):
        state = lax.fori_loop(jnp.maximum(lower - skip, 0), jnp.minimum(upper - skip, NEAR), make(subs), state)
    return state


def every_far(range_ref, make, state):
    end = SPAN + REACH + 1
    for subs, lower, upper in segments_of(range_ref):
        first = jnp.where(lower < SIDE, lower, jnp.maximum(lower, end) - NEAR)
        last = jnp.where(upper > end, upper - NEAR, jnp.minimum(upper, SIDE))
        state = lax.fori_loop(first, last, make(subs), state)
    return state


def score_block(subs, at, first_key, limit_ref, win, q_st, s_ref, top):
    keys = win[keys_of(at), :]
    key_pos = first_key + lax.broadcasted_iota(jnp.int32, (ROWS, CHUNK), 0)
    valid = {
        sub: (key_pos >= limit_ref[2 * sub : 2 * sub + 1, :]) & (key_pos < limit_ref[2 * sub + 1 : 2 * sub + 2, :])
        for sub in subs
    }
    out = list(top)
    for c in chunks_of(subs):
        s = dot_nt(keys, q_st[chunk_cols(c), :]) * SCALE2
        s = jnp.where(valid[c // CHUNKS], s, NEG)
        s_ref[rows_of(at), chunk_cols(c)] = s
        out[c] = jnp.maximum(top[c], jnp.max(s, axis=0, keepdims=True))
    return tuple(out)


def weigh_block(subs, at, win, s_ref, p_ref, acc, top, total):
    vals_t = win[vals_of(at), :].T
    out = list(total)
    for c in chunks_of(subs):
        cols = chunk_cols(c)
        p = jnp.exp2(s_ref[rows_of(at), cols] - top[c])
        out[c] = total[c] + jnp.sum(p, axis=0, keepdims=True)
        p = p.astype(jnp.bfloat16)
        p_ref[rows_of(at), cols] = p
        acc[:, cols] += dot_nn(vals_t, p)
    return tuple(out)


def back_block(subs, at, win, p_ref, do_st, qs_st, dos_st, stats_ref, ds_scr, dq_acc, out_win):
    keys_t = win[keys_of(at), :].T
    vals = win[vals_of(at), :]
    for c in chunks_of(subs):
        cols = chunk_cols(c)
        dp = dot_nt(vals, do_st[cols, :])
        ds = (p_ref[rows_of(at), cols].astype(jnp.float32) * (dp - stats_ref[1:2, cols])).astype(jnp.bfloat16)
        ds_scr[:, cols] = ds
        dq_acc[:, cols] += dot_nn(keys_t, ds)
    cols = slice(subs[0] * TILE, (subs[-1] + 1) * TILE)
    out_win[keys_of(at), :] = dot_nn(ds_scr[:, cols], qs_st[cols, :]).astype(jnp.bfloat16)
    out_win[vals_of(at), :] = dot_nn(p_ref[rows_of(at), cols], dos_st[cols, :]).astype(jnp.bfloat16)


def near_scores_kernel(
    place_ref, len_ref, full_ref, q_ref, own_ref, at1_ref, at2_ref, twin1_ref, twin2_ref,
    range_ref, limit_ref, q_st, win, s_ref, top_ref,
):
    way = 1 - 2 * place_ref[1]
    base = place_ref[0] - SPAN
    low, high = limits(place_ref[0], len_ref[...], full_ref[...])
    for sub in range(SUBS):
        cut = sub_rows(sub)
        limit_ref[2 * sub : 2 * sub + 1, :] = jnp.concatenate([low[:, cut]] * (CHUNK // SUB), axis=1)
        limit_ref[2 * sub + 1 : 2 * sub + 2, :] = jnp.concatenate([high[:, cut]] * (CHUNK // SUB), axis=1)
        range_ref[2 * sub] = jnp.maximum(jnp.min(low[:, cut]) // ROWS - base, 0)
        range_ref[2 * sub + 1] = jnp.minimum((jnp.max(high[:, cut]) + ROWS - 1) // ROWS - base, WIDE)
        for h in range(GROUPS):
            q_st[staged(sub, h), :] = q_ref[cut, head_cols(h)]
    win[pair_of(REACH), :] = own_ref[0:PAIR, :]
    for k, ring, twin in ((1, at1_ref, twin1_ref), (2, at2_ref, twin2_ref)):
        win[pair_of(REACH - k * way), :] = ring[0:PAIR, :]
        win[pair_of(REACH + k * way), :] = twin[...]

    def scores(subs):
        def body(at, top):
            first_key = (base + SPAN - REACH + at) * ROWS
            return score_block(subs, at, first_key, limit_ref, win, q_st, s_ref, top)

        return body

    none = jnp.full((1, CHUNK), NEG, jnp.float32)
    top = every_near(range_ref, scores, (none,) * (SUBS * CHUNKS))
    for c in range(SUBS * CHUNKS):
        top_ref[0:1, chunk_cols(c)] = top[c]


def middle_kernel(
    place_ref, range_ref, limit_ref, q_st, near_win, near_s, top_ref, at3_ref, at4_ref, twin3_ref, twin4_ref, do_ref,
    attn_ref, do_st, qs_st, dos_st, near_p, stats_ref, dq_acc, ahead_ref, across_ref,
    win, out_win, s_scr, p_scr, ds_scr, acc,
):
    core = place_ref[1]
    base = place_ref[0] - SPAN

    def slot(n):
        return n + core * (FAR - 1 - 2 * n)

    for n, ref in enumerate((at4_ref, at3_ref, twin3_ref, twin4_ref)):
        win[pair_of(slot(n)), :] = ref[0:PAIR, :]
    for sub in range(SUBS):
        for h in range(GROUPS):
            do_st[staged(sub, h), :] = do_ref[sub_rows(sub), head_cols(h)]

    def scores(subs):
        def body(at, top):
            first_key = (base + jnp.where(at < SIDE, at, at + NEAR)) * ROWS
            return score_block(subs, at, first_key, limit_ref, win, q_st, s_scr, top)

        return body

    top = tuple(top_ref[0:1, chunk_cols(c)] for c in range(SUBS * CHUNKS))
    top = every_far(range_ref, scores, top)
    acc[...] = jnp.zeros_like(acc)

    def weigh(subs):
        return lambda at, total: weigh_block(subs, at, near_win, near_s, near_p, acc, top, total)

    def weigh_far(subs):
        return lambda at, total: weigh_block(subs, at, win, s_scr, p_scr, acc, top, total)

    total = every_near(range_ref, weigh, (jnp.zeros((1, CHUNK), jnp.float32),) * (SUBS * CHUNKS))
    total = every_far(range_ref, weigh_far, total)
    for c in range(SUBS * CHUNKS):
        stats_ref[0:1, chunk_cols(c)] = 1.0 / total[c]
    for sub in range(SUBS):
        for h in range(GROUPS):
            cols = staged(sub, h)
            inv = stats_ref[0:1, cols]
            attn_t = (acc[:, cols] * inv).astype(jnp.bfloat16).astype(jnp.float32)
            attn_ref[sub_rows(sub), head_cols(h)] = attn_t.T.astype(jnp.bfloat16)
            grad = do_st[cols, :].astype(jnp.float32)
            stats_ref[1:2, cols] = jnp.sum(attn_t * grad.T, axis=0, keepdims=True)
            inv_col = jnp.broadcast_to(inv, (DH, SUB)).T
            dos_st[cols, :] = (grad * inv_col).astype(jnp.bfloat16)
            qs_st[cols, :] = (q_st[cols, :].astype(jnp.float32) * (inv_col * SCALE)).astype(jnp.bfloat16)
    dq_acc[...] = jnp.zeros_like(dq_acc)
    out_win[...] = jnp.zeros_like(out_win)

    def back(subs):
        def body(at, carry):
            back_block(subs, at, win, p_scr, do_st, qs_st, dos_st, stats_ref, ds_scr, dq_acc, out_win)
            return carry

        return body

    every_far(range_ref, back, 0)
    for n in range(SIDE):
        ahead_ref[n * PAIR : (n + 1) * PAIR, :] = out_win[pair_of(slot(FAR - 1 - n)), :]
        across_ref[n * PAIR : (n + 1) * PAIR, :] = out_win[pair_of(slot(n)), :]


def near_back_kernel(
    place_ref, range_ref, win, p_ref, do_st, qs_st, dos_st, stats_ref, dq_far,
    dq_ref, ahead_ref, across_ref, mid_ref,
    out_win, ds_scr, dq_acc,
):
    way = 1 - 2 * place_ref[1]
    dq_acc[...] = dq_far[...]
    out_win[...] = jnp.zeros_like(out_win)

    def back(subs):
        def body(at, carry):
            back_block(subs, at, win, p_ref, do_st, qs_st, dos_st, stats_ref, ds_scr, dq_acc, out_win)
            return carry

        return body

    every_near(range_ref, back, 0)
    mid_ref[...] = out_win[pair_of(REACH), :]
    for n in range(REACH):
        k = REACH - n
        ahead_ref[n * PAIR : (n + 1) * PAIR, :] = out_win[pair_of(REACH + k * way), :]
        across_ref[n * PAIR : (n + 1) * PAIR, :] = out_win[pair_of(REACH - k * way), :]
    for sub in range(SUBS):
        for h in range(GROUPS):
            cols = staged(sub, h)
            dq = dq_acc[:, cols] * (stats_ref[0:1, cols] * SCALE)
            dq_ref[sub_rows(sub), head_cols(h)] = dq.T.astype(jnp.bfloat16)


def bf16(*shape):
    return jax.ShapeDtypeStruct(shape, jnp.bfloat16)


def f32(*shape):
    return jax.ShapeDtypeStruct(shape, jnp.float32)


def i32(*shape):
    return jax.ShapeDtypeStruct(shape, jnp.int32)


def near_scores(*args):
    return pl.pallas_call(
        near_scores_kernel,
        out_shape=(
            i32(4), i32(8, CHUNK), bf16(STACK, DH), bf16(NEAR * PAIR, DH), f32(NEAR * ROWS, STACK), f32(8, STACK),
        ),
        in_specs=[SMEM] + [VMEM] * 8,
        out_specs=(SMEM,) + (VMEM,) * 5,
        compiler_params=pltpu.CompilerParams(vmem_limit_bytes=16 * 1024 * 1024),
        cost_estimate=pl.CostEstimate(flops=10**9, bytes_accessed=6 * 10**6, transcendentals=0),
    )(*args)


def middle(*args):
    return pl.pallas_call(
        middle_kernel,
        out_shape=(
            bf16(ROWS, GROUPS * DH), bf16(STACK, DH), bf16(STACK, DH), bf16(STACK, DH), bf16(NEAR * ROWS, STACK),
            f32(8, STACK), f32(DH, STACK), bf16(SIDE * PAIR, DH), bf16(SIDE * PAIR, DH),
        ),
        in_specs=[SMEM, SMEM] + [VMEM] * 10,
        out_specs=(VMEM,) * 9,
        scratch_shapes=[
            pltpu.VMEM((FAR * PAIR, DH), jnp.bfloat16),
            pltpu.VMEM((FAR * PAIR, DH), jnp.bfloat16),
            pltpu.VMEM((FAR * ROWS, STACK), jnp.float32),
            pltpu.VMEM((FAR * ROWS, STACK), jnp.bfloat16),
            pltpu.VMEM((ROWS, STACK), jnp.bfloat16),
            pltpu.VMEM((DH, STACK), jnp.float32),
        ],
        compiler_params=pltpu.CompilerParams(vmem_limit_bytes=26 * 1024 * 1024),
        cost_estimate=pl.CostEstimate(flops=10**9, bytes_accessed=6 * 10**6, transcendentals=10**6),
    )(*args)


def near_back(*args):
    return pl.pallas_call(
        near_back_kernel,
        out_shape=(bf16(ROWS, GROUPS * DH), bf16(REACH * PAIR, DH), bf16(REACH * PAIR, DH), bf16(PAIR, DH)),
        in_specs=[SMEM, SMEM] + [VMEM] * 7,
        out_specs=(VMEM,) * 4,
        scratch_shapes=[
            pltpu.VMEM((NEAR * PAIR, DH), jnp.bfloat16),
            pltpu.VMEM((ROWS, STACK), jnp.bfloat16),
            pltpu.VMEM((DH, STACK), jnp.float32),
        ],
        compiler_params=pltpu.CompilerParams(vmem_limit_bytes=16 * 1024 * 1024),
        cost_estimate=pl.CostEstimate(flops=2 * 10**10, bytes_accessed=3 * 10**7, transcendentals=0),
    )(*args)


def small_call(body, out_rows, *args):
    shapes = [jax.ShapeDtypeStruct((rows, DH), jnp.bfloat16) for rows in out_rows]
    return pl.pallas_call(
        body,
        out_shape=shapes,
        in_specs=[VMEM] * len(args),
        out_specs=[VMEM] * len(shapes),
        compiler_params=SMALL,
        cost_estimate=pl.CostEstimate(flops=10**5, bytes_accessed=10**5, transcendentals=0),
    )(*args)


def stacked(*parts):
    def body(*refs):
        at = 0
        for ref in refs[:-1]:
            refs[-1][at : at + ref.shape[0], :] = ref[...]
            at += ref.shape[0]

    return small_call(body, [sum(part.shape[0] for part in parts)], *parts)[0]


def far_and_near(ahead, across, came):
    def body(ahead_ref, across_ref, came_ref, far_ref, near_ref):
        for n, ref in enumerate((ahead_ref, across_ref)):
            at = slice(n * PAIR, (n + 1) * PAIR)
            far_ref[at, :] = (ref[0:PAIR, :].astype(jnp.float32) + came_ref[at, :].astype(jnp.float32)).astype(jnp.bfloat16)
            near_ref[at, :] = ref[PAIR : 2 * PAIR, :]

    return small_call(body, [2 * PAIR] * 2, ahead, across, came)


def packed(*parts):
    n = len(parts)
    rows = parts[0].shape[0]

    def body(*refs):
        copies = [
            pltpu.make_async_copy(refs[k], refs[n].at[k * rows : (k + 1) * rows, :], refs[n + 1].at[k]) for k in range(n)
        ]
        for copy in copies:
            copy.start()
        for copy in copies:
            copy.wait()

    return pl.pallas_call(
        body,
        out_shape=bf16(n * rows, DH),
        in_specs=[ANY] * n,
        out_specs=VMEM,
        scratch_shapes=[pltpu.SemaphoreType.DMA((n,))],
        compiler_params=pltpu.CompilerParams(vmem_limit_bytes=48 * 1024 * 1024),
        cost_estimate=pl.CostEstimate(flops=0, bytes_accessed=10**6, transcendentals=0),
    )(*parts)


def both_heads(ahead, across):
    def body(ahead_ref, across_ref, *out_refs):
        for n, out_ref in enumerate(out_refs):
            out_ref[0:PAIR, :] = ahead_ref[n * PAIR : (n + 1) * PAIR, :]
            out_ref[PAIR : 2 * PAIR, :] = across_ref[n * PAIR : (n + 1) * PAIR, :]

    return small_call(body, [2 * PAIR] * 2, ahead, across)


def summed(*parts):
    def body(*refs):
        total = refs[0][...].astype(jnp.float32)
        for ref in refs[1:-1]:
            total += ref[...].astype(jnp.float32)
        refs[-1][...] = total.astype(jnp.bfloat16)

    return small_call(body, [parts[0].shape[0]], *parts)[0]


def last_sum(*parts):
    def body(*refs):
        for at, out_ref in ((0, refs[-2]), (ROWS, refs[-1])):
            total = refs[0][at : at + ROWS, :].astype(jnp.float32)
            for ref in refs[1:-2]:
                total += ref[at : at + ROWS, :].astype(jnp.float32)
            out_ref[...] = total.astype(jnp.bfloat16)

    return small_call(body, [ROWS, ROWS], *parts)


def half_of(core, size):
    return pl.ds(pl.multiple_of(core * size, size), size)


def project_back(core, own, other, w):
    rows, depth = own.shape
    cols = w.shape[1]

    def body(core_ref, own_ref, other_ref, w_ref, out_ref):
        core = core_ref[0]
        part = dot_nn(own_ref[...], w_ref[half_of(core, depth), :])
        out_ref[...] = (part + dot_nn(other_ref[...], w_ref[half_of(1 - core, depth), :])).astype(jnp.bfloat16)

    return pl.pallas_call(
        body,
        out_shape=bf16(rows, cols),
        in_specs=[SMEM, VMEM, VMEM, VMEM],
        out_specs=VMEM,
        compiler_params=pltpu.CompilerParams(vmem_limit_bytes=12 * 1024 * 1024),
        cost_estimate=pl.CostEstimate(flops=4 * rows * depth * cols, bytes_accessed=6 * 10**6, transcendentals=0),
    )(core, own, other, w)


def project(half, attn, w, other=None):
    rows, depth = attn.shape
    cols = w.shape[0] // 2
    more = () if other is None else (other,)

    def body(half_ref, a_ref, w_ref, *refs):
        out = dot_nt(a_ref[...], w_ref[half_of(half_ref[0], cols), :])
        if more:
            out += refs[0][...].astype(jnp.float32)
        refs[-1][...] = out.astype(jnp.bfloat16)

    return pl.pallas_call(
        body,
        out_shape=bf16(rows, cols),
        in_specs=[SMEM, VMEM, VMEM] + [VMEM] * len(more),
        out_specs=VMEM,
        compiler_params=pltpu.CompilerParams(vmem_limit_bytes=12 * 1024 * 1024),
        cost_estimate=pl.CostEstimate(flops=2 * rows * depth * cols, bytes_accessed=4 * 10**6, transcendentals=0),
    )(half, attn, w, *more)


def on_device(queries, keys, values, out_weight, doc_lengths, doc_full, out_grad):
    devices = lax.axis_size("cp")
    index = lax.axis_index("cp").astype(jnp.int32)
    core = lax.axis_index("hd").astype(jnp.int32)
    place = jnp.stack([index, core])
    core = core.reshape(1)

    def step(block, far):
        ways = [(2 * i, 2 * (i + far) if i + far < devices else 2 * i + 1) for i in range(devices)]
        ways += [(2 * i + 1, 2 * (i - far) + 1 if i >= far else 2 * i) for i in range(devices)]
        return lax.ppermute(block, ("cp", "hd"), ways)

    def twin(block):
        return lax.ppermute(block, "hd", [(0, 1), (1, 0)])

    own = packed(keys, values)
    other_keys, other_values, own = lax.optimization_barrier((twin(keys), twin(values), own))
    block = stacked(own, other_keys, other_values)
    block, late_grad = lax.optimization_barrier((block, out_grad))
    other_grad = twin(late_grad)
    at2 = step(block, 2)
    at1 = step(block, 1)
    attn_grad = project_back(core, out_grad, other_grad, out_weight)
    at2, attn_grad = lax.optimization_barrier((at2, attn_grad))
    at4 = step(at2, 2)
    at3 = step(at2, 1)
    ranges, limit, q_st, win, s, top = near_scores(
        place, doc_lengths.reshape(1, -1), doc_full.reshape(1, -1), queries,
        own, at1, at2, twin(at1[PAIR:]), twin(at2[PAIR:]),
    )
    at4, at3, top = lax.optimization_barrier((at4, at3, top))
    twin3, twin4 = twin(at3[PAIR:]), twin(at4[PAIR:])
    attn, do_st, qs_st, dos_st, p, stats, dq_far, ahead, across = middle(
        place, ranges, limit, q_st, win, s, top, at3, at4, twin3, twin4, attn_grad
    )
    away = project(1 - core, attn, out_weight)
    across, away = lax.optimization_barrier((twin(across), away))
    out4, out3 = both_heads(ahead, across)
    out4, out3, stats = lax.optimization_barrier((out4, out3, stats))
    in4 = step(out4, 2)
    in3 = step(out3, 1)
    query_grad, ahead, across, mid = near_back(place, ranges, win, p, do_st, qs_st, dos_st, stats, dq_far)
    came = summed(in4, in3)
    came, across = lax.optimization_barrier((came, twin(across)))
    far_out, near_out = far_and_near(ahead, across, came)
    far_out, away = lax.optimization_barrier((far_out, away))
    far = step(far_out, 2)
    near = step(near_out, 1)
    layer_out = project(core, attn, out_weight, twin(away))
    far, near, layer_out = lax.optimization_barrier((far, near, layer_out))
    key_grad, value_grad = last_sum(mid, near, far, twin(near[PAIR:]), twin(far[PAIR:]))
    return (layer_out, query_grad, key_grad, value_grad)


def solution(mesh):
    placed = (P("cp", "hd"), P("cp", "hd"), P("cp", "hd"), P(None, "hd"), P(), P(), P("cp", "hd"))
    return jax.shard_map(
        on_device,
        mesh=mesh,
        in_specs=placed,
        out_specs=(P("cp", "hd"), P("cp", "hd"), P("cp", "hd"), P("cp", "hd")),
        check_vma=False,
    )
```

```python
import math

import jax
import jax.numpy as jnp
from jax import lax
from jax.experimental import pallas as pl
from jax.experimental.pallas import tpu as pltpu
from jax.sharding import PartitionSpec as P

HQ = 8
HK = 2
DH = 128
SPAN = 4
ROWS = 256
GROUPS = HQ // HK
WIDE = 2 * SPAN + 1
PAIR = 2 * ROWS
REACH = 2
NEAR = 2 * REACH + 1
FAR = WIDE - NEAR
SIDE = FAR // 2
SUB = 128
SUBS = ROWS // SUB
TILE = GROUPS * SUB
CHUNK = 256
CHUNKS = TILE // CHUNK
STACK = SUBS * TILE
NEG = -1e30
BIG = 60 * 1024 * 1024
SCALE = 1.0 / math.sqrt(DH)
SCALE2 = SCALE / math.log(2.0)
VMEM = pl.BlockSpec(memory_space=pltpu.VMEM)
ANY = pl.BlockSpec(memory_space=pl.ANY)
SMALL = pltpu.CompilerParams(vmem_limit_bytes=4 * 1024 * 1024)
SMEM = pl.BlockSpec(memory_space=pltpu.SMEM)


def dot_nn(a, b):
    return lax.dot_general(a, b, (((1,), (0,)), ((), ())), preferred_element_type=jnp.float32)


def dot_nt(a, b):
    return lax.dot_general(a, b, (((1,), (1,)), ((), ())), preferred_element_type=jnp.float32)


def limits(index, lengths_row, full_row):
    n = lengths_row.shape[1]
    row = lax.broadcasted_iota(jnp.int32, (n, n), 0)
    col = lax.broadcasted_iota(jnp.int32, (n, n), 1)
    ends = jnp.sum(jnp.where(col <= row, lengths_row, 0), axis=1, keepdims=True)
    starts = jnp.sum(jnp.where(col < row, lengths_row, 0), axis=1, keepdims=True)
    full = jnp.sum(jnp.where(col == row, full_row, 0), axis=1, keepdims=True)
    pos = index * ROWS + lax.broadcasted_iota(jnp.int32, (n, ROWS), 1)
    inside = (pos >= starts) & (pos < ends)
    low = jnp.sum(jnp.where(inside, starts, 0), axis=0, keepdims=True)
    high = jnp.sum(jnp.where(inside, jnp.where(full == 1, ends, pos + 1), 0), axis=0, keepdims=True)
    return low, high


def rows_of(r):
    return pl.ds(pl.multiple_of(r * ROWS, ROWS), ROWS)


def keys_of(r):
    return pl.ds(pl.multiple_of(r * 2 * ROWS, ROWS), ROWS)


def vals_of(r):
    return pl.ds(pl.multiple_of(r * 2 * ROWS + ROWS, ROWS), ROWS)


def pair_of(r):
    return pl.ds(pl.multiple_of(r * PAIR, ROWS), PAIR)


def staged(sub, h):
    return slice(sub * TILE + h * SUB, sub * TILE + (h + 1) * SUB)


def sub_rows(sub):
    return slice(sub * SUB, (sub + 1) * SUB)


def head_cols(h):
    return slice(h * DH, (h + 1) * DH)


def chunks_of(subs):
    return range(subs[0] * CHUNKS, (subs[-1] + 1) * CHUNKS)


def chunk_cols(c):
    return slice(c * CHUNK, (c + 1) * CHUNK)


def segments_of(range_ref):
    low0, high0, low1, high1 = [range_ref[n] for n in range(4)]
    return (
        ((0,), low0, jnp.minimum(low1, high0)),
        ((0, 1), low1, high0),
        ((1,), jnp.maximum(low1, high0), high1),
    )


def every_near(range_ref, make, state):
    skip = SPAN - REACH
    for subs, lower, upper in segments_of(range_ref):
        state = lax.fori_loop(jnp.maximum(lower - skip, 0), jnp.minimum(upper - skip, NEAR), make(subs), state)
    return state


def every_far(range_ref, make, state):
    end = SPAN + REACH + 1
    for subs, lower, upper in segments_of(range_ref):
        first = jnp.where(lower < SIDE, lower, jnp.maximum(lower, end) - NEAR)
        last = jnp.where(upper > end, upper - NEAR, jnp.minimum(upper, SIDE))
        state = lax.fori_loop(first, last, make(subs), state)
    return state


def score_block(subs, at, first_key, limit_ref, win, q_st, s_ref, top):
    keys = win[keys_of(at), :]
    key_pos = first_key + lax.broadcasted_iota(jnp.int32, (ROWS, CHUNK), 0)
    valid = {
        sub: (key_pos >= limit_ref[2 * sub : 2 * sub + 1, :]) & (key_pos < limit_ref[2 * sub + 1 : 2 * sub + 2, :])
        for sub in subs
    }
    out = list(top)
    for c in chunks_of(subs):
        s = dot_nt(keys, q_st[chunk_cols(c), :]) * SCALE2
        s = jnp.where(valid[c // CHUNKS], s, NEG)
        s_ref[rows_of(at), chunk_cols(c)] = s
        out[c] = jnp.maximum(top[c], jnp.max(s, axis=0, keepdims=True))
    return tuple(out)


def weigh_block(subs, at, win, s_ref, p_ref, acc, top, total):
    vals_t = win[vals_of(at), :].T
    out = list(total)
    for c in chunks_of(subs):
        cols = chunk_cols(c)
        p = jnp.exp2(s_ref[rows_of(at), cols] - top[c])
        out[c] = total[c] + jnp.sum(p, axis=0, keepdims=True)
        p = p.astype(jnp.bfloat16)
        p_ref[rows_of(at), cols] = p
        acc[:, cols] += dot_nn(vals_t, p)
    return tuple(out)


def back_block(subs, at, win, p_ref, do_st, qs_st, dos_st, stats_ref, ds_scr, dq_acc, out_win):
    keys_t = win[keys_of(at), :].T
    vals = win[vals_of(at), :]
    for c in chunks_of(subs):
        cols = chunk_cols(c)
        dp = dot_nt(vals, do_st[cols, :])
        ds = (p_ref[rows_of(at), cols].astype(jnp.float32) * (dp - stats_ref[1:2, cols])).astype(jnp.bfloat16)
        ds_scr[:, cols] = ds
        dq_acc[:, cols] += dot_nn(keys_t, ds)
    cols = slice(subs[0] * TILE, (subs[-1] + 1) * TILE)
    out_win[keys_of(at), :] = dot_nn(ds_scr[:, cols], qs_st[cols, :]).astype(jnp.bfloat16)
    out_win[vals_of(at), :] = dot_nn(p_ref[rows_of(at), cols], dos_st[cols, :]).astype(jnp.bfloat16)


def near_scores_kernel(
    place_ref, len_ref, full_ref, q_ref, own_ref, at1_ref, at2_ref, twin1_ref, twin2_ref,
    range_ref, limit_ref, q_st, win, s_ref, top_ref,
):
    way = 1 - 2 * place_ref[1]
    base = place_ref[0] - SPAN
    low, high = limits(place_ref[0], len_ref[...], full_ref[...])
    for sub in range(SUBS):
        cut = sub_rows(sub)
        limit_ref[2 * sub : 2 * sub + 1, :] = jnp.concatenate([low[:, cut]] * (CHUNK // SUB), axis=1)
        limit_ref[2 * sub + 1 : 2 * sub + 2, :] = jnp.concatenate([high[:, cut]] * (CHUNK // SUB), axis=1)
        range_ref[2 * sub] = jnp.maximum(jnp.min(low[:, cut]) // ROWS - base, 0)
        range_ref[2 * sub + 1] = jnp.minimum((jnp.max(high[:, cut]) + ROWS - 1) // ROWS - base, WIDE)
        for h in range(GROUPS):
            q_st[staged(sub, h), :] = q_ref[cut, head_cols(h)]
    win[pair_of(REACH), :] = own_ref[0:PAIR, :]
    for k, ring, twin in ((1, at1_ref, twin1_ref), (2, at2_ref, twin2_ref)):
        win[pair_of(REACH - k * way), :] = ring[0:PAIR, :]
        win[pair_of(REACH + k * way), :] = twin[...]

    def scores(subs):
        def body(at, top):
            first_key = (base + SPAN - REACH + at) * ROWS
            return score_block(subs, at, first_key, limit_ref, win, q_st, s_ref, top)

        return body

    none = jnp.full((1, CHUNK), NEG, jnp.float32)
    top = every_near(range_ref, scores, (none,) * (SUBS * CHUNKS))
    for c in range(SUBS * CHUNKS):
        top_ref[0:1, chunk_cols(c)] = top[c]


def middle_kernel(
    place_ref, range_ref, limit_ref, q_st, near_win, near_s, top_ref, at3_ref, at4_ref, twin3_ref, twin4_ref, do_ref,
    attn_ref, do_st, qs_st, dos_st, near_p, stats_ref, dq_acc, ahead_ref, across_ref,
    win, out_win, s_scr, p_scr, ds_scr, acc,
):
    core = place_ref[1]
    base = place_ref[0] - SPAN

    def slot(n):
        return n + core * (FAR - 1 - 2 * n)

    for n, ref in enumerate((at4_ref, at3_ref, twin3_ref, twin4_ref)):
        win[pair_of(slot(n)), :] = ref[0:PAIR, :]
    for sub in range(SUBS):
        for h in range(GROUPS):
            do_st[staged(sub, h), :] = do_ref[sub_rows(sub), head_cols(h)]

    def scores(subs):
        def body(at, top):
            first_key = (base + jnp.where(at < SIDE, at, at + NEAR)) * ROWS
            return score_block(subs, at, first_key, limit_ref, win, q_st, s_scr, top)

        return body

    top = tuple(top_ref[0:1, chunk_cols(c)] for c in range(SUBS * CHUNKS))
    top = every_far(range_ref, scores, top)
    acc[...] = jnp.zeros_like(acc)

    def weigh(subs):
        return lambda at, total: weigh_block(subs, at, near_win, near_s, near_p, acc, top, total)

    def weigh_far(subs):
        return lambda at, total: weigh_block(subs, at, win, s_scr, p_scr, acc, top, total)

    total = every_near(range_ref, weigh, (jnp.zeros((1, CHUNK), jnp.float32),) * (SUBS * CHUNKS))
    total = every_far(range_ref, weigh_far, total)
    for c in range(SUBS * CHUNKS):
        stats_ref[0:1, chunk_cols(c)] = 1.0 / total[c]
    for sub in range(SUBS):
        for h in range(GROUPS):
            cols = staged(sub, h)
            inv = stats_ref[0:1, cols]
            attn_t = (acc[:, cols] * inv).astype(jnp.bfloat16).astype(jnp.float32)
            attn_ref[sub_rows(sub), head_cols(h)] = attn_t.T.astype(jnp.bfloat16)
            grad = do_st[cols, :].astype(jnp.float32)
            stats_ref[1:2, cols] = jnp.sum(attn_t * grad.T, axis=0, keepdims=True)
            inv_col = jnp.broadcast_to(inv, (DH, SUB)).T
            dos_st[cols, :] = (grad * inv_col).astype(jnp.bfloat16)
            qs_st[cols, :] = (q_st[cols, :].astype(jnp.float32) * (inv_col * SCALE)).astype(jnp.bfloat16)
    dq_acc[...] = jnp.zeros_like(dq_acc)
    out_win[...] = jnp.zeros_like(out_win)

    def back(subs):
        def body(at, carry):
            back_block(subs, at, win, p_scr, do_st, qs_st, dos_st, stats_ref, ds_scr, dq_acc, out_win)
            return carry

        return body

    every_far(range_ref, back, 0)
    for n in range(SIDE):
        ahead_ref[n * PAIR : (n + 1) * PAIR, :] = out_win[pair_of(slot(FAR - 1 - n)), :]
        across_ref[n * PAIR : (n + 1) * PAIR, :] = out_win[pair_of(slot(n)), :]


def near_back_kernel(
    place_ref, range_ref, win, p_ref, do_st, qs_st, dos_st, stats_ref, dq_far,
    dq_ref, ahead_ref, across_ref, mid_ref,
    out_win, ds_scr, dq_acc,
):
    way = 1 - 2 * place_ref[1]
    dq_acc[...] = dq_far[...]
    out_win[...] = jnp.zeros_like(out_win)

    def back(subs):
        def body(at, carry):
            back_block(subs, at, win, p_ref, do_st, qs_st, dos_st, stats_ref, ds_scr, dq_acc, out_win)
            return carry

        return body

    every_near(range_ref, back, 0)
    mid_ref[...] = out_win[pair_of(REACH), :]
    for n in range(REACH):
        k = REACH - n
        ahead_ref[n * PAIR : (n + 1) * PAIR, :] = out_win[pair_of(REACH + k * way), :]
        across_ref[n * PAIR : (n + 1) * PAIR, :] = out_win[pair_of(REACH - k * way), :]
    for sub in range(SUBS):
        for h in range(GROUPS):
            cols = staged(sub, h)
            dq = dq_acc[:, cols] * (stats_ref[0:1, cols] * SCALE)
            dq_ref[sub_rows(sub), head_cols(h)] = dq.T.astype(jnp.bfloat16)


def bf16(*shape):
    return jax.ShapeDtypeStruct(shape, jnp.bfloat16)


def f32(*shape):
    return jax.ShapeDtypeStruct(shape, jnp.float32)


def i32(*shape):
    return jax.ShapeDtypeStruct(shape, jnp.int32)


def near_scores(*args):
    return pl.pallas_call(
        near_scores_kernel,
        out_shape=(
            i32(4), i32(8, CHUNK), bf16(STACK, DH), bf16(NEAR * PAIR, DH), f32(NEAR * ROWS, STACK), f32(8, STACK),
        ),
        in_specs=[SMEM] + [VMEM] * 8,
        out_specs=(SMEM,) + (VMEM,) * 5,
        compiler_params=pltpu.CompilerParams(vmem_limit_bytes=16 * 1024 * 1024),
        cost_estimate=pl.CostEstimate(flops=10**9, bytes_accessed=6 * 10**6, transcendentals=0),
    )(*args)


def middle(*args):
    return pl.pallas_call(
        middle_kernel,
        out_shape=(
            bf16(ROWS, GROUPS * DH), bf16(STACK, DH), bf16(STACK, DH), bf16(STACK, DH), bf16(NEAR * ROWS, STACK),
            f32(8, STACK), f32(DH, STACK), bf16(SIDE * PAIR, DH), bf16(SIDE * PAIR, DH),
        ),
        in_specs=[SMEM, SMEM] + [VMEM] * 10,
        out_specs=(VMEM,) * 9,
        scratch_shapes=[
            pltpu.VMEM((FAR * PAIR, DH), jnp.bfloat16),
            pltpu.VMEM((FAR * PAIR, DH), jnp.bfloat16),
            pltpu.VMEM((FAR * ROWS, STACK), jnp.float32),
            pltpu.VMEM((FAR * ROWS, STACK), jnp.bfloat16),
            pltpu.VMEM((ROWS, STACK), jnp.bfloat16),
            pltpu.VMEM((DH, STACK), jnp.float32),
        ],
        compiler_params=pltpu.CompilerParams(vmem_limit_bytes=26 * 1024 * 1024),
        cost_estimate=pl.CostEstimate(flops=10**9, bytes_accessed=6 * 10**6, transcendentals=10**6),
    )(*args)


def near_back(*args):
    return pl.pallas_call(
        near_back_kernel,
        out_shape=(bf16(ROWS, GROUPS * DH), bf16(REACH * PAIR, DH), bf16(REACH * PAIR, DH), bf16(PAIR, DH)),
        in_specs=[SMEM, SMEM] + [VMEM] * 7,
        out_specs=(VMEM,) * 4,
        scratch_shapes=[
            pltpu.VMEM((NEAR * PAIR, DH), jnp.bfloat16),
            pltpu.VMEM((ROWS, STACK), jnp.bfloat16),
            pltpu.VMEM((DH, STACK), jnp.float32),
        ],
        compiler_params=pltpu.CompilerParams(vmem_limit_bytes=16 * 1024 * 1024),
        cost_estimate=pl.CostEstimate(flops=2 * 10**10, bytes_accessed=3 * 10**7, transcendentals=0),
    )(*args)


def small_call(body, out_rows, *args):
    shapes = [jax.ShapeDtypeStruct((rows, DH), jnp.bfloat16) for rows in out_rows]
    return pl.pallas_call(
        body,
        out_shape=shapes,
        in_specs=[VMEM] * len(args),
        out_specs=[VMEM] * len(shapes),
        compiler_params=SMALL,
        cost_estimate=pl.CostEstimate(flops=10**5, bytes_accessed=10**5, transcendentals=0),
    )(*args)


def stacked(*parts):
    def body(*refs):
        at = 0
        for ref in refs[:-1]:
            refs[-1][at : at + ref.shape[0], :] = ref[...]
            at += ref.shape[0]

    return small_call(body, [sum(part.shape[0] for part in parts)], *parts)[0]


def far_and_near(ahead, across, came):
    def body(ahead_ref, across_ref, came_ref, far_ref, near_ref):
        for n, ref in enumerate((ahead_ref, across_ref)):
            at = slice(n * PAIR, (n + 1) * PAIR)
            far_ref[at, :] = (ref[0:PAIR, :].astype(jnp.float32) + came_ref[at, :].astype(jnp.float32)).astype(jnp.bfloat16)
            near_ref[at, :] = ref[PAIR : 2 * PAIR, :]

    return small_call(body, [2 * PAIR] * 2, ahead, across, came)


def stacked_after(hello, *parts):
    def body(hello_ref, *refs):
        at = 0
        for ref in refs[:-1]:
            refs[-1][at : at + ref.shape[0], :] = ref[...]
            at += ref.shape[0]

    return small_call(body, [sum(part.shape[0] for part in parts)], hello, *parts)[0]


def packed(*parts):
    n = len(parts)
    rows = parts[0].shape[0]

    def body(*refs):
        copies = [
            pltpu.make_async_copy(refs[k], refs[n].at[k * rows : (k + 1) * rows, :], refs[n + 1].at[k]) for k in range(n)
        ]
        for copy in copies:
            copy.start()
        for copy in copies:
            copy.wait()

    return pl.pallas_call(
        body,
        out_shape=bf16(n * rows, DH),
        in_specs=[ANY] * n,
        out_specs=VMEM,
        scratch_shapes=[pltpu.SemaphoreType.DMA((n,))],
        compiler_params=pltpu.CompilerParams(vmem_limit_bytes=48 * 1024 * 1024),
        cost_estimate=pl.CostEstimate(flops=0, bytes_accessed=10**6, transcendentals=0),
    )(*parts)


def both_heads(ahead, across):
    def body(ahead_ref, across_ref, *out_refs):
        for n, out_ref in enumerate(out_refs):
            out_ref[0:PAIR, :] = ahead_ref[n * PAIR : (n + 1) * PAIR, :]
            out_ref[PAIR : 2 * PAIR, :] = across_ref[n * PAIR : (n + 1) * PAIR, :]

    return small_call(body, [2 * PAIR] * 2, ahead, across)


def summed(*parts):
    def body(*refs):
        total = refs[0][...].astype(jnp.float32)
        for ref in refs[1:-1]:
            total += ref[...].astype(jnp.float32)
        refs[-1][...] = total.astype(jnp.bfloat16)

    return small_call(body, [parts[0].shape[0]], *parts)[0]


def last_sum(*parts):
    def body(*refs):
        for at, out_ref in ((0, refs[-2]), (ROWS, refs[-1])):
            total = refs[0][at : at + ROWS, :].astype(jnp.float32)
            for ref in refs[1:-2]:
                total += ref[at : at + ROWS, :].astype(jnp.float32)
            out_ref[...] = total.astype(jnp.bfloat16)

    return small_call(body, [ROWS, ROWS], *parts)


def half_of(core, size):
    return pl.ds(pl.multiple_of(core * size, size), size)


def project_back(core, own, other, w):
    rows, depth = own.shape
    cols = w.shape[1]

    def body(core_ref, own_ref, other_ref, w_ref, out_ref):
        core = core_ref[0]
        part = dot_nn(own_ref[...], w_ref[half_of(core, depth), :])
        out_ref[...] = (part + dot_nn(other_ref[...], w_ref[half_of(1 - core, depth), :])).astype(jnp.bfloat16)

    return pl.pallas_call(
        body,
        out_shape=bf16(rows, cols),
        in_specs=[SMEM, VMEM, VMEM, VMEM],
        out_specs=VMEM,
        compiler_params=pltpu.CompilerParams(vmem_limit_bytes=12 * 1024 * 1024),
        cost_estimate=pl.CostEstimate(flops=4 * rows * depth * cols, bytes_accessed=6 * 10**6, transcendentals=0),
    )(core, own, other, w)


def project(half, attn, w, other=None):
    rows, depth = attn.shape
    cols = w.shape[0] // 2
    more = () if other is None else (other,)

    def body(half_ref, a_ref, w_ref, *refs):
        out = dot_nt(a_ref[...], w_ref[half_of(half_ref[0], cols), :])
        if more:
            out += refs[0][...].astype(jnp.float32)
        refs[-1][...] = out.astype(jnp.bfloat16)

    return pl.pallas_call(
        body,
        out_shape=bf16(rows, cols),
        in_specs=[SMEM, VMEM, VMEM] + [VMEM] * len(more),
        out_specs=VMEM,
        compiler_params=pltpu.CompilerParams(vmem_limit_bytes=12 * 1024 * 1024),
        cost_estimate=pl.CostEstimate(flops=2 * rows * depth * cols, bytes_accessed=4 * 10**6, transcendentals=0),
    )(half, attn, w, *more)


def on_device(queries, keys, values, out_weight, doc_lengths, doc_full, out_grad):
    devices = lax.axis_size("cp")
    index = lax.axis_index("cp").astype(jnp.int32)
    core = lax.axis_index("hd").astype(jnp.int32)
    place = jnp.stack([index, core])
    core = core.reshape(1)

    def step(block, far):
        ways = [(2 * i, 2 * (i + far) if i + far < devices else 2 * i + 1) for i in range(devices)]
        ways += [(2 * i + 1, 2 * (i - far) + 1 if i >= far else 2 * i) for i in range(devices)]
        return lax.ppermute(block, ("cp", "hd"), ways)

    def twin(block):
        return lax.ppermute(block, "hd", [(0, 1), (1, 0)])

    own = packed(keys, values)
    other_keys, other_values, own = lax.optimization_barrier((twin(keys), twin(values), own))
    hello = step(jnp.broadcast_to(index.astype(jnp.bfloat16), (16, DH)), 1)
    block = stacked_after(hello, own, other_keys, other_values)
    block, late_grad = lax.optimization_barrier((block, out_grad))
    other_grad = twin(late_grad)
    at2 = step(block, 2)
    at1 = step(block, 1)
    attn_grad = project_back(core, out_grad, other_grad, out_weight)
    at2, attn_grad = lax.optimization_barrier((at2, attn_grad))
    at4 = step(at2, 2)
    at3 = step(at2, 1)
    ranges, limit, q_st, win, s, top = near_scores(
        place, doc_lengths.reshape(1, -1), doc_full.reshape(1, -1), queries,
        own, at1, at2, twin(at1[PAIR:]), twin(at2[PAIR:]),
    )
    at4, at3, top = lax.optimization_barrier((at4, at3, top))
    twin3, twin4 = twin(at3[PAIR:]), twin(at4[PAIR:])
    attn, do_st, qs_st, dos_st, p, stats, dq_far, ahead, across = middle(
        place, ranges, limit, q_st, win, s, top, at3, at4, twin3, twin4, attn_grad
    )
    away = project(1 - core, attn, out_weight)
    across, away = lax.optimization_barrier((twin(across), away))
    out4, out3 = both_heads(ahead, across)
    out4, out3, stats = lax.optimization_barrier((out4, out3, stats))
    in4 = step(out4, 2)
    in3 = step(out3, 1)
    query_grad, ahead, across, mid = near_back(place, ranges, win, p, do_st, qs_st, dos_st, stats, dq_far)
    came = summed(in4, in3)
    came, across = lax.optimization_barrier((came, twin(across)))
    far_out, near_out = far_and_near(ahead, across, came)
    far_out, away = lax.optimization_barrier((far_out, away))
    far = step(far_out, 2)
    near = step(near_out, 1)
    layer_out = project(core, attn, out_weight, twin(away))
    far, near, layer_out = lax.optimization_barrier((far, near, layer_out))
    key_grad, value_grad = last_sum(mid, near, far, twin(near[PAIR:]), twin(far[PAIR:]))
    return (layer_out, query_grad, key_grad, value_grad)


def solution(mesh):
    placed = (P("cp", "hd"), P("cp", "hd"), P("cp", "hd"), P(None, "hd"), P(), P(), P("cp", "hd"))
    return jax.shard_map(
        on_device,
        mesh=mesh,
        in_specs=placed,
        out_specs=(P("cp", "hd"), P("cp", "hd"), P("cp", "hd"), P("cp", "hd")),
        check_vma=False,
    )
```

```python
import math

import jax
import jax.numpy as jnp
from jax import lax
from jax.experimental import pallas as pl
from jax.experimental.pallas import tpu as pltpu
from jax.sharding import PartitionSpec as P

HQ = 8
HK = 2
DH = 128
SPAN = 4
ROWS = 256
GROUPS = HQ // HK
WIDE = 2 * SPAN + 1
PAIR = 2 * ROWS
REACH = 2
NEAR = 2 * REACH + 1
FAR = WIDE - NEAR
SIDE = FAR // 2
SUB = 128
SUBS = ROWS // SUB
TILE = GROUPS * SUB
CHUNK = 256
CHUNKS = TILE // CHUNK
STACK = SUBS * TILE
NEG = -1e30
BIG = 60 * 1024 * 1024
SCALE = 1.0 / math.sqrt(DH)
SCALE2 = SCALE / math.log(2.0)
VMEM = pl.BlockSpec(memory_space=pltpu.VMEM)
ANY = pl.BlockSpec(memory_space=pl.ANY)
SMALL = pltpu.CompilerParams(vmem_limit_bytes=4 * 1024 * 1024)
SMEM = pl.BlockSpec(memory_space=pltpu.SMEM)


def dot_nn(a, b):
    return lax.dot_general(a, b, (((1,), (0,)), ((), ())), preferred_element_type=jnp.float32)


def dot_nt(a, b):
    return lax.dot_general(a, b, (((1,), (1,)), ((), ())), preferred_element_type=jnp.float32)


def limits(index, lengths_row, full_row):
    n = lengths_row.shape[1]
    row = lax.broadcasted_iota(jnp.int32, (n, n), 0)
    col = lax.broadcasted_iota(jnp.int32, (n, n), 1)
    ends = jnp.sum(jnp.where(col <= row, lengths_row, 0), axis=1, keepdims=True)
    starts = jnp.sum(jnp.where(col < row, lengths_row, 0), axis=1, keepdims=True)
    full = jnp.sum(jnp.where(col == row, full_row, 0), axis=1, keepdims=True)
    pos = index * ROWS + lax.broadcasted_iota(jnp.int32, (n, ROWS), 1)
    inside = (pos >= starts) & (pos < ends)
    low = jnp.sum(jnp.where(inside, starts, 0), axis=0, keepdims=True)
    high = jnp.sum(jnp.where(inside, jnp.where(full == 1, ends, pos + 1), 0), axis=0, keepdims=True)
    return low, high


def rows_of(r):
    return pl.ds(pl.multiple_of(r * ROWS, ROWS), ROWS)


def keys_of(r):
    return pl.ds(pl.multiple_of(r * 2 * ROWS, ROWS), ROWS)


def vals_of(r):
    return pl.ds(pl.multiple_of(r * 2 * ROWS + ROWS, ROWS), ROWS)


def pair_of(r):
    return pl.ds(pl.multiple_of(r * PAIR, ROWS), PAIR)


def staged(sub, h):
    return slice(sub * TILE + h * SUB, sub * TILE + (h + 1) * SUB)


def sub_rows(sub):
    return slice(sub * SUB, (sub + 1) * SUB)


def head_cols(h):
    return slice(h * DH, (h + 1) * DH)


def chunks_of(subs):
    return range(subs[0] * CHUNKS, (subs[-1] + 1) * CHUNKS)


def chunk_cols(c):
    return slice(c * CHUNK, (c + 1) * CHUNK)


def segments_of(range_ref):
    low0, high0, low1, high1 = [range_ref[n] for n in range(4)]
    return (
        ((0,), low0, jnp.minimum(low1, high0)),
        ((0, 1), low1, high0),
        ((1,), jnp.maximum(low1, high0), high1),
    )


def every_near(range_ref, make, state):
    skip = SPAN - REACH
    for subs, lower, upper in segments_of(range_ref):
        state = lax.fori_loop(jnp.maximum(lower - skip, 0), jnp.minimum(upper - skip, NEAR), make(subs), state)
    return state


def every_far(range_ref, make, state):
    end = SPAN + REACH + 1
    for subs, lower, upper in segments_of(range_ref):
        first = jnp.where(lower < SIDE, lower, jnp.maximum(lower, end) - NEAR)
        last = jnp.where(upper > end, upper - NEAR, jnp.minimum(upper, SIDE))
        state = lax.fori_loop(first, last, make(subs), state)
    return state


def score_block(subs, at, first_key, limit_ref, win, q_st, s_ref, top):
    keys = win[keys_of(at), :]
    key_pos = first_key + lax.broadcasted_iota(jnp.int32, (ROWS, CHUNK), 0)
    valid = {
        sub: (key_pos >= limit_ref[2 * sub : 2 * sub + 1, :]) & (key_pos < limit_ref[2 * sub + 1 : 2 * sub + 2, :])
        for sub in subs
    }
    out = list(top)
    for c in chunks_of(subs):
        s = dot_nt(keys, q_st[chunk_cols(c), :]) * SCALE2
        s = jnp.where(valid[c // CHUNKS], s, NEG)
        s_ref[rows_of(at), chunk_cols(c)] = s
        out[c] = jnp.maximum(top[c], jnp.max(s, axis=0, keepdims=True))
    return tuple(out)


def weigh_block(subs, at, win, s_ref, p_ref, acc, top, total):
    vals_t = win[vals_of(at), :].T
    out = list(total)
    for c in chunks_of(subs):
        cols = chunk_cols(c)
        p = jnp.exp2(s_ref[rows_of(at), cols] - top[c])
        out[c] = total[c] + jnp.sum(p, axis=0, keepdims=True)
        p = p.astype(jnp.bfloat16)
        p_ref[rows_of(at), cols] = p
        acc[:, cols] += dot_nn(vals_t, p)
    return tuple(out)


def back_block(subs, at, win, p_ref, do_st, qs_st, dos_st, stats_ref, ds_scr, dq_acc, out_win):
    keys_t = win[keys_of(at), :].T
    vals = win[vals_of(at), :]
    for c in chunks_of(subs):
        cols = chunk_cols(c)
        dp = dot_nt(vals, do_st[cols, :])
        ds = (p_ref[rows_of(at), cols].astype(jnp.float32) * (dp - stats_ref[1:2, cols])).astype(jnp.bfloat16)
        ds_scr[:, cols] = ds
        dq_acc[:, cols] += dot_nn(keys_t, ds)
    cols = slice(subs[0] * TILE, (subs[-1] + 1) * TILE)
    out_win[keys_of(at), :] = dot_nn(ds_scr[:, cols], qs_st[cols, :]).astype(jnp.bfloat16)
    out_win[vals_of(at), :] = dot_nn(p_ref[rows_of(at), cols], dos_st[cols, :]).astype(jnp.bfloat16)


def scaled_copies(q_st, do_st, inv_row, qs_st, dos_st):
    for n in range(SUBS * GROUPS):
        cols = slice(n * SUB, (n + 1) * SUB)
        inv_col = jnp.broadcast_to(inv_row[:, cols], (DH, SUB)).T
        dos_st[cols, :] = (do_st[cols, :].astype(jnp.float32) * inv_col).astype(jnp.bfloat16)
        qs_st[cols, :] = (q_st[cols, :].astype(jnp.float32) * (inv_col * SCALE)).astype(jnp.bfloat16)


def near_scores_kernel(
    place_ref, len_ref, full_ref, q_ref, own_ref, at1_ref, at2_ref, twin1_ref, twin2_ref,
    range_ref, limit_ref, q_st, win, p_ref, acc, top_ref,
    s_ref,
):
    way = 1 - 2 * place_ref[1]
    base = place_ref[0] - SPAN
    low, high = limits(place_ref[0], len_ref[...], full_ref[...])
    for sub in range(SUBS):
        cut = sub_rows(sub)
        limit_ref[2 * sub : 2 * sub + 1, :] = jnp.concatenate([low[:, cut]] * (CHUNK // SUB), axis=1)
        limit_ref[2 * sub + 1 : 2 * sub + 2, :] = jnp.concatenate([high[:, cut]] * (CHUNK // SUB), axis=1)
        range_ref[2 * sub] = jnp.maximum(jnp.min(low[:, cut]) // ROWS - base, 0)
        range_ref[2 * sub + 1] = jnp.minimum((jnp.max(high[:, cut]) + ROWS - 1) // ROWS - base, WIDE)
        for h in range(GROUPS):
            q_st[staged(sub, h), :] = q_ref[cut, head_cols(h)]
    win[pair_of(REACH), :] = own_ref[0:PAIR, :]
    for k, ring, twin in ((1, at1_ref, twin1_ref), (2, at2_ref, twin2_ref)):
        win[pair_of(REACH - k * way), :] = ring[0:PAIR, :]
        win[pair_of(REACH + k * way), :] = twin[...]

    def scores(subs):
        def body(at, top):
            first_key = (base + SPAN - REACH + at) * ROWS
            return score_block(subs, at, first_key, limit_ref, win, q_st, s_ref, top)

        return body

    none = jnp.full((1, CHUNK), NEG, jnp.float32)
    top = every_near(range_ref, scores, (none,) * (SUBS * CHUNKS))
    acc[...] = jnp.zeros_like(acc)

    def weigh(subs):
        return lambda at, total: weigh_block(subs, at, win, s_ref, p_ref, acc, top, total)

    total = every_near(range_ref, weigh, (jnp.zeros((1, CHUNK), jnp.float32),) * (SUBS * CHUNKS))
    for c in range(SUBS * CHUNKS):
        top_ref[0:1, chunk_cols(c)] = top[c]
        top_ref[1:2, chunk_cols(c)] = total[c]


def middle_kernel(
    place_ref, range_ref, limit_ref, q_st, near_acc, top_ref, at3_ref, at4_ref, twin3_ref, twin4_ref, do_ref,
    attn_ref, do_st, stats_ref, dq_acc, ahead_ref, across_ref,
    win, out_win, s_scr, p_scr, ds_scr, acc, qs_st, dos_st,
):
    core = place_ref[1]
    base = place_ref[0] - SPAN

    def slot(n):
        return n + core * (FAR - 1 - 2 * n)

    for n, ref in enumerate((at4_ref, at3_ref, twin3_ref, twin4_ref)):
        win[pair_of(slot(n)), :] = ref[0:PAIR, :]

    def scores(subs):
        def body(at, top):
            first_key = (base + jnp.where(at < SIDE, at, at + NEAR)) * ROWS
            return score_block(subs, at, first_key, limit_ref, win, q_st, s_scr, top)

        return body

    near_top = tuple(top_ref[0:1, chunk_cols(c)] for c in range(SUBS * CHUNKS))
    top = every_far(range_ref, scores, near_top)
    share = [jnp.exp2(near_top[c] - top[c]) for c in range(SUBS * CHUNKS)]
    for c in range(SUBS * CHUNKS):
        acc[:, chunk_cols(c)] = near_acc[:, chunk_cols(c)] * share[c]

    def weigh(subs):
        return lambda at, total: weigh_block(subs, at, win, s_scr, p_scr, acc, top, total)

    total = tuple(top_ref[1:2, chunk_cols(c)] * share[c] for c in range(SUBS * CHUNKS))
    total = every_far(range_ref, weigh, total)
    for c in range(SUBS * CHUNKS):
        inv = 1.0 / total[c]
        stats_ref[0:1, chunk_cols(c)] = inv
        stats_ref[2:3, chunk_cols(c)] = inv * share[c]
    for sub in range(SUBS):
        for h in range(GROUPS):
            cols = staged(sub, h)
            attn_t = (acc[:, cols] * stats_ref[0:1, cols]).astype(jnp.bfloat16).astype(jnp.float32)
            attn_ref[sub_rows(sub), head_cols(h)] = attn_t.T.astype(jnp.bfloat16)
            grad = do_ref[sub_rows(sub), head_cols(h)]
            do_st[cols, :] = grad
            stats_ref[1:2, cols] = jnp.sum(attn_t * grad.astype(jnp.float32).T, axis=0, keepdims=True)
    dq_acc[...] = jnp.zeros_like(dq_acc)
    out_win[...] = jnp.zeros_like(out_win)

    @pl.when((range_ref[0] < SIDE) | (range_ref[3] > SIDE + NEAR))
    def _():
        scaled_copies(q_st, do_st, stats_ref[0:1, :], qs_st, dos_st)

    def back(subs):
        def body(at, carry):
            back_block(subs, at, win, p_scr, do_st, qs_st, dos_st, stats_ref, ds_scr, dq_acc, out_win)
            return carry

        return body

    every_far(range_ref, back, 0)
    for n in range(SIDE):
        ahead_ref[n * PAIR : (n + 1) * PAIR, :] = out_win[pair_of(slot(FAR - 1 - n)), :]
        across_ref[n * PAIR : (n + 1) * PAIR, :] = out_win[pair_of(slot(n)), :]


def near_back_kernel(
    place_ref, range_ref, win, p_ref, q_st, do_st, stats_ref, dq_far,
    dq_ref, ahead_ref, across_ref, mid_ref,
    out_win, ds_scr, dq_acc, qs_st, dos_st,
):
    way = 1 - 2 * place_ref[1]
    dq_acc[...] = jnp.zeros_like(dq_acc)
    scaled_copies(q_st, do_st, stats_ref[2:3, :], qs_st, dos_st)
    out_win[...] = jnp.zeros_like(out_win)

    def back(subs):
        def body(at, carry):
            back_block(subs, at, win, p_ref, do_st, qs_st, dos_st, stats_ref, ds_scr, dq_acc, out_win)
            return carry

        return body

    every_near(range_ref, back, 0)
    mid_ref[...] = out_win[pair_of(REACH), :]
    for n in range(REACH):
        k = REACH - n
        ahead_ref[n * PAIR : (n + 1) * PAIR, :] = out_win[pair_of(REACH + k * way), :]
        across_ref[n * PAIR : (n + 1) * PAIR, :] = out_win[pair_of(REACH - k * way), :]
    for sub in range(SUBS):
        for h in range(GROUPS):
            cols = staged(sub, h)
            dq = dq_acc[:, cols] * (stats_ref[2:3, cols] * SCALE) + dq_far[:, cols] * (stats_ref[0:1, cols] * SCALE)
            dq_ref[sub_rows(sub), head_cols(h)] = dq.T.astype(jnp.bfloat16)


def bf16(*shape):
    return jax.ShapeDtypeStruct(shape, jnp.bfloat16)


def f32(*shape):
    return jax.ShapeDtypeStruct(shape, jnp.float32)


def i32(*shape):
    return jax.ShapeDtypeStruct(shape, jnp.int32)


def near_scores(*args):
    return pl.pallas_call(
        near_scores_kernel,
        out_shape=(
            i32(4), i32(8, CHUNK), bf16(STACK, DH), bf16(NEAR * PAIR, DH), bf16(NEAR * ROWS, STACK), f32(DH, STACK),
            f32(8, STACK),
        ),
        in_specs=[SMEM] + [VMEM] * 8,
        out_specs=(SMEM,) + (VMEM,) * 6,
        scratch_shapes=[pltpu.VMEM((NEAR * ROWS, STACK), jnp.float32)],
        compiler_params=pltpu.CompilerParams(vmem_limit_bytes=18 * 1024 * 1024),
        cost_estimate=pl.CostEstimate(flops=10**9, bytes_accessed=6 * 10**6, transcendentals=0),
    )(*args)


def middle(*args):
    return pl.pallas_call(
        middle_kernel,
        out_shape=(
            bf16(ROWS, GROUPS * DH), bf16(STACK, DH), f32(8, STACK), f32(DH, STACK),
            bf16(SIDE * PAIR, DH), bf16(SIDE * PAIR, DH),
        ),
        in_specs=[SMEM, SMEM] + [VMEM] * 9,
        out_specs=(VMEM,) * 6,
        scratch_shapes=[
            pltpu.VMEM((FAR * PAIR, DH), jnp.bfloat16),
            pltpu.VMEM((FAR * PAIR, DH), jnp.bfloat16),
            pltpu.VMEM((FAR * ROWS, STACK), jnp.float32),
            pltpu.VMEM((FAR * ROWS, STACK), jnp.bfloat16),
            pltpu.VMEM((ROWS, STACK), jnp.bfloat16),
            pltpu.VMEM((DH, STACK), jnp.float32),
            pltpu.VMEM((STACK, DH), jnp.bfloat16),
            pltpu.VMEM((STACK, DH), jnp.bfloat16),
        ],
        compiler_params=pltpu.CompilerParams(vmem_limit_bytes=20 * 1024 * 1024),
        cost_estimate=pl.CostEstimate(flops=10**9, bytes_accessed=6 * 10**6, transcendentals=10**6),
    )(*args)


def near_back(*args):
    return pl.pallas_call(
        near_back_kernel,
        out_shape=(bf16(ROWS, GROUPS * DH), bf16(REACH * PAIR, DH), bf16(REACH * PAIR, DH), bf16(PAIR, DH)),
        in_specs=[SMEM, SMEM] + [VMEM] * 6,
        out_specs=(VMEM,) * 4,
        scratch_shapes=[
            pltpu.VMEM((NEAR * PAIR, DH), jnp.bfloat16),
            pltpu.VMEM((ROWS, STACK), jnp.bfloat16),
            pltpu.VMEM((DH, STACK), jnp.float32),
            pltpu.VMEM((STACK, DH), jnp.bfloat16),
            pltpu.VMEM((STACK, DH), jnp.bfloat16),
        ],
        compiler_params=pltpu.CompilerParams(vmem_limit_bytes=16 * 1024 * 1024),
        cost_estimate=pl.CostEstimate(flops=2 * 10**10, bytes_accessed=3 * 10**7, transcendentals=0),
    )(*args)


def small_call(body, out_rows, *args):
    shapes = [jax.ShapeDtypeStruct((rows, DH), jnp.bfloat16) for rows in out_rows]
    return pl.pallas_call(
        body,
        out_shape=shapes,
        in_specs=[VMEM] * len(args),
        out_specs=[VMEM] * len(shapes),
        compiler_params=SMALL,
        cost_estimate=pl.CostEstimate(flops=10**5, bytes_accessed=10**5, transcendentals=0),
    )(*args)


def stacked(*parts):
    def body(*refs):
        at = 0
        for ref in refs[:-1]:
            refs[-1][at : at + ref.shape[0], :] = ref[...]
            at += ref.shape[0]

    return small_call(body, [sum(part.shape[0] for part in parts)], *parts)[0]


def far_and_near(ahead, across, came):
    def body(ahead_ref, across_ref, came_ref, far_ref, near_ref):
        for n, ref in enumerate((ahead_ref, across_ref)):
            at = slice(n * PAIR, (n + 1) * PAIR)
            far_ref[at, :] = (ref[0:PAIR, :].astype(jnp.float32) + came_ref[at, :].astype(jnp.float32)).astype(jnp.bfloat16)
            near_ref[at, :] = ref[PAIR : 2 * PAIR, :]

    return small_call(body, [2 * PAIR] * 2, ahead, across, came)


def packed(*parts):
    n = len(parts)
    rows = parts[0].shape[0]

    def body(*refs):
        copies = [
            pltpu.make_async_copy(refs[k], refs[n].at[k * rows : (k + 1) * rows, :], refs[n + 1].at[k]) for k in range(n)
        ]
        for copy in copies:
            copy.start()
        for copy in copies:
            copy.wait()

    return pl.pallas_call(
        body,
        out_shape=bf16(n * rows, DH),
        in_specs=[ANY] * n,
        out_specs=VMEM,
        scratch_shapes=[pltpu.SemaphoreType.DMA((n,))],
        compiler_params=pltpu.CompilerParams(vmem_limit_bytes=48 * 1024 * 1024),
        cost_estimate=pl.CostEstimate(flops=0, bytes_accessed=10**6, transcendentals=0),
    )(*parts)


def both_heads(ahead, across):
    def body(ahead_ref, across_ref, *out_refs):
        for n, out_ref in enumerate(out_refs):
            out_ref[0:PAIR, :] = ahead_ref[n * PAIR : (n + 1) * PAIR, :]
            out_ref[PAIR : 2 * PAIR, :] = across_ref[n * PAIR : (n + 1) * PAIR, :]

    return small_call(body, [2 * PAIR] * 2, ahead, across)


def summed(*parts):
    def body(*refs):
        total = refs[0][...].astype(jnp.float32)
        for ref in refs[1:-1]:
            total += ref[...].astype(jnp.float32)
        refs[-1][...] = total.astype(jnp.bfloat16)

    return small_call(body, [parts[0].shape[0]], *parts)[0]


def last_sum(*parts):
    def body(*refs):
        for at, out_ref in ((0, refs[-2]), (ROWS, refs[-1])):
            total = refs[0][at : at + ROWS, :].astype(jnp.float32)
            for ref in refs[1:-2]:
                total += ref[at : at + ROWS, :].astype(jnp.float32)
            out_ref[...] = total.astype(jnp.bfloat16)

    return small_call(body, [ROWS, ROWS], *parts)


def half_of(core, size):
    return pl.ds(pl.multiple_of(core * size, size), size)


def project_back(core, own, other, w):
    rows, depth = own.shape
    cols = w.shape[1]

    def body(core_ref, own_ref, other_ref, w_ref, out_ref):
        core = core_ref[0]
        part = dot_nn(own_ref[...], w_ref[half_of(core, depth), :])
        out_ref[...] = (part + dot_nn(other_ref[...], w_ref[half_of(1 - core, depth), :])).astype(jnp.bfloat16)

    return pl.pallas_call(
        body,
        out_shape=bf16(rows, cols),
        in_specs=[SMEM, VMEM, VMEM, VMEM],
        out_specs=VMEM,
        compiler_params=pltpu.CompilerParams(vmem_limit_bytes=12 * 1024 * 1024),
        cost_estimate=pl.CostEstimate(flops=4 * rows * depth * cols, bytes_accessed=6 * 10**6, transcendentals=0),
    )(core, own, other, w)


def project(half, attn, w, other=None):
    rows, depth = attn.shape
    cols = w.shape[0] // 2
    more = () if other is None else (other,)

    def body(half_ref, a_ref, w_ref, *refs):
        out = dot_nt(a_ref[...], w_ref[half_of(half_ref[0], cols), :])
        if more:
            out += refs[0][...].astype(jnp.float32)
        refs[-1][...] = out.astype(jnp.bfloat16)

    return pl.pallas_call(
        body,
        out_shape=bf16(rows, cols),
        in_specs=[SMEM, VMEM, VMEM] + [VMEM] * len(more),
        out_specs=VMEM,
        compiler_params=pltpu.CompilerParams(vmem_limit_bytes=12 * 1024 * 1024),
        cost_estimate=pl.CostEstimate(flops=2 * rows * depth * cols, bytes_accessed=4 * 10**6, transcendentals=0),
    )(half, attn, w, *more)


def on_device(queries, keys, values, out_weight, doc_lengths, doc_full, out_grad):
    devices = lax.axis_size("cp")
    index = lax.axis_index("cp").astype(jnp.int32)
    core = lax.axis_index("hd").astype(jnp.int32)
    place = jnp.stack([index, core])
    core = core.reshape(1)

    def step(block, far):
        ways = [(2 * i, 2 * (i + far) if i + far < devices else 2 * i + 1) for i in range(devices)]
        ways += [(2 * i + 1, 2 * (i - far) + 1 if i >= far else 2 * i) for i in range(devices)]
        return lax.ppermute(block, ("cp", "hd"), ways)

    def twin(block):
        return lax.ppermute(block, "hd", [(0, 1), (1, 0)])

    own = packed(keys, values)
    other_keys, other_values, own = lax.optimization_barrier((twin(keys), twin(values), own))
    block = stacked(own, other_keys, other_values)
    block, late_grad = lax.optimization_barrier((block, out_grad))
    other_grad = twin(late_grad)
    at2 = step(block, 2)
    at1 = step(block, 1)
    attn_grad = project_back(core, out_grad, other_grad, out_weight)
    at2, attn_grad = lax.optimization_barrier((at2, attn_grad))
    at4 = step(at2, 2)
    at3 = step(at2, 1)
    ranges, limit, q_st, win, p, near_acc, top = near_scores(
        place, doc_lengths.reshape(1, -1), doc_full.reshape(1, -1), queries,
        own, at1, at2, twin(at1[PAIR:]), twin(at2[PAIR:]),
    )
    at4, at3, top = lax.optimization_barrier((at4, at3, top))
    twin3, twin4 = twin(at3[PAIR:]), twin(at4[PAIR:])
    attn, do_st, stats, dq_far, ahead, across = middle(
        place, ranges, limit, q_st, near_acc, top, at3, at4, twin3, twin4, attn_grad
    )
    away = project(1 - core, attn, out_weight)
    across, away = lax.optimization_barrier((twin(across), away))
    out4, out3 = both_heads(ahead, across)
    out4, out3, stats = lax.optimization_barrier((out4, out3, stats))
    in4 = step(out4, 2)
    in3 = step(out3, 1)
    query_grad, ahead, across, mid = near_back(place, ranges, win, p, q_st, do_st, stats, dq_far)
    came = summed(in4, in3)
    came, across = lax.optimization_barrier((came, twin(across)))
    far_out, near_out = far_and_near(ahead, across, came)
    far_out, away = lax.optimization_barrier((far_out, away))
    far = step(far_out, 2)
    near = step(near_out, 1)
    layer_out = project(core, attn, out_weight, twin(away))
    far, near, layer_out = lax.optimization_barrier((far, near, layer_out))
    key_grad, value_grad = last_sum(mid, near, far, twin(near[PAIR:]), twin(far[PAIR:]))
    return (layer_out, query_grad, key_grad, value_grad)


def solution(mesh):
    placed = (P("cp", "hd"), P("cp", "hd"), P("cp", "hd"), P(None, "hd"), P(), P(), P("cp", "hd"))
    return jax.shard_map(
        on_device,
        mesh=mesh,
        in_specs=placed,
        out_specs=(P("cp", "hd"), P("cp", "hd"), P("cp", "hd"), P("cp", "hd")),
        check_vma=False,
    )
```

```python
import math

import jax
import jax.numpy as jnp
from jax import lax
from jax.experimental import pallas as pl
from jax.experimental.pallas import tpu as pltpu
from jax.sharding import PartitionSpec as P

HQ = 8
HK = 2
DH = 128
SPAN = 4
ROWS = 256
GROUPS = HQ // HK
WIDE = 2 * SPAN + 1
PAIR = 2 * ROWS
REACH = 2
NEAR = 2 * REACH + 1
FAR = WIDE - NEAR
SIDE = FAR // 2
SUB = 128
SUBS = ROWS // SUB
TILE = GROUPS * SUB
CHUNK = 256
CHUNKS = TILE // CHUNK
STACK = SUBS * TILE
NEG = -1e30
BIG = 60 * 1024 * 1024
SCALE = 1.0 / math.sqrt(DH)
SCALE2 = SCALE / math.log(2.0)
VMEM = pl.BlockSpec(memory_space=pltpu.VMEM)
ANY = pl.BlockSpec(memory_space=pl.ANY)
SMALL = pltpu.CompilerParams(vmem_limit_bytes=4 * 1024 * 1024)
SMEM = pl.BlockSpec(memory_space=pltpu.SMEM)


def dot_nn(a, b):
    return lax.dot_general(a, b, (((1,), (0,)), ((), ())), preferred_element_type=jnp.float32)


def dot_nt(a, b):
    return lax.dot_general(a, b, (((1,), (1,)), ((), ())), preferred_element_type=jnp.float32)


def limits(index, lengths_row, full_row):
    n = lengths_row.shape[1]
    row = lax.broadcasted_iota(jnp.int32, (n, n), 0)
    col = lax.broadcasted_iota(jnp.int32, (n, n), 1)
    ends = jnp.sum(jnp.where(col <= row, lengths_row, 0), axis=1, keepdims=True)
    starts = jnp.sum(jnp.where(col < row, lengths_row, 0), axis=1, keepdims=True)
    full = jnp.sum(jnp.where(col == row, full_row, 0), axis=1, keepdims=True)
    pos = index * ROWS + lax.broadcasted_iota(jnp.int32, (n, ROWS), 1)
    inside = (pos >= starts) & (pos < ends)
    low = jnp.sum(jnp.where(inside, starts, 0), axis=0, keepdims=True)
    high = jnp.sum(jnp.where(inside, jnp.where(full == 1, ends, pos + 1), 0), axis=0, keepdims=True)
    return low, high


def rows_of(r):
    return pl.ds(pl.multiple_of(r * ROWS, ROWS), ROWS)


def keys_of(r):
    return pl.ds(pl.multiple_of(r * 2 * ROWS, ROWS), ROWS)


def vals_of(r):
    return pl.ds(pl.multiple_of(r * 2 * ROWS + ROWS, ROWS), ROWS)


def pair_of(r):
    return pl.ds(pl.multiple_of(r * PAIR, ROWS), PAIR)


def staged(sub, h):
    return slice(sub * TILE + h * SUB, sub * TILE + (h + 1) * SUB)


def sub_rows(sub):
    return slice(sub * SUB, (sub + 1) * SUB)


def head_cols(h):
    return slice(h * DH, (h + 1) * DH)


def chunks_of(subs):
    return range(subs[0] * CHUNKS, (subs[-1] + 1) * CHUNKS)


def chunk_cols(c):
    return slice(c * CHUNK, (c + 1) * CHUNK)


def segments_of(range_ref):
    low0, high0, low1, high1 = [range_ref[n] for n in range(4)]
    return (
        ((0,), low0, jnp.minimum(low1, high0)),
        ((0, 1), low1, high0),
        ((1,), jnp.maximum(low1, high0), high1),
    )


def every_near(range_ref, make, state):
    skip = SPAN - REACH
    for subs, lower, upper in segments_of(range_ref):
        state = lax.fori_loop(jnp.maximum(lower - skip, 0), jnp.minimum(upper - skip, NEAR), make(subs), state)
    return state


def every_far(range_ref, make, state):
    end = SPAN + REACH + 1
    for subs, lower, upper in segments_of(range_ref):
        first = jnp.where(lower < SIDE, lower, jnp.maximum(lower, end) - NEAR)
        last = jnp.where(upper > end, upper - NEAR, jnp.minimum(upper, SIDE))
        state = lax.fori_loop(first, last, make(subs), state)
    return state


def score_block(subs, at, first_key, limit_ref, win, q_st, s_ref, top):
    keys = win[keys_of(at), :]
    key_pos = first_key + lax.broadcasted_iota(jnp.int32, (ROWS, CHUNK), 0)
    valid = {
        sub: (key_pos >= limit_ref[2 * sub : 2 * sub + 1, :]) & (key_pos < limit_ref[2 * sub + 1 : 2 * sub + 2, :])
        for sub in subs
    }
    out = list(top)
    for c in chunks_of(subs):
        s = dot_nt(keys, q_st[chunk_cols(c), :]) * SCALE2
        s = jnp.where(valid[c // CHUNKS], s, NEG)
        s_ref[rows_of(at), chunk_cols(c)] = s
        out[c] = jnp.maximum(top[c], jnp.max(s, axis=0, keepdims=True))
    return tuple(out)


def weigh_block(subs, at, win, s_ref, p_ref, acc, top, total):
    vals_t = win[vals_of(at), :].T
    out = list(total)
    for c in chunks_of(subs):
        cols = chunk_cols(c)
        p = jnp.exp2(s_ref[rows_of(at), cols] - top[c])
        out[c] = total[c] + jnp.sum(p, axis=0, keepdims=True)
        p = p.astype(jnp.bfloat16)
        p_ref[rows_of(at), cols] = p
        acc[:, cols] += dot_nn(vals_t, p)
    return tuple(out)


def back_block(subs, at, win, p_ref, do_st, qs_st, dos_st, stats_ref, ds_scr, dq_acc, out_win):
    keys_t = win[keys_of(at), :].T
    vals = win[vals_of(at), :]
    for c in chunks_of(subs):
        cols = chunk_cols(c)
        dp = dot_nt(vals, do_st[cols, :])
        ds = (p_ref[rows_of(at), cols].astype(jnp.float32) * (dp - stats_ref[1:2, cols])).astype(jnp.bfloat16)
        ds_scr[:, cols] = ds
        dq_acc[:, cols] += dot_nn(keys_t, ds)
    cols = slice(subs[0] * TILE, (subs[-1] + 1) * TILE)
    out_win[keys_of(at), :] = dot_nn(ds_scr[:, cols], qs_st[cols, :]).astype(jnp.bfloat16)
    out_win[vals_of(at), :] = dot_nn(p_ref[rows_of(at), cols], dos_st[cols, :]).astype(jnp.bfloat16)


def scaled_copies(q_st, do_st, inv_row, qs_st, dos_st):
    for n in range(SUBS * GROUPS):
        cols = slice(n * SUB, (n + 1) * SUB)
        inv_col = jnp.broadcast_to(inv_row[:, cols], (DH, SUB)).T
        dos_st[cols, :] = (do_st[cols, :].astype(jnp.float32) * inv_col).astype(jnp.bfloat16)
        qs_st[cols, :] = (q_st[cols, :].astype(jnp.float32) * (inv_col * SCALE)).astype(jnp.bfloat16)


def near_scores_kernel(
    place_ref, len_ref, full_ref, q_ref, own_ref, at1_ref, at2_ref, twin1_ref, twin2_ref,
    range_ref, limit_ref, q_st, win, p_ref, acc, top_ref,
    s_ref,
):
    way = 1 - 2 * place_ref[1]
    base = place_ref[0] - SPAN
    low, high = limits(place_ref[0], len_ref[...], full_ref[...])
    for sub in range(SUBS):
        cut = sub_rows(sub)
        limit_ref[2 * sub : 2 * sub + 1, :] = jnp.concatenate([low[:, cut]] * (CHUNK // SUB), axis=1)
        limit_ref[2 * sub + 1 : 2 * sub + 2, :] = jnp.concatenate([high[:, cut]] * (CHUNK // SUB), axis=1)
        range_ref[2 * sub] = jnp.maximum(jnp.min(low[:, cut]) // ROWS - base, 0)
        range_ref[2 * sub + 1] = jnp.minimum((jnp.max(high[:, cut]) + ROWS - 1) // ROWS - base, WIDE)
        for h in range(GROUPS):
            q_st[staged(sub, h), :] = q_ref[cut, head_cols(h)]
    win[pair_of(REACH), :] = own_ref[0:PAIR, :]
    for k, ring, twin in ((1, at1_ref, twin1_ref), (2, at2_ref, twin2_ref)):
        win[pair_of(REACH - k * way), :] = ring[0:PAIR, :]
        win[pair_of(REACH + k * way), :] = twin[...]

    def scores(subs):
        def body(at, top):
            first_key = (base + SPAN - REACH + at) * ROWS
            return score_block(subs, at, first_key, limit_ref, win, q_st, s_ref, top)

        return body

    none = jnp.full((1, CHUNK), NEG, jnp.float32)
    top = every_near(range_ref, scores, (none,) * (SUBS * CHUNKS))
    acc[...] = jnp.zeros_like(acc)

    def weigh(subs):
        return lambda at, total: weigh_block(subs, at, win, s_ref, p_ref, acc, top, total)

    total = every_near(range_ref, weigh, (jnp.zeros((1, CHUNK), jnp.float32),) * (SUBS * CHUNKS))
    for c in range(SUBS * CHUNKS):
        top_ref[0:1, chunk_cols(c)] = top[c]
        top_ref[1:2, chunk_cols(c)] = total[c]


def middle_kernel(
    place_ref, range_ref, limit_ref, q_st, near_acc, top_ref, at3_ref, at4_ref, twin3_ref, twin4_ref, do_ref,
    attn_ref, do_st, stats_ref, dq_acc, ahead_ref, across_ref,
    win, out_win, s_scr, p_scr, ds_scr, acc, qs_st, dos_st,
):
    core = place_ref[1]
    base = place_ref[0] - SPAN

    def slot(n):
        return n + core * (FAR - 1 - 2 * n)

    for n, ref in enumerate((at4_ref, at3_ref, twin3_ref, twin4_ref)):
        win[pair_of(slot(n)), :] = ref[0:PAIR, :]

    def scores(subs):
        def body(at, top):
            first_key = (base + jnp.where(at < SIDE, at, at + NEAR)) * ROWS
            return score_block(subs, at, first_key, limit_ref, win, q_st, s_scr, top)

        return body

    near_top = tuple(top_ref[0:1, chunk_cols(c)] for c in range(SUBS * CHUNKS))
    top = every_far(range_ref, scores, near_top)
    share = [jnp.exp2(near_top[c] - top[c]) for c in range(SUBS * CHUNKS)]
    for c in range(SUBS * CHUNKS):
        acc[:, chunk_cols(c)] = near_acc[:, chunk_cols(c)] * share[c]

    def weigh(subs):
        return lambda at, total: weigh_block(subs, at, win, s_scr, p_scr, acc, top, total)

    total = tuple(top_ref[1:2, chunk_cols(c)] * share[c] for c in range(SUBS * CHUNKS))
    total = every_far(range_ref, weigh, total)
    for c in range(SUBS * CHUNKS):
        inv = 1.0 / total[c]
        stats_ref[0:1, chunk_cols(c)] = inv
        stats_ref[2:3, chunk_cols(c)] = inv * share[c]
    for sub in range(SUBS):
        for h in range(GROUPS):
            cols = staged(sub, h)
            attn_t = (acc[:, cols] * stats_ref[0:1, cols]).astype(jnp.bfloat16).astype(jnp.float32)
            attn_ref[sub_rows(sub), head_cols(h)] = attn_t.T.astype(jnp.bfloat16)
            grad = do_ref[sub_rows(sub), head_cols(h)]
            do_st[cols, :] = grad
            stats_ref[1:2, cols] = jnp.sum(attn_t * grad.astype(jnp.float32).T, axis=0, keepdims=True)
    dq_acc[...] = jnp.zeros_like(dq_acc)
    out_win[...] = jnp.zeros_like(out_win)

    @pl.when((range_ref[0] < SIDE) | (range_ref[3] > SIDE + NEAR))
    def _():
        scaled_copies(q_st, do_st, stats_ref[0:1, :], qs_st, dos_st)

    def back(subs):
        def body(at, carry):
            back_block(subs, at, win, p_scr, do_st, qs_st, dos_st, stats_ref, ds_scr, dq_acc, out_win)
            return carry

        return body

    every_far(range_ref, back, 0)
    for n in range(SIDE):
        ahead_ref[n * PAIR : (n + 1) * PAIR, :] = out_win[pair_of(slot(FAR - 1 - n)), :]
        across_ref[n * PAIR : (n + 1) * PAIR, :] = out_win[pair_of(slot(n)), :]


def near_back_kernel(
    place_ref, range_ref, win, p_ref, q_st, do_st, stats_ref, dq_far,
    dq_ref, ahead_ref, across_ref, mid_ref,
    out_win, ds_scr, dq_acc, qs_st, dos_st,
):
    way = 1 - 2 * place_ref[1]
    dq_acc[...] = jnp.zeros_like(dq_acc)
    scaled_copies(q_st, do_st, stats_ref[2:3, :], qs_st, dos_st)
    out_win[...] = jnp.zeros_like(out_win)

    def back(subs):
        def body(at, carry):
            back_block(subs, at, win, p_ref, do_st, qs_st, dos_st, stats_ref, ds_scr, dq_acc, out_win)
            return carry

        return body

    every_near(range_ref, back, 0)
    mid_ref[...] = out_win[pair_of(REACH), :]
    for n in range(REACH):
        k = REACH - n
        ahead_ref[n * PAIR : (n + 1) * PAIR, :] = out_win[pair_of(REACH + k * way), :]
        across_ref[n * PAIR : (n + 1) * PAIR, :] = out_win[pair_of(REACH - k * way), :]
    for sub in range(SUBS):
        for h in range(GROUPS):
            cols = staged(sub, h)
            dq = dq_acc[:, cols] * (stats_ref[2:3, cols] * SCALE) + dq_far[:, cols] * (stats_ref[0:1, cols] * SCALE)
            dq_ref[sub_rows(sub), head_cols(h)] = dq.T.astype(jnp.bfloat16)


def bf16(*shape):
    return jax.ShapeDtypeStruct(shape, jnp.bfloat16)


def f32(*shape):
    return jax.ShapeDtypeStruct(shape, jnp.float32)


def i32(*shape):
    return jax.ShapeDtypeStruct(shape, jnp.int32)


def near_scores(*args):
    return pl.pallas_call(
        near_scores_kernel,
        out_shape=(
            i32(4), i32(8, CHUNK), bf16(STACK, DH), bf16(NEAR * PAIR, DH), bf16(NEAR * ROWS, STACK), f32(DH, STACK),
            f32(8, STACK),
        ),
        in_specs=[SMEM] + [VMEM] * 8,
        out_specs=(SMEM,) + (VMEM,) * 6,
        scratch_shapes=[pltpu.VMEM((NEAR * ROWS, STACK), jnp.float32)],
        compiler_params=pltpu.CompilerParams(vmem_limit_bytes=18 * 1024 * 1024),
        cost_estimate=pl.CostEstimate(flops=10**9, bytes_accessed=6 * 10**6, transcendentals=0),
    )(*args)


def middle(*args):
    return pl.pallas_call(
        middle_kernel,
        out_shape=(
            bf16(ROWS, GROUPS * DH), bf16(STACK, DH), f32(8, STACK), f32(DH, STACK),
            bf16(SIDE * PAIR, DH), bf16(SIDE * PAIR, DH),
        ),
        in_specs=[SMEM, SMEM] + [VMEM] * 9,
        out_specs=(VMEM,) * 6,
        scratch_shapes=[
            pltpu.VMEM((FAR * PAIR, DH), jnp.bfloat16),
            pltpu.VMEM((FAR * PAIR, DH), jnp.bfloat16),
            pltpu.VMEM((FAR * ROWS, STACK), jnp.float32),
            pltpu.VMEM((FAR * ROWS, STACK), jnp.bfloat16),
            pltpu.VMEM((ROWS, STACK), jnp.bfloat16),
            pltpu.VMEM((DH, STACK), jnp.float32),
            pltpu.VMEM((STACK, DH), jnp.bfloat16),
            pltpu.VMEM((STACK, DH), jnp.bfloat16),
        ],
        compiler_params=pltpu.CompilerParams(vmem_limit_bytes=20 * 1024 * 1024),
        cost_estimate=pl.CostEstimate(flops=10**9, bytes_accessed=6 * 10**6, transcendentals=10**6),
    )(*args)


def near_back(*args):
    return pl.pallas_call(
        near_back_kernel,
        out_shape=(bf16(ROWS, GROUPS * DH), bf16(REACH * PAIR, DH), bf16(REACH * PAIR, DH), bf16(PAIR, DH)),
        in_specs=[SMEM, SMEM] + [VMEM] * 6,
        out_specs=(VMEM,) * 4,
        scratch_shapes=[
            pltpu.VMEM((NEAR * PAIR, DH), jnp.bfloat16),
            pltpu.VMEM((ROWS, STACK), jnp.bfloat16),
            pltpu.VMEM((DH, STACK), jnp.float32),
            pltpu.VMEM((STACK, DH), jnp.bfloat16),
            pltpu.VMEM((STACK, DH), jnp.bfloat16),
        ],
        compiler_params=pltpu.CompilerParams(vmem_limit_bytes=16 * 1024 * 1024),
        cost_estimate=pl.CostEstimate(flops=2 * 10**10, bytes_accessed=3 * 10**7, transcendentals=0),
    )(*args)


def small_call(body, out_rows, *args):
    shapes = [jax.ShapeDtypeStruct((rows, DH), jnp.bfloat16) for rows in out_rows]
    return pl.pallas_call(
        body,
        out_shape=shapes,
        in_specs=[VMEM] * len(args),
        out_specs=[VMEM] * len(shapes),
        compiler_params=SMALL,
        cost_estimate=pl.CostEstimate(flops=10**5, bytes_accessed=10**5, transcendentals=0),
    )(*args)


def stacked(*parts):
    def body(*refs):
        at = 0
        for ref in refs[:-1]:
            refs[-1][at : at + ref.shape[0], :] = ref[...]
            at += ref.shape[0]

    return small_call(body, [sum(part.shape[0] for part in parts)], *parts)[0]


def far_and_near(ahead, across, came):
    def body(ahead_ref, across_ref, came_ref, far_ref, near_ref):
        for n, ref in enumerate((ahead_ref, across_ref)):
            at = slice(n * PAIR, (n + 1) * PAIR)
            far_ref[at, :] = (ref[0:PAIR, :].astype(jnp.float32) + came_ref[at, :].astype(jnp.float32)).astype(jnp.bfloat16)
            near_ref[at, :] = ref[PAIR : 2 * PAIR, :]

    return small_call(body, [2 * PAIR] * 2, ahead, across, came)


def packed(*parts):
    n = len(parts)
    rows = parts[0].shape[0]

    def body(*refs):
        copies = [
            pltpu.make_async_copy(refs[k], refs[n].at[k * rows : (k + 1) * rows, :], refs[n + 1].at[k]) for k in range(n)
        ]
        for copy in copies:
            copy.start()
        for copy in copies:
            copy.wait()

    return pl.pallas_call(
        body,
        out_shape=bf16(n * rows, DH),
        in_specs=[ANY] * n,
        out_specs=VMEM,
        scratch_shapes=[pltpu.SemaphoreType.DMA((n,))],
        compiler_params=pltpu.CompilerParams(vmem_limit_bytes=48 * 1024 * 1024),
        cost_estimate=pl.CostEstimate(flops=0, bytes_accessed=10**6, transcendentals=0),
    )(*parts)


def both_heads(ahead, across):
    def body(ahead_ref, across_ref, *out_refs):
        for n, out_ref in enumerate(out_refs):
            out_ref[0:PAIR, :] = ahead_ref[n * PAIR : (n + 1) * PAIR, :]
            out_ref[PAIR : 2 * PAIR, :] = across_ref[n * PAIR : (n + 1) * PAIR, :]

    return small_call(body, [2 * PAIR] * 2, ahead, across)


def summed(*parts):
    def body(*refs):
        total = refs[0][...].astype(jnp.float32)
        for ref in refs[1:-1]:
            total += ref[...].astype(jnp.float32)
        refs[-1][...] = total.astype(jnp.bfloat16)

    return small_call(body, [parts[0].shape[0]], *parts)[0]


def last_sum(*parts):
    def body(*refs):
        for at, out_ref in ((0, refs[-2]), (ROWS, refs[-1])):
            total = refs[0][at : at + ROWS, :].astype(jnp.float32)
            for ref in refs[1:-2]:
                total += ref[at : at + ROWS, :].astype(jnp.float32)
            out_ref[...] = total.astype(jnp.bfloat16)

    return small_call(body, [ROWS, ROWS], *parts)


def half_of(core, size):
    return pl.ds(pl.multiple_of(core * size, size), size)


def project_back(core, own, other, w):
    rows, depth = own.shape
    cols = w.shape[1]

    def body(core_ref, own_ref, other_ref, w_ref, out_ref):
        core = core_ref[0]
        part = dot_nn(own_ref[...], w_ref[half_of(core, depth), :])
        out_ref[...] = (part + dot_nn(other_ref[...], w_ref[half_of(1 - core, depth), :])).astype(jnp.bfloat16)

    return pl.pallas_call(
        body,
        out_shape=bf16(rows, cols),
        in_specs=[SMEM, VMEM, VMEM, VMEM],
        out_specs=VMEM,
        compiler_params=pltpu.CompilerParams(vmem_limit_bytes=12 * 1024 * 1024),
        cost_estimate=pl.CostEstimate(flops=4 * rows * depth * cols, bytes_accessed=6 * 10**6, transcendentals=0),
    )(core, own, other, w)


def project(half, attn, w, other=None):
    rows, depth = attn.shape
    cols = w.shape[0] // 2
    more = () if other is None else (other,)

    def body(half_ref, a_ref, w_ref, *refs):
        out = dot_nt(a_ref[...], w_ref[half_of(half_ref[0], cols), :])
        if more:
            out += refs[0][...].astype(jnp.float32)
        refs[-1][...] = out.astype(jnp.bfloat16)

    return pl.pallas_call(
        body,
        out_shape=bf16(rows, cols),
        in_specs=[SMEM, VMEM, VMEM] + [VMEM] * len(more),
        out_specs=VMEM,
        compiler_params=pltpu.CompilerParams(vmem_limit_bytes=12 * 1024 * 1024),
        cost_estimate=pl.CostEstimate(flops=2 * rows * depth * cols, bytes_accessed=4 * 10**6, transcendentals=0),
    )(half, attn, w, *more)


def on_device(queries, keys, values, out_weight, doc_lengths, doc_full, out_grad):
    devices = lax.axis_size("cp")
    index = lax.axis_index("cp").astype(jnp.int32)
    core = lax.axis_index("hd").astype(jnp.int32)
    place = jnp.stack([index, core])
    core = core.reshape(1)

    def step(block, far):
        ways = [(2 * i, 2 * (i + far) if i + far < devices else 2 * i + 1) for i in range(devices)]
        ways += [(2 * i + 1, 2 * (i - far) + 1 if i >= far else 2 * i) for i in range(devices)]
        return lax.ppermute(block, ("cp", "hd"), ways)

    def twin(block):
        return lax.ppermute(block, "hd", [(0, 1), (1, 0)])

    own = packed(keys, values)
    other_keys, other_values, own = lax.optimization_barrier((twin(keys), twin(values), own))
    block = stacked(own, other_keys, other_values)
    block, late_grad = lax.optimization_barrier((block, out_grad))
    other_grad = twin(late_grad)
    at2 = step(block, 2)
    at1 = step(block, 1)
    attn_grad = project_back(core, out_grad, other_grad, out_weight)
    at2, attn_grad = lax.optimization_barrier((at2, attn_grad))
    at4 = step(at2, 2)
    at3 = step(at2, 1)
    ranges, limit, q_st, win, p, near_acc, top = near_scores(
        place, doc_lengths.reshape(1, -1), doc_full.reshape(1, -1), queries,
        own, at1, at2, twin(at1[PAIR:]), twin(at2[PAIR:]),
    )
    at4, at3, top = lax.optimization_barrier((at4, at3, top))
    twin3, twin4 = twin(at3[PAIR:]), twin(at4[PAIR:])
    attn, do_st, stats, dq_far, ahead, across = middle(
        place, ranges, limit, q_st, near_acc, top, at3, at4, twin3, twin4, attn_grad
    )
    away = project(1 - core, attn, out_weight)
    across, away = lax.optimization_barrier((twin(across), away))
    out4, out3 = both_heads(ahead, across)
    out4, out3, stats = lax.optimization_barrier((out4, out3, stats))
    in4 = step(out4, 2)
    in3 = step(out3, 1)
    query_grad, ahead, across, mid = near_back(place, ranges, win, p, q_st, do_st, stats, dq_far)
    came = summed(in4, in3)
    came, across = lax.optimization_barrier((came, twin(across)))
    far_out, near_out = far_and_near(ahead, across, came)
    far_out, away = lax.optimization_barrier((far_out, away))
    far = step(far_out, 2)
    near = step(near_out, 1)
    layer_out = project(core, attn, out_weight, twin(away))
    far, layer_out = lax.optimization_barrier((far, layer_out))
    near, far_twin = lax.optimization_barrier((near, twin(far[PAIR:])))
    key_grad, value_grad = last_sum(mid, near, far, twin(near[PAIR:]), far_twin)
    return (layer_out, query_grad, key_grad, value_grad)


def solution(mesh):
    placed = (P("cp", "hd"), P("cp", "hd"), P("cp", "hd"), P(None, "hd"), P(), P(), P("cp", "hd"))
    return jax.shard_map(
        on_device,
        mesh=mesh,
        in_specs=placed,
        out_specs=(P("cp", "hd"), P("cp", "hd"), P("cp", "hd"), P("cp", "hd")),
        check_vma=False,
    )
```
